32 devices in a mesh: tm: 2 (over x), space: 16 (over z, y, core).
Axes of the slice: x: 2, y: 2, z: 4, core: 2. Of those that a mesh axis runs over, the one named last changes fastest.
Arguments:
- eof_basis: bfloat16 [131072, 256], P('space'), may hold values from -0.015625 to 0.015625
- snapshots: bfloat16 [131072, 128], P('space', 'tm'), may hold values from -6 to 6
- inverse_energy: float32 [256], replicated, may hold values from 0.044194173 to 0.44194174
- eigen_vectors: bfloat16 [256, 512], replicated, may hold values from -0.375 to 0.375
Outputs:
- reduced_operator: float32 [256, 256], replicated
- rebuilt_modes: bfloat16 [512, 131072], P('tm', 'space')
The draws below stay inside these ranges and needn't reach their ends.
All inputs are finite; a program needn't handle non-finite values.
Results may differ from the reference program's by a relative error of at most 0.0049.
Values may be sent and summed in bfloat16 or wider, within the bound.
No kernel may reach another device: no remote copies, remote signals or barrier semaphores. Data moves between devices by JAX's collectives and lax.ppermute only.
A program may use at most 64 MiB of HBM per device.

```python
import math
import jax
import jax.numpy as jnp
from jax import lax

R = 256
CELLS = 131072
HOURS = 128


def block_levels(rng, shape, split, least, top_value):
    level = 1.0
    for dim, parts in split:
        draws = jax.random.uniform(jax.random.fold_in(jax.random.fold_in(rng, 6), dim), (parts,), jnp.float32, least / len(split), top_value / len(split))
        level = level * jnp.repeat(jnp.exp(draws), shape[dim] // parts).reshape((-1,) + (1,) * (len(shape) - 1 - dim))
    return level


def gaussian(own_key, shape, width, bound, pieces=(), held_as=jnp.bfloat16):
    drawn = jax.random.normal(own_key, shape, jnp.float32) * width
    if len(pieces) > 0:
        drawn = block_levels(own_key, shape, pieces, -0.22, 0.18) * drawn
    return jnp.clip(drawn, min=-bound, max=bound).astype(held_as)


def setup_inputs(seed: int = 0) -> dict:
    keys = jax.random.split(jax.random.key(seed), 5)
    return {
        "eof_basis": gaussian(keys[0], (CELLS, R), CELLS ** -0.5, 0.015625, ((0, 16),)),
        "snapshots": gaussian(keys[1], (CELLS, HOURS), 1.0, 6.0, ((0, 16), (1, 2))),
        "inverse_energy": jnp.clip(jnp.exp(jax.random.uniform(keys[2], (R,), jnp.float32, math.log(0.044194173), math.log(0.44194174))), 0.044194173, 0.44194174),
        "eigen_vectors": gaussian(keys[3], (R, 2 * R), R ** -0.5, 0.375),
    }


def reference(eof_basis, snapshots, inverse_energy, eigen_vectors):
    coeffs = lax.dot_general(eof_basis, snapshots, (((0,), (0,)), ((), ())), preferred_element_type=jnp.float32)
    lagged = jnp.concatenate([jnp.zeros((coeffs.shape[0], 1), jnp.float32), coeffs[:, :-1]], axis=1)
    scaled = lagged * inverse_energy[:, None]
    reduced_operator = jnp.dot(coeffs, scaled.T, precision=lax.Precision.HIGHEST)
    hour_weights = jnp.dot(scaled.T, eigen_vectors.astype(jnp.float32), precision=lax.Precision.HIGHEST).astype(jnp.bfloat16)
    modes = lax.dot_general(hour_weights, snapshots, (((0,), (1,)), ((), ())), preferred_element_type=jnp.float32)
    return reduced_operator, modes.astype(jnp.bfloat16)
```

```python
import jax
import jax.numpy as jnp
from jax import lax
from jax.sharding import PartitionSpec as P


def per_device(eof_basis, snapshots, inverse_energy, eigen_vectors):
    tm, space = lax.axis_size("tm"), lax.axis_size("space")
    me = lax.axis_index("tm")
    hours, rank = snapshots.shape[1], eof_basis.shape[1]

    held = [snapshots]
    for k in range(1, tm):
        route = [((i + k) % tm, i) for i in range(tm)]
        held.append(lax.ppermute(snapshots, "tm", route))

    partial_sum = lax.dot_general(
        snapshots, eof_basis, (((0,), (0,)), ((), ())), preferred_element_type=jnp.float32
    )
    pieces = (
        partial_sum.reshape(hours // 8, 8, rank // 128, 128)
        .transpose(0, 2, 1, 3)
        .reshape(space, -1, 128)
    )
    shares = lax.all_to_all(pieces, "space", 0, 0, tiled=True)
    mine = jnp.sum(shares, axis=0)
    every = lax.all_gather(mine, ("tm", "space"), axis=0)
    coeffs = (
        every.reshape(tm * hours // 8, rank // 128, 8, 128)
        .transpose(0, 2, 1, 3)
        .reshape(tm * hours, rank)
    )
    lagged = jnp.concatenate([jnp.zeros((1, rank), jnp.float32), coeffs[:-1]], axis=0)
    scaled = lagged * inverse_energy[None, :]
    reduced_operator = lax.dot_general(
        coeffs, scaled, (((0,), (0,)), ((), ())), precision=lax.Precision.HIGHEST
    )
    rows = eigen_vectors.shape[1] // tm
    vectors = lax.dynamic_slice_in_dim(eigen_vectors, me * rows, rows, 1)
    weights = jnp.dot(
        scaled, vectors.astype(jnp.float32), precision=lax.Precision.HIGHEST
    ).astype(jnp.bfloat16)
    rebuilt = 0.0
    for k in range(tm):
        part = lax.dynamic_slice_in_dim(weights, ((me + k) % tm) * hours, hours, 0)
        rebuilt = rebuilt + lax.dot_general(
            part, held[k], (((0,), (1,)), ((), ())), preferred_element_type=jnp.float32
        )
    return (reduced_operator, rebuilt.astype(jnp.bfloat16))


def solution(mesh):
    in_specs = (P("space", None), P("space", "tm"), P(), P())
    out_specs = (P(), P("tm", "space"))
    return jax.shard_map(
        per_device, mesh=mesh, in_specs=in_specs, out_specs=out_specs, check_vma=False
    )
```

```python
import jax
import jax.numpy as jnp
import numpy as np
from jax import lax
from jax.sharding import Mesh, PartitionSpec as P


def sent_to_all(block, axes):
    count = lax.axis_size(axes)
    copies = jnp.broadcast_to(block[None], (count,) + block.shape)
    return lax.all_to_all(copies, axes, 0, 0, tiled=True)


def per_device(eof_basis, snapshots, inverse_energy, eigen_vectors):
    tm, inner = lax.axis_size("tm"), lax.axis_size("inner")
    me = lax.axis_index("tm")
    hours, rank = snapshots.shape[1], eof_basis.shape[1]

    held = [snapshots]
    for k in range(1, tm):
        route = [((i + k) % tm, i) for i in range(tm)]
        held.append(lax.ppermute(snapshots, "tm", route))

    partial_sum = lax.dot_general(
        snapshots, eof_basis, (((0,), (0,)), ((), ())), preferred_element_type=jnp.float32
    )
    pieces = partial_sum.reshape(inner, hours // inner, rank)
    mine = jnp.sum(lax.all_to_all(pieces, "inner", 0, 0, tiled=True), axis=0)
    mine = jnp.sum(sent_to_all(mine, "outer"), axis=0)
    coeffs = sent_to_all(mine, ("tm", "inner")).reshape(tm * hours, rank)

    lagged = jnp.concatenate([jnp.zeros((1, rank), jnp.float32), coeffs[:-1]], axis=0)
    scaled = lagged * inverse_energy[None, :]
    reduced_operator = lax.dot_general(
        coeffs, scaled, (((0,), (0,)), ((), ())), precision=lax.Precision.HIGHEST
    )
    rows = eigen_vectors.shape[1] // tm
    vectors = lax.dynamic_slice_in_dim(eigen_vectors, me * rows, rows, 1)
    weights = jnp.dot(
        scaled, vectors.astype(jnp.float32), precision=lax.Precision.HIGHEST
    ).astype(jnp.bfloat16)
    rebuilt = 0.0
    for k in range(tm):
        part = lax.dynamic_slice_in_dim(weights, ((me + k) % tm) * hours, hours, 0)
        rebuilt = rebuilt + lax.dot_general(
            part, held[k], (((0,), (1,)), ((), ())), preferred_element_type=jnp.float32
        )
    return (reduced_operator, rebuilt.astype(jnp.bfloat16))


def solution(mesh):
    tm, space = mesh.shape["tm"], mesh.shape["space"]
    inner = 1
    while inner * inner < space and space % (2 * inner) == 0:
        inner *= 2
    split = Mesh(mesh.devices.reshape(tm, space // inner, inner), ("tm", "outer", "inner"))
    cells = ("outer", "inner")
    in_specs = (P(cells, None), P(cells, "tm"), P(), P())
    out_specs = (P(), P("tm", cells))
    return jax.shard_map(
        per_device, mesh=split, in_specs=in_specs, out_specs=out_specs, check_vma=False
    )
```

```python
import jax
import jax.numpy as jnp
import numpy as np
from jax import lax
from jax.sharding import Mesh, PartitionSpec as P


def per_device(eof_basis, snapshots, inverse_energy, eigen_vectors):
    tm, inner = lax.axis_size("tm"), lax.axis_size("inner")
    me = lax.axis_index("tm")
    hours, rank = snapshots.shape[1], eof_basis.shape[1]

    held = [snapshots]
    for k in range(1, tm):
        route = [((i + k) % tm, i) for i in range(tm)]
        held.append(lax.ppermute(snapshots, "tm", route))

    partial_sum = lax.dot_general(
        snapshots, eof_basis, (((0,), (0,)), ((), ())), preferred_element_type=jnp.float32
    )
    pieces = partial_sum.reshape(inner, hours // inner, rank)
    mine = jnp.sum(lax.all_to_all(pieces, "inner", 0, 0, tiled=True), axis=0)
    mine = jnp.sum(lax.all_gather(mine, "outer", axis=0), axis=0)
    coeffs = lax.all_gather(mine, ("tm", "inner"), axis=0).reshape(tm * hours, rank)

    lagged = jnp.concatenate([jnp.zeros((1, rank), jnp.float32), coeffs[:-1]], axis=0)
    scaled = lagged * inverse_energy[None, :]
    reduced_operator = lax.dot_general(
        coeffs, scaled, (((0,), (0,)), ((), ())), precision=lax.Precision.HIGHEST
    )
    rows = eigen_vectors.shape[1] // tm
    vectors = lax.dynamic_slice_in_dim(eigen_vectors, me * rows, rows, 1)
    weights = jnp.dot(
        scaled, vectors.astype(jnp.float32), precision=lax.Precision.HIGHEST
    ).astype(jnp.bfloat16)
    rebuilt = 0.0
    for k in range(tm):
        part = lax.dynamic_slice_in_dim(weights, ((me + k) % tm) * hours, hours, 0)
        rebuilt = rebuilt + lax.dot_general(
            part, held[k], (((0,), (1,)), ((), ())), preferred_element_type=jnp.float32
        )
    return (reduced_operator, rebuilt.astype(jnp.bfloat16))


def solution(mesh):
    tm, space = mesh.shape["tm"], mesh.shape["space"]
    inner = 1
    while inner * inner < space and space % (2 * inner) == 0:
        inner *= 2
    split = Mesh(mesh.devices.reshape(tm, space // inner, inner), ("tm", "outer", "inner"))
    cells = ("outer", "inner")
    in_specs = (P(cells, None), P(cells, "tm"), P(), P())
    out_specs = (P(), P("tm", cells))
    return jax.shard_map(
        per_device, mesh=split, in_specs=in_specs, out_specs=out_specs, check_vma=False
    )
```

```python
import functools

import jax
import jax.numpy as jnp
from jax import lax
from jax.experimental import pallas as pl
from jax.experimental.pallas import tpu as pltpu
from jax.sharding import Mesh, PartitionSpec as P

ROWS = (((1,), (0,)), ((), ()))
FIRST = (((0,), (0,)), ((), ()))
LAST = (((1,), (1,)), ((), ()))
FREE = pl.CostEstimate(flops=0, bytes_accessed=0, transcendentals=0)


def in_parts(value):
    high = value.astype(jnp.bfloat16)
    return high, (value - high.astype(jnp.float32)).astype(jnp.bfloat16)


def product(left, right, dims):
    return lax.dot_general(left, right, dims, preferred_element_type=jnp.float32)


def project_kernel(tiles, snapshots, basis, out, fields, patterns, arrived):
    cells = snapshots.shape[1]
    tile = cells // tiles
    copies = []
    for i in range(tiles):
        span = pl.ds(i * tile, tile)
        copies.append(
            (
                pltpu.make_async_copy(snapshots.at[:, span], fields.at[:, span], arrived.at[0, i]),
                pltpu.make_async_copy(basis.at[span], patterns.at[span], arrived.at[1, i]),
            )
        )
    for pair in copies:
        for copy in pair:
            copy.start()
    total = jnp.zeros(out.shape, jnp.float32)
    for i, pair in enumerate(copies):
        for copy in pair:
            copy.wait()
        span = pl.ds(i * tile, tile)
        total += product(fields[:, span], patterns[span], ROWS)
    out[...] = total


def project(snapshots, basis, tiles):
    hours = snapshots.shape[0]
    rank = basis.shape[1]
    return pl.pallas_call(
        functools.partial(project_kernel, tiles),
        out_shape=jax.ShapeDtypeStruct((hours, rank), jnp.float32),
        in_specs=[pl.BlockSpec(memory_space=pl.ANY)] * 2,
        out_specs=pl.BlockSpec(memory_space=pltpu.VMEM),
        scratch_shapes=[
            pltpu.VMEM(snapshots.shape, snapshots.dtype),
            pltpu.VMEM(basis.shape, basis.dtype),
            pltpu.SemaphoreType.DMA((2, tiles)),
        ],
        compiler_params=pltpu.CompilerParams(vmem_limit_bytes=59 * 2**20),
        cost_estimate=FREE,
        name="project",
    )(snapshots, basis)


def rebuild_kernel(tiles, me, energy, coeffs, vectors, *refs):
    count = len(refs) - 9
    held, refs = refs[:count], refs[count:]
    operator, modes, fields, known, turned, scaled, made, arrived, sent = refs
    hours, cells = held[0].shape
    tile = cells // tiles
    inputs = [
        pltpu.make_async_copy(coeffs, known, arrived.at[count]),
        pltpu.make_async_copy(vectors, turned, arrived.at[count + 1]),
    ]
    blocks = [
        pltpu.make_async_copy(block, fields.at[pl.ds(k * hours, hours)], arrived.at[k])
        for k, block in enumerate(held)
    ]
    for copy in inputs + blocks:
        copy.start()
    for copy in inputs:
        copy.wait()
    every = known[...]
    hour = lax.broadcasted_iota(jnp.int32, every.shape, 0)
    scaled[...] = jnp.where(hour == 0, 0.0, pltpu.roll(every, 1, 0)) * energy[...]
    first = [pl.multiple_of(lax.rem(me[0] + k, count) * hours, hours) for k in range(count)]
    ordered = jnp.concatenate([scaled[pl.ds(at, hours)] for at in first], axis=0)
    high, low = in_parts(ordered)
    weights = (product(turned[...], high, LAST) + product(turned[...], low, LAST)).astype(
        jnp.bfloat16
    )
    for copy in blocks:
        copy.wait()
    outgoing = []
    for i in range(tiles):
        span = pl.ds(i * tile, tile)
        made[:, span] = product(weights, fields[:, span], ROWS).astype(made.dtype)
        copy = pltpu.make_async_copy(made.at[:, span], modes.at[:, span], sent.at[i])
        copy.start()
        outgoing.append(copy)
    high, low = in_parts(every)
    s_high, s_low = in_parts(scaled[...])
    operator[...] = (
        product(high, s_high, FIRST) + product(high, s_low, FIRST) + product(low, s_high, FIRST)
    )
    for copy in outgoing:
        copy.wait()


def rebuild(me, energy, coeffs, vectors, held, tiles):
    cells = held[0].shape[1]
    total, rank = coeffs.shape
    modes = vectors.shape[0]
    anywhere = pl.BlockSpec(memory_space=pl.ANY)
    return pl.pallas_call(
        functools.partial(rebuild_kernel, tiles),
        out_shape=(
            jax.ShapeDtypeStruct((rank, rank), jnp.float32),
            jax.ShapeDtypeStruct((modes, cells), jnp.bfloat16),
        ),
        in_specs=[
            pl.BlockSpec(memory_space=pltpu.SMEM),
            pl.BlockSpec(memory_space=pltpu.VMEM),
        ]
        + [anywhere] * (2 + len(held)),
        out_specs=(pl.BlockSpec(memory_space=pltpu.VMEM), anywhere),
        scratch_shapes=[
            pltpu.VMEM((total, cells), held[0].dtype),
            pltpu.VMEM(coeffs.shape, coeffs.dtype),
            pltpu.VMEM(vectors.shape, vectors.dtype),
            pltpu.VMEM(coeffs.shape, jnp.float32),
            pltpu.VMEM((modes, cells), jnp.bfloat16),
            pltpu.SemaphoreType.DMA((len(held) + 2,)),
            pltpu.SemaphoreType.DMA((tiles,)),
        ],
        compiler_params=pltpu.CompilerParams(vmem_limit_bytes=40 * 2**20),
        cost_estimate=FREE,
        name="rebuild",
    )(me[None], energy[None, :], coeffs, vectors, *held)


def swapped(value, axis, bit):
    route = [(i ^ bit, i) for i in range(lax.axis_size(axis))]
    return lax.ppermute(value, axis, route)


def per_device(eof_basis, snapshots, inverse_energy, eigen_vectors):
    tm, outer, inner = (lax.axis_size(a) for a in ("tm", "outer", "inner"))
    me = lax.axis_index("tm")
    fields = snapshots.T
    hours, rank = fields.shape[0], eof_basis.shape[1]

    held = [fields]
    for k in range(1, tm):
        route = [((i + k) % tm, i) for i in range(tm)]
        held.append(lax.ppermute(fields, "tm", route))

    pieces = project(fields, eof_basis, 8).reshape(inner, hours // inner, rank)
    mine = jnp.sum(lax.all_to_all(pieces, "inner", 0, 0, tiled=True), axis=0)
    bit = 1
    while bit < outer:
        mine = mine + swapped(mine, "outer", bit)
        bit *= 2
    coeffs = lax.all_gather(mine, ("tm", "inner"), axis=0).reshape(tm * hours, rank)

    rows = eigen_vectors.shape[1] // tm
    vectors = lax.dynamic_slice_in_dim(eigen_vectors, me * rows, rows, 1)
    return rebuild(me, inverse_energy, coeffs, vectors.T, held, 8)


def solution(mesh):
    tm, space = mesh.shape["tm"], mesh.shape["space"]
    inner = 1
    while inner * inner < space and space % (2 * inner) == 0:
        inner *= 2
    split = Mesh(mesh.devices.reshape(tm, space // inner, inner), ("tm", "outer", "inner"))
    cells = ("outer", "inner")
    in_specs = (P(cells, None), P(cells, "tm"), P(), P())
    out_specs = (P(), P("tm", cells))
    return jax.shard_map(
        per_device, mesh=split, in_specs=in_specs, out_specs=out_specs, check_vma=False
    )
```

```python
import functools

import jax
import jax.numpy as jnp
from jax import lax
from jax.experimental import pallas as pl
from jax.experimental.pallas import tpu as pltpu
from jax.sharding import Mesh, PartitionSpec as P

ROWS = (((1,), (0,)), ((), ()))
FIRST = (((0,), (0,)), ((), ()))
LAST = (((1,), (1,)), ((), ()))
AHEAD = 4
FREE = pl.CostEstimate(flops=0, bytes_accessed=0, transcendentals=0)


def in_parts(value):
    high = value.astype(jnp.bfloat16)
    return high, (value - high.astype(jnp.float32)).astype(jnp.bfloat16)


def product(left, right, dims):
    return lax.dot_general(left, right, dims, preferred_element_type=jnp.float32)


def project_kernel(tiles, snapshots, basis, out, fields, patterns, arrived):
    cells = snapshots.shape[1]
    tile = cells // tiles
    copies = []
    for i in range(tiles):
        span = pl.ds(i * tile, tile)
        copies.append(
            (
                pltpu.make_async_copy(snapshots.at[:, span], fields.at[:, span], arrived.at[0, i]),
                pltpu.make_async_copy(basis.at[span], patterns.at[span], arrived.at[1, i]),
            )
        )
    for pair in copies[:AHEAD]:
        for copy in pair:
            copy.start()
    total = jnp.zeros(out.shape, jnp.float32)
    for i, pair in enumerate(copies):
        for copy in pair:
            copy.wait()
        for pair in copies[i + AHEAD : i + AHEAD + 1]:
            for copy in pair:
                copy.start()
        span = pl.ds(i * tile, tile)
        total += product(fields[:, span], patterns[span], ROWS)
    out[...] = total


def project(snapshots, basis, tiles):
    hours = snapshots.shape[0]
    rank = basis.shape[1]
    return pl.pallas_call(
        functools.partial(project_kernel, tiles),
        out_shape=jax.ShapeDtypeStruct((hours, rank), jnp.float32),
        in_specs=[pl.BlockSpec(memory_space=pl.ANY)] * 2,
        out_specs=pl.BlockSpec(memory_space=pltpu.VMEM),
        scratch_shapes=[
            pltpu.VMEM(snapshots.shape, snapshots.dtype),
            pltpu.VMEM(basis.shape, basis.dtype),
            pltpu.SemaphoreType.DMA((2, tiles)),
        ],
        compiler_params=pltpu.CompilerParams(vmem_limit_bytes=59 * 2**20),
        cost_estimate=FREE,
        name="project",
    )(snapshots, basis)


def rebuild_kernel(tiles, me, energy, coeffs, vectors, *refs):
    count = len(refs) - 9
    held, refs = refs[:count], refs[count:]
    operator, modes, fields, known, turned, scaled, made, arrived, sent = refs
    hours, cells = held[0].shape
    tile = cells // tiles
    inputs = [
        pltpu.make_async_copy(coeffs, known, arrived.at[count]),
        pltpu.make_async_copy(vectors, turned, arrived.at[count + 1]),
    ]
    blocks = [
        pltpu.make_async_copy(block, fields.at[pl.ds(k * hours, hours)], arrived.at[k])
        for k, block in enumerate(held)
    ]
    for copy in inputs + blocks:
        copy.start()
    for copy in inputs:
        copy.wait()
    every = known[...]
    hour = lax.broadcasted_iota(jnp.int32, every.shape, 0)
    scaled[...] = jnp.where(hour == 0, 0.0, pltpu.roll(every, 1, 0)) * energy[...]
    first = [pl.multiple_of(lax.rem(me[0] + k, count) * hours, hours) for k in range(count)]
    ordered = jnp.concatenate([scaled[pl.ds(at, hours)] for at in first], axis=0)
    high, low = in_parts(ordered)
    weights = (product(turned[...], high, LAST) + product(turned[...], low, LAST)).astype(
        jnp.bfloat16
    )
    for copy in blocks:
        copy.wait()
    outgoing = []
    for i in range(tiles):
        span = pl.ds(i * tile, tile)
        made[:, span] = product(weights, fields[:, span], ROWS).astype(made.dtype)
        copy = pltpu.make_async_copy(made.at[:, span], modes.at[:, span], sent.at[i])
        copy.start()
        outgoing.append(copy)
    high, low = in_parts(every)
    s_high, s_low = in_parts(scaled[...])
    operator[...] = (
        product(high, s_high, FIRST) + product(high, s_low, FIRST) + product(low, s_high, FIRST)
    )
    for copy in outgoing:
        copy.wait()


def rebuild(me, energy, coeffs, vectors, held, tiles):
    cells = held[0].shape[1]
    total, rank = coeffs.shape
    modes = vectors.shape[0]
    anywhere = pl.BlockSpec(memory_space=pl.ANY)
    return pl.pallas_call(
        functools.partial(rebuild_kernel, tiles),
        out_shape=(
            jax.ShapeDtypeStruct((rank, rank), jnp.float32),
            jax.ShapeDtypeStruct((modes, cells), jnp.bfloat16),
        ),
        in_specs=[
            pl.BlockSpec(memory_space=pltpu.SMEM),
            pl.BlockSpec(memory_space=pltpu.VMEM),
        ]
        + [anywhere] * (2 + len(held)),
        out_specs=(pl.BlockSpec(memory_space=pltpu.VMEM), anywhere),
        scratch_shapes=[
            pltpu.VMEM((total, cells), held[0].dtype),
            pltpu.VMEM(coeffs.shape, coeffs.dtype),
            pltpu.VMEM(vectors.shape, vectors.dtype),
            pltpu.VMEM(coeffs.shape, jnp.float32),
            pltpu.VMEM((modes, cells), jnp.bfloat16),
            pltpu.SemaphoreType.DMA((len(held) + 2,)),
            pltpu.SemaphoreType.DMA((tiles,)),
        ],
        compiler_params=pltpu.CompilerParams(vmem_limit_bytes=40 * 2**20),
        cost_estimate=FREE,
        name="rebuild",
    )(me[None], energy[None, :], coeffs, vectors, *held)


def swapped(value, axis, bit):
    route = [(i ^ bit, i) for i in range(lax.axis_size(axis))]
    return lax.ppermute(value, axis, route)


def per_device(eof_basis, snapshots, inverse_energy, eigen_vectors):
    tm, outer, inner = (lax.axis_size(a) for a in ("tm", "outer", "inner"))
    me = lax.axis_index("tm")
    fields = snapshots.T
    hours, rank = fields.shape[0], eof_basis.shape[1]

    held = [fields]
    for k in range(1, tm):
        route = [((i + k) % tm, i) for i in range(tm)]
        held.append(lax.ppermute(fields, "tm", route))

    halves = project(fields, eof_basis, 8).reshape(inner, hours // inner, rank)
    core = lax.axis_index("inner")
    given = lax.dynamic_index_in_dim(halves, 1 - core, 0, keepdims=False)
    kept = lax.dynamic_index_in_dim(halves, core, 0, keepdims=False)
    mine = kept + swapped(given, "inner", 1)
    mine = lax.psum(mine, "outer")
    coeffs = lax.all_gather(mine, ("tm", "inner"), axis=0).reshape(tm * hours, rank)

    rows = eigen_vectors.shape[1] // tm
    vectors = lax.dynamic_slice_in_dim(eigen_vectors, me * rows, rows, 1)
    return rebuild(me, inverse_energy, coeffs, vectors.T, held, 8)


def solution(mesh):
    tm, space = mesh.shape["tm"], mesh.shape["space"]
    inner = 2
    split = Mesh(mesh.devices.reshape(tm, space // inner, inner), ("tm", "outer", "inner"))
    cells = ("outer", "inner")
    in_specs = (P(cells, None), P(cells, "tm"), P(), P())
    out_specs = (P(), P("tm", cells))
    return jax.shard_map(
        per_device, mesh=split, in_specs=in_specs, out_specs=out_specs, check_vma=False
    )
```

```python
import functools

import jax
import jax.numpy as jnp
from jax import lax
from jax.experimental import pallas as pl
from jax.experimental.pallas import tpu as pltpu
from jax.sharding import Mesh, PartitionSpec as P

ROWS = (((1,), (0,)), ((), ()))
FIRST = (((0,), (0,)), ((), ()))
LAST = (((1,), (1,)), ((), ()))
FREE = pl.CostEstimate(flops=0, bytes_accessed=0, transcendentals=0)


def in_parts(value):
    high = value.astype(jnp.bfloat16)
    return high, (value - high.astype(jnp.float32)).astype(jnp.bfloat16)


def product(left, right, dims):
    return lax.dot_general(left, right, dims, preferred_element_type=jnp.float32)


def project_kernel(tiles, core, snapshots, basis, kept, given, fields, patterns, halves, arrived):
    cells = snapshots.shape[1]
    tile = cells // tiles
    copies = []
    for i in range(tiles):
        span = pl.ds(i * tile, tile)
        copies.append(
            (
                pltpu.make_async_copy(snapshots.at[:, span], fields.at[:, span], arrived.at[0, i]),
                pltpu.make_async_copy(basis.at[span], patterns.at[span], arrived.at[1, i]),
            )
        )
    for pair in copies:
        for copy in pair:
            copy.start()
    total = jnp.zeros((fields.shape[0], patterns.shape[1]), jnp.float32)
    for i, pair in enumerate(copies):
        for copy in pair:
            copy.wait()
        span = pl.ds(i * tile, tile)
        total += product(fields[:, span], patterns[span], ROWS)
    half = kept.shape[0]
    halves[0] = total[:half]
    halves[1] = total[half:]
    kept[...] = halves[core[0]]
    given[...] = halves[1 - core[0]]


def project(core, snapshots, basis, tiles):
    hours = snapshots.shape[0]
    rank = basis.shape[1]
    half = jax.ShapeDtypeStruct((hours // 2, rank), jnp.float32)
    return pl.pallas_call(
        functools.partial(project_kernel, tiles),
        out_shape=(half, half),
        in_specs=[pl.BlockSpec(memory_space=pltpu.SMEM)]
        + [pl.BlockSpec(memory_space=pl.ANY)] * 2,
        out_specs=(pl.BlockSpec(memory_space=pltpu.VMEM),) * 2,
        scratch_shapes=[
            pltpu.VMEM(snapshots.shape, snapshots.dtype),
            pltpu.VMEM(basis.shape, basis.dtype),
            pltpu.VMEM((2, hours // 2, rank), jnp.float32),
            pltpu.SemaphoreType.DMA((2, tiles)),
        ],
        compiler_params=pltpu.CompilerParams(vmem_limit_bytes=58 * 2**20),
        cost_estimate=FREE,
        name="project",
    )(core[None], snapshots, basis)


def rebuild_kernel(tiles, place, energy, vectors, *refs):
    count = (len(refs) - 9) // 2
    held, coeffs, refs = refs[:count], refs[count : 2 * count], refs[2 * count :]
    operator, modes, fields, known, turned, scaled, made, arrived, sent = refs
    hours, cells = held[0].shape
    tile = cells // tiles
    half = hours // 2
    first = [pl.multiple_of(lax.rem(place[0] + k, count) * hours, hours) for k in range(count)]
    inputs = [pltpu.make_async_copy(vectors, turned, arrived.at[count])]
    for k, block in enumerate(coeffs):
        for own in range(2):
            at = pl.multiple_of(first[k] + lax.rem(place[1] + own, 2) * half, half)
            inputs.append(
                pltpu.make_async_copy(
                    block.at[own], known.at[pl.ds(at, half)], arrived.at[count + 1 + 2 * k + own]
                )
            )
    blocks = [
        pltpu.make_async_copy(block, fields.at[pl.ds(k * hours, hours)], arrived.at[k])
        for k, block in enumerate(held)
    ]
    for copy in inputs + blocks:
        copy.start()
    for copy in inputs:
        copy.wait()
    every = known[...]
    hour = lax.broadcasted_iota(jnp.int32, every.shape, 0)
    scaled[...] = jnp.where(hour == 0, 0.0, pltpu.roll(every, 1, 0)) * energy[...]
    ordered = jnp.concatenate([scaled[pl.ds(at, hours)] for at in first], axis=0)
    high, low = in_parts(ordered)
    weights = (product(turned[...], high, LAST) + product(turned[...], low, LAST)).astype(
        jnp.bfloat16
    )
    for copy in blocks:
        copy.wait()
    outgoing = []
    for i in range(tiles):
        span = pl.ds(i * tile, tile)
        made[:, span] = product(weights, fields[:, span], ROWS).astype(made.dtype)
        copy = pltpu.make_async_copy(made.at[:, span], modes.at[:, span], sent.at[i])
        copy.start()
        outgoing.append(copy)
    high, low = in_parts(every)
    s_high, s_low = in_parts(scaled[...])
    operator[...] = (
        product(high, s_high, FIRST) + product(high, s_low, FIRST) + product(low, s_high, FIRST)
    )
    for copy in outgoing:
        copy.wait()


def rebuild(place, energy, vectors, held, coeffs, tiles):
    hours, cells = held[0].shape
    total, rank = len(held) * hours, coeffs[0].shape[2]
    modes = vectors.shape[0]
    anywhere = pl.BlockSpec(memory_space=pl.ANY)
    return pl.pallas_call(
        functools.partial(rebuild_kernel, tiles),
        out_shape=(
            jax.ShapeDtypeStruct((rank, rank), jnp.float32),
            jax.ShapeDtypeStruct((modes, cells), jnp.bfloat16),
        ),
        in_specs=[
            pl.BlockSpec(memory_space=pltpu.SMEM),
            pl.BlockSpec(memory_space=pltpu.VMEM),
        ]
        + [anywhere] * (1 + 2 * len(held)),
        out_specs=(pl.BlockSpec(memory_space=pltpu.VMEM), anywhere),
        scratch_shapes=[
            pltpu.VMEM((total, cells), held[0].dtype),
            pltpu.VMEM((total, rank), jnp.float32),
            pltpu.VMEM(vectors.shape, vectors.dtype),
            pltpu.VMEM((total, rank), jnp.float32),
            pltpu.VMEM((modes, cells), jnp.bfloat16),
            pltpu.SemaphoreType.DMA((3 * len(held) + 1,)),
            pltpu.SemaphoreType.DMA((tiles,)),
        ],
        compiler_params=pltpu.CompilerParams(vmem_limit_bytes=40 * 2**20),
        cost_estimate=FREE,
        name="rebuild",
    )(place, energy[None, :], vectors, *held, *coeffs)


def swapped(value, axis, bit):
    route = [(i ^ bit, i) for i in range(lax.axis_size(axis))]
    return lax.ppermute(value, axis, route)


def turned_round(value, axis):
    size = lax.axis_size(axis)
    routes = [[((i + k) % size, i) for i in range(size)] for k in range(1, size)]
    return [value] + [lax.ppermute(value, axis, route) for route in routes]


def per_device(eof_basis, snapshots, inverse_energy, eigen_vectors):
    tm, outer = lax.axis_size("tm"), lax.axis_size("outer")
    me, core = lax.axis_index("tm"), lax.axis_index("inner")
    fields = snapshots.T

    held = turned_round(fields, "tm")

    kept, given = project(core, fields, eof_basis, 8)
    mine = kept + swapped(given, "inner", 1)
    bit = 1
    while bit < outer:
        near = swapped(mine, "outer", bit)
        if 2 * bit < outer:
            far, both = (swapped(mine, "outer", b) for b in (2 * bit, 3 * bit))
            mine = (mine + near) + (far + both)
        else:
            mine = mine + near
        bit *= 4
    coeffs = turned_round(jnp.stack([mine, swapped(mine, "inner", 1)]), "tm")

    rows = eigen_vectors.shape[1] // tm
    vectors = lax.dynamic_slice_in_dim(eigen_vectors, me * rows, rows, 1)
    return rebuild(jnp.stack([me, core]), inverse_energy, vectors.T, held, coeffs, 8)


def solution(mesh):
    tm, space = mesh.shape["tm"], mesh.shape["space"]
    split = Mesh(mesh.devices.reshape(tm, space // 2, 2), ("tm", "outer", "inner"))
    cells = ("outer", "inner")
    in_specs = (P(cells, None), P(cells, "tm"), P(), P())
    out_specs = (P(), P("tm", cells))
    return jax.shard_map(
        per_device, mesh=split, in_specs=in_specs, out_specs=out_specs, check_vma=False
    )
```

```python
import functools

import jax
import jax.numpy as jnp
from jax import lax
from jax.experimental import pallas as pl
from jax.experimental.pallas import tpu as pltpu
from jax.sharding import Mesh, PartitionSpec as P

ROWS = (((1,), (0,)), ((), ()))
FIRST = (((0,), (0,)), ((), ()))
LAST = (((1,), (1,)), ((), ()))
FREE = pl.CostEstimate(flops=0, bytes_accessed=0, transcendentals=0)


def in_parts(value):
    high = value.astype(jnp.bfloat16)
    return high, (value - high.astype(jnp.float32)).astype(jnp.bfloat16)


def product(left, right, dims):
    return lax.dot_general(left, right, dims, preferred_element_type=jnp.float32)


def project_kernel(tiles, core, snapshots, basis, kept, given, fields, patterns, halves, arrived):
    cells = snapshots.shape[1]
    tile = cells // tiles
    copies = []
    for i in range(tiles):
        span = pl.ds(i * tile, tile)
        copies.append(
            (
                pltpu.make_async_copy(snapshots.at[:, span], fields.at[:, span], arrived.at[0, i]),
                pltpu.make_async_copy(basis.at[span], patterns.at[span], arrived.at[1, i]),
            )
        )
    for pair in copies:
        for copy in pair:
            copy.start()
    total = jnp.zeros((fields.shape[0], patterns.shape[1]), jnp.float32)
    for i, pair in enumerate(copies):
        for copy in pair:
            copy.wait()
        span = pl.ds(i * tile, tile)
        total += product(fields[:, span], patterns[span], ROWS)
    half = kept.shape[0]
    halves[0] = total[:half]
    halves[1] = total[half:]
    kept[...] = halves[core[0]]
    given[...] = halves[1 - core[0]]


def project(core, snapshots, basis, tiles):
    hours = snapshots.shape[0]
    rank = basis.shape[1]
    half = jax.ShapeDtypeStruct((hours // 2, rank), jnp.float32)
    return pl.pallas_call(
        functools.partial(project_kernel, tiles),
        out_shape=(half, half),
        in_specs=[pl.BlockSpec(memory_space=pltpu.SMEM)]
        + [pl.BlockSpec(memory_space=pl.ANY)] * 2,
        out_specs=(pl.BlockSpec(memory_space=pltpu.VMEM),) * 2,
        scratch_shapes=[
            pltpu.VMEM(snapshots.shape, snapshots.dtype),
            pltpu.VMEM(basis.shape, basis.dtype),
            pltpu.VMEM((2, hours // 2, rank), jnp.float32),
            pltpu.SemaphoreType.DMA((2, tiles)),
        ],
        compiler_params=pltpu.CompilerParams(vmem_limit_bytes=53 * 2**20),
        cost_estimate=FREE,
        name="project",
    )(core[None], snapshots, basis)


def rebuild_kernel(tiles, place, energy, vectors, *refs):
    count = (len(refs) - 10) // 3
    held, coeffs, refs = refs[:count], refs[count : 3 * count], refs[3 * count :]
    operator, modes, fields, known, turned, scaled, made, square, arrived, sent = refs
    hours, cells = held[0].shape
    half, tile = hours // 2, cells // tiles
    spans = [pl.ds(i * tile, tile) for i in range(tiles)]
    first = [pl.multiple_of(lax.rem(place[0] + k, count) * hours, hours) for k in range(count)]
    inputs = [pltpu.make_async_copy(vectors, turned, arrived.at[tiles, 0])]
    for n, block in enumerate(coeffs):
        at = pl.multiple_of(first[n // 2] + lax.rem(place[1] + n % 2, 2) * half, half)
        inputs.append(
            pltpu.make_async_copy(
                block, known.at[pl.ds(at, half)], arrived.at[tiles + 1 + n % 2, n // 2]
            )
        )
    blocks = [
        [
            pltpu.make_async_copy(
                block.at[:, span], fields.at[pl.ds(k * hours, hours), span], arrived.at[i, k]
            )
            for k, block in enumerate(held)
        ]
        for i, span in enumerate(spans)
    ]
    for copy in inputs + sum(blocks, []):
        copy.start()
    for copy in inputs:
        copy.wait()
    every = known[...]
    hour = lax.broadcasted_iota(jnp.int32, every.shape, 0)
    scaled[...] = jnp.where(hour == 0, 0.0, pltpu.roll(every, 1, 0)) * energy[...]
    ordered = jnp.concatenate([scaled[pl.ds(at, hours)] for at in first], axis=0)
    high, low = in_parts(ordered)
    weights = (product(turned[...], high, LAST) + product(turned[...], low, LAST)).astype(
        jnp.bfloat16
    )
    outgoing = []
    for i, span in enumerate(spans):
        if i == tiles - 1:
            high, low = in_parts(every)
            s_high, s_low = in_parts(scaled[...])
            square[...] = (
                product(high, s_high, FIRST)
                + product(high, s_low, FIRST)
                + product(low, s_high, FIRST)
            )
            outgoing.append(pltpu.make_async_copy(square, operator, sent.at[tiles]))
            outgoing[-1].start()
        for copy in blocks[i]:
            copy.wait()
        made[:, span] = product(weights, fields[:, span], ROWS).astype(made.dtype)
        outgoing.append(pltpu.make_async_copy(made.at[:, span], modes.at[:, span], sent.at[i]))
        outgoing[-1].start()
    for copy in outgoing:
        copy.wait()


def rebuild(place, energy, vectors, held, coeffs, tiles):
    hours, cells = held[0].shape
    total, rank = len(held) * hours, coeffs[0].shape[1]
    modes = vectors.shape[0]
    anywhere = pl.BlockSpec(memory_space=pl.ANY)
    return pl.pallas_call(
        functools.partial(rebuild_kernel, tiles),
        out_shape=(
            jax.ShapeDtypeStruct((rank, rank), jnp.float32),
            jax.ShapeDtypeStruct((modes, cells), jnp.bfloat16),
        ),
        in_specs=[
            pl.BlockSpec(memory_space=pltpu.SMEM),
            pl.BlockSpec(memory_space=pltpu.VMEM),
        ]
        + [anywhere] * (1 + 3 * len(held)),
        out_specs=(anywhere, anywhere),
        scratch_shapes=[
            pltpu.VMEM((total, cells), held[0].dtype),
            pltpu.VMEM((total, rank), jnp.float32),
            pltpu.VMEM(vectors.shape, vectors.dtype),
            pltpu.VMEM((total, rank), jnp.float32),
            pltpu.VMEM((modes, cells), jnp.bfloat16),
            pltpu.VMEM((rank, rank), jnp.float32),
            pltpu.SemaphoreType.DMA((tiles + 3, len(held))),
            pltpu.SemaphoreType.DMA((tiles + 1,)),
        ],
        compiler_params=pltpu.CompilerParams(vmem_limit_bytes=40 * 2**20),
        cost_estimate=FREE,
        name="rebuild",
    )(place, energy[None, :], vectors, *held, *coeffs)


def swapped(value, axis, bit):
    route = [(i ^ bit, i) for i in range(lax.axis_size(axis))]
    return lax.ppermute(value, axis, route)


def moved(value, by, swap):
    size = lax.axis_size("tm")
    route = [
        (2 * ((i + by) % size) + (core ^ swap), 2 * i + core)
        for i in range(size)
        for core in range(2)
    ]
    return lax.ppermute(value, ("tm", "inner"), route)


def per_device(eof_basis, snapshots, inverse_energy, eigen_vectors):
    tm, outer = lax.axis_size("tm"), lax.axis_size("outer")
    me, core = lax.axis_index("tm"), lax.axis_index("inner")
    fields = snapshots.T

    held = [fields] + [moved(fields, k, 0) for k in range(1, tm)]

    kept, given = project(core, fields, eof_basis, 8)
    mine = kept + swapped(given, "inner", 1)
    bit = 1
    while bit < outer:
        near = swapped(mine, "outer", bit)
        if 2 * bit < outer:
            far, both = (swapped(mine, "outer", b) for b in (2 * bit, 3 * bit))
            mine = (mine + near) + (far + both)
        else:
            mine = mine + near
        bit *= 4
    coeffs = [mine, moved(mine, 0, 1)]
    for k in range(1, tm):
        coeffs += [moved(mine, k, 0), moved(mine, k, 1)]

    rows = eigen_vectors.shape[1] // tm
    vectors = lax.dynamic_slice_in_dim(eigen_vectors, me * rows, rows, 1)
    return rebuild(jnp.stack([me, core]), inverse_energy, vectors.T, held, coeffs, 8)


def solution(mesh):
    tm, space = mesh.shape["tm"], mesh.shape["space"]
    split = Mesh(mesh.devices.reshape(tm, space // 2, 2), ("tm", "outer", "inner"))
    cells = ("outer", "inner")
    in_specs = (P(cells, None), P(cells, "tm"), P(), P())
    out_specs = (P(), P("tm", cells))
    return jax.shard_map(
        per_device, mesh=split, in_specs=in_specs, out_specs=out_specs, check_vma=False
    )
```

```python
import functools

import jax
import jax.numpy as jnp
from jax import lax
from jax.experimental import pallas as pl
from jax.experimental.pallas import tpu as pltpu
from jax.sharding import Mesh, PartitionSpec as P

ROWS = (((1,), (0,)), ((), ()))
FIRST = (((0,), (0,)), ((), ()))
LAST = (((1,), (1,)), ((), ()))
FREE = pl.CostEstimate(flops=0, bytes_accessed=0, transcendentals=0)


def in_parts(value):
    high = value.astype(jnp.bfloat16)
    return high, (value - high.astype(jnp.float32)).astype(jnp.bfloat16)


def product(left, right, dims):
    return lax.dot_general(left, right, dims, preferred_element_type=jnp.float32)


def project_kernel(tiles, core, snapshots, basis, kept, given, fields, patterns, halves, arrived):
    cells = snapshots.shape[1]
    tile = cells // tiles
    copies = []
    for i in range(tiles):
        span = pl.ds(i * tile, tile)
        copies.append(
            (
                pltpu.make_async_copy(snapshots.at[:, span], fields.at[:, span], arrived.at[0, i]),
                pltpu.make_async_copy(basis.at[span], patterns.at[span], arrived.at[1, i]),
            )
        )
    for pair in copies:
        for copy in pair:
            copy.start()
    total = jnp.zeros((fields.shape[0], patterns.shape[1]), jnp.float32)
    for i, pair in enumerate(copies):
        for copy in pair:
            copy.wait()
        span = pl.ds(i * tile, tile)
        total += product(fields[:, span], patterns[span], ROWS)
    half = kept.shape[0]
    halves[0] = total[:half]
    halves[1] = total[half:]
    kept[...] = halves[core[0]]
    given[...] = halves[1 - core[0]]


def project(core, snapshots, basis, tiles):
    hours = snapshots.shape[0]
    rank = basis.shape[1]
    half = jax.ShapeDtypeStruct((hours // 2, rank), jnp.float32)
    return pl.pallas_call(
        functools.partial(project_kernel, tiles),
        out_shape=(half, half),
        in_specs=[pl.BlockSpec(memory_space=pltpu.SMEM)]
        + [pl.BlockSpec(memory_space=pl.ANY)] * 2,
        out_specs=(pl.BlockSpec(memory_space=pltpu.VMEM),) * 2,
        scratch_shapes=[
            pltpu.VMEM(snapshots.shape, snapshots.dtype),
            pltpu.VMEM(basis.shape, basis.dtype),
            pltpu.VMEM((2, hours // 2, rank), jnp.float32),
            pltpu.SemaphoreType.DMA((2, tiles)),
        ],
        compiler_params=pltpu.CompilerParams(vmem_limit_bytes=53 * 2**20),
        cost_estimate=FREE,
        name="project",
    )(core[None], snapshots, basis)


def started(copies):
    for copy in copies:
        copy.start()
    return copies


def waited(copies):
    for copy in copies:
        copy.wait()


def gathered(held, fields, arrived):
    rows = held[0].shape[0]
    return [
        pltpu.make_async_copy(block, fields.at[pl.ds(k * rows, rows)], arrived.at[k])
        for k, block in enumerate(held)
    ]


def rebuild_kernel(tiles, place, energy, vectors, coeffs, *refs):
    count = coeffs.shape[0] // 2
    held, refs = refs[:count], refs[count:]
    operator, modes, fields, known, turned, scaled, made, square, arrived, sent = refs
    half = coeffs.shape[1]
    inputs = started(
        [
            pltpu.make_async_copy(coeffs, known, arrived.at[len(held)]),
            pltpu.make_async_copy(vectors, turned, arrived.at[len(held) + 1]),
        ]
    )
    blocks = started(gathered(held, fields, arrived))
    waited(inputs)
    order = [
        2 * lax.rem(count + block - place[0], count) + lax.rem(2 + core - place[1], 2)
        for block in range(count)
        for core in range(2)
    ]
    every = jnp.concatenate([known[at] for at in order], axis=0)
    hour = lax.broadcasted_iota(jnp.int32, every.shape, 0)
    scaled[...] = jnp.where(hour == 0, 0.0, pltpu.roll(every, 1, 0)) * energy[...]
    first = [lax.rem(place[0] + k, count) * 2 * half for k in range(count)]
    ordered = jnp.concatenate(
        [scaled[pl.ds(pl.multiple_of(at, half), 2 * half)] for at in first], axis=0
    )
    high, low = in_parts(ordered)
    weights = (product(turned[...], high, LAST) + product(turned[...], low, LAST)).astype(
        jnp.bfloat16
    )

    waited(blocks)
    width = fields.shape[1] // tiles
    outgoing = []
    for i in range(tiles):
        span = pl.ds(i * width, width)
        if i == tiles - 1:
            high, low = in_parts(every)
            s_high, s_low = in_parts(scaled[...])
            square[...] = (
                product(high, s_high, FIRST)
                + product(high, s_low, FIRST)
                + product(low, s_high, FIRST)
            )
            outgoing += started([pltpu.make_async_copy(square, operator, sent.at[tiles])])
        made[:, span] = product(weights, fields[:, span], ROWS).astype(made.dtype)
        copy = pltpu.make_async_copy(made.at[:, span], modes.at[:, span], sent.at[i])
        outgoing += started([copy])
    waited(outgoing)


ANYWHERE = pl.BlockSpec(memory_space=pl.ANY)
IN_VMEM = pl.BlockSpec(memory_space=pltpu.VMEM)


def rebuild(place, energy, vectors, coeffs, held, tiles):
    cells = held[0].shape[1]
    blocks, half, rank = coeffs.shape
    hours, modes = blocks * half, vectors.shape[0]
    return pl.pallas_call(
        functools.partial(rebuild_kernel, tiles),
        out_shape=(
            jax.ShapeDtypeStruct((rank, rank), jnp.float32),
            jax.ShapeDtypeStruct((modes, cells), jnp.bfloat16),
        ),
        in_specs=[pl.BlockSpec(memory_space=pltpu.SMEM), IN_VMEM]
        + [ANYWHERE] * (2 + len(held)),
        out_specs=(ANYWHERE, ANYWHERE),
        scratch_shapes=[
            pltpu.VMEM((hours, cells), jnp.bfloat16),
            pltpu.VMEM(coeffs.shape, jnp.float32),
            pltpu.VMEM(vectors.shape, vectors.dtype),
            pltpu.VMEM((hours, rank), jnp.float32),
            pltpu.VMEM((modes, cells), jnp.bfloat16),
            pltpu.VMEM((rank, rank), jnp.float32),
            pltpu.SemaphoreType.DMA((len(held) + 2,)),
            pltpu.SemaphoreType.DMA((tiles + 1,)),
        ],
        compiler_params=pltpu.CompilerParams(vmem_limit_bytes=40 * 2**20),
        cost_estimate=FREE,
        name="rebuild",
    )(place, energy[None, :], vectors, coeffs, *held)


def swapped(value, axis, bit):
    route = [(i ^ bit, i) for i in range(lax.axis_size(axis))]
    return lax.ppermute(value, axis, route)


def moved(value, by, swap):
    size = lax.axis_size("tm")
    route = [
        (2 * ((i + by) % size) + (core ^ swap), 2 * i + core)
        for i in range(size)
        for core in range(2)
    ]
    return lax.ppermute(value, ("tm", "inner"), route)


def per_device(eof_basis, snapshots, inverse_energy, eigen_vectors):
    tm, outer = lax.axis_size("tm"), lax.axis_size("outer")
    me, core = lax.axis_index("tm"), lax.axis_index("inner")
    fields = snapshots.T

    held = [fields] + [moved(fields, k, 0) for k in range(1, tm)]

    kept, given = project(core, fields, eof_basis, 8)
    mine = kept + swapped(given, "inner", 1)
    bit = 1
    while bit < outer:
        near = swapped(mine, "outer", bit)
        if 2 * bit < outer:
            far, both = (swapped(mine, "outer", b) for b in (2 * bit, 3 * bit))
            mine = (mine + near) + (far + both)
        else:
            mine = mine + near
        bit *= 4
    coeffs = [mine, moved(mine, 0, 1)]
    for k in range(1, tm):
        coeffs += [moved(mine, k, 0), moved(mine, k, 1)]

    rows = eigen_vectors.shape[1] // tm
    vectors = lax.dynamic_slice_in_dim(eigen_vectors, me * rows, rows, 1)
    place = jnp.stack([me, core])
    return rebuild(place, inverse_energy, vectors.T, jnp.stack(coeffs), held, 4)


def solution(mesh):
    tm, space = mesh.shape["tm"], mesh.shape["space"]
    split = Mesh(mesh.devices.reshape(tm, space // 2, 2), ("tm", "outer", "inner"))
    cells = ("outer", "inner")
    in_specs = (P(cells, None), P(cells, "tm"), P(), P())
    out_specs = (P(), P("tm", cells))
    return jax.shard_map(
        per_device, mesh=split, in_specs=in_specs, out_specs=out_specs, check_vma=False
    )
```

```python
import functools

import jax
import jax.numpy as jnp
from jax import lax
from jax.experimental import pallas as pl
from jax.experimental.pallas import tpu as pltpu
from jax.sharding import Mesh, PartitionSpec as P

ROWS = (((1,), (0,)), ((), ()))
FIRST = (((0,), (0,)), ((), ()))
LAST = (((1,), (1,)), ((), ()))
FREE = pl.CostEstimate(flops=0, bytes_accessed=0, transcendentals=0)
COST_A = pl.CostEstimate(flops=6 * 10**9, bytes_accessed=0, transcendentals=0)


def in_parts(value):
    high = value.astype(jnp.bfloat16)
    return high, (value - high.astype(jnp.float32)).astype(jnp.bfloat16)


def product(left, right, dims):
    return lax.dot_general(left, right, dims, preferred_element_type=jnp.float32)


def project_kernel(tiles, core, snapshots, basis, kept, given, fields, patterns, halves, arrived):
    cells = snapshots.shape[1]
    tile = cells // tiles
    copies = []
    for i in range(tiles):
        span = pl.ds(i * tile, tile)
        copies.append(
            (
                pltpu.make_async_copy(snapshots.at[:, span], fields.at[:, span], arrived.at[0, i]),
                pltpu.make_async_copy(basis.at[span], patterns.at[span], arrived.at[1, i]),
            )
        )
    for pair in copies:
        for copy in pair:
            copy.start()
    total = jnp.zeros((fields.shape[0], patterns.shape[1]), jnp.float32)
    for i, pair in enumerate(copies):
        for copy in pair:
            copy.wait()
        span = pl.ds(i * tile, tile)
        total += product(fields[:, span], patterns[span], ROWS)
    half = kept.shape[0]
    halves[0] = total[:half]
    halves[1] = total[half:]
    kept[...] = halves[core[0]]
    given[...] = halves[1 - core[0]]


def project(core, snapshots, basis, tiles):
    hours = snapshots.shape[0]
    rank = basis.shape[1]
    half = jax.ShapeDtypeStruct((hours // 2, rank), jnp.float32)
    return pl.pallas_call(
        functools.partial(project_kernel, tiles),
        out_shape=(half, half),
        in_specs=[pl.BlockSpec(memory_space=pltpu.SMEM)]
        + [pl.BlockSpec(memory_space=pl.ANY)] * 2,
        out_specs=(pl.BlockSpec(memory_space=pltpu.VMEM),) * 2,
        scratch_shapes=[
            pltpu.VMEM(snapshots.shape, snapshots.dtype),
            pltpu.VMEM(basis.shape, basis.dtype),
            pltpu.VMEM((2, hours // 2, rank), jnp.float32),
            pltpu.SemaphoreType.DMA((2, tiles)),
        ],
        compiler_params=pltpu.CompilerParams(vmem_limit_bytes=53 * 2**20),
        cost_estimate=FREE,
        name="project",
    )(core[None], snapshots, basis)


def started(copies):
    for copy in copies:
        copy.start()
    return copies


def waited(copies):
    for copy in copies:
        copy.wait()


def gathered(held, fields, begin, arrived):
    width = fields.shape[1]
    copies, row = [], 0
    for n, (block, offset) in enumerate(held):
        rows = block.shape[0]
        copies.append(
            pltpu.make_async_copy(
                block.at[:, pl.ds(begin - offset, width)],
                fields.at[pl.ds(row, rows)],
                arrived.at[n],
            )
        )
        row += rows
    return copies


def rebuilt(weights, fields, made, modes, begin, tiles, sent, between):
    width = fields.shape[1] // tiles
    copies = []
    for i in range(tiles):
        span = pl.ds(i * width, width)
        if i == tiles - 1:
            copies += between()
        made[:, span] = product(weights, fields[:, span], ROWS).astype(made.dtype)
        target = modes.at[:, pl.ds(begin + i * width, width)]
        copies += started([pltpu.make_async_copy(made.at[:, span], target, sent.at[i])])
    return copies


def first_kernel(offsets, tiles, place, energy, vectors, coeffs, *refs):
    held, refs = refs[: len(offsets)], refs[len(offsets) :]
    operator, modes, weights, fields, known, turned, scaled, made, square, arrived, sent = refs
    half = coeffs.shape[1]
    count = coeffs.shape[0] // 2
    inputs = started(
        [
            pltpu.make_async_copy(coeffs, known, arrived.at[len(held)]),
            pltpu.make_async_copy(vectors, turned, arrived.at[len(held) + 1]),
        ]
    )
    blocks = started(gathered(list(zip(held, offsets)), fields, 0, arrived))
    waited(inputs)
    order = [
        2 * lax.rem(count + block - place[0], count) + lax.rem(2 + core - place[1], 2)
        for block in range(count)
        for core in range(2)
    ]
    every = jnp.concatenate([known[at] for at in order], axis=0)
    hour = lax.broadcasted_iota(jnp.int32, every.shape, 0)
    scaled[...] = jnp.where(hour == 0, 0.0, pltpu.roll(every, 1, 0)) * energy[...]
    first = [lax.rem(place[0] + k, count) * 2 * half for k in range(count)]
    ordered = jnp.concatenate(
        [scaled[pl.ds(pl.multiple_of(at, half), 2 * half)] for at in first], axis=0
    )
    high, low = in_parts(ordered)
    weights[...] = (product(turned[...], high, LAST) + product(turned[...], low, LAST)).astype(
        jnp.bfloat16
    )

    def rest():
        high, low = in_parts(every)
        s_high, s_low = in_parts(scaled[...])
        square[...] = (
            product(high, s_high, FIRST)
            + product(high, s_low, FIRST)
            + product(low, s_high, FIRST)
        )
        return started([pltpu.make_async_copy(square, operator, sent.at[tiles])])

    waited(blocks)
    waited(rebuilt(weights[...], fields, made, modes, 0, tiles, sent, rest))


def last_kernel(offsets, begin, tiles, weights, *refs):
    held, refs = refs[: len(offsets)], refs[len(offsets) :]
    _, modes, fields, made, arrived, sent = refs
    waited(started(gathered(list(zip(held, offsets)), fields, begin, arrived)))
    waited(rebuilt(weights[...], fields, made, modes, begin, tiles, sent, list))


ANYWHERE = pl.BlockSpec(memory_space=pl.ANY)
IN_VMEM = pl.BlockSpec(memory_space=pltpu.VMEM)


def rebuild_first(place, energy, vectors, coeffs, held, cells, width, tiles):
    blocks, half, rank = coeffs.shape
    hours, modes = blocks * half, vectors.shape[0]
    return pl.pallas_call(
        functools.partial(first_kernel, [0] * len(held), tiles),
        out_shape=(
            jax.ShapeDtypeStruct((rank, rank), jnp.float32),
            jax.ShapeDtypeStruct((modes, cells), jnp.bfloat16),
            jax.ShapeDtypeStruct((modes, hours), jnp.bfloat16),
        ),
        in_specs=[pl.BlockSpec(memory_space=pltpu.SMEM), IN_VMEM]
        + [ANYWHERE] * (2 + len(held)),
        out_specs=(ANYWHERE, ANYWHERE, IN_VMEM),
        scratch_shapes=[
            pltpu.VMEM((hours, width), jnp.bfloat16),
            pltpu.VMEM(coeffs.shape, jnp.float32),
            pltpu.VMEM(vectors.shape, vectors.dtype),
            pltpu.VMEM((hours, rank), jnp.float32),
            pltpu.VMEM((modes, width), jnp.bfloat16),
            pltpu.VMEM((rank, rank), jnp.float32),
            pltpu.SemaphoreType.DMA((len(held) + 2,)),
            pltpu.SemaphoreType.DMA((tiles + 1,)),
        ],
        compiler_params=pltpu.CompilerParams(vmem_limit_bytes=40 * 2**20),
        cost_estimate=COST_A,
        name="rebuild_first",
    )(place, energy[None, :], vectors, coeffs, *held)


def rebuild_last(weights, held, offsets, modes, begin, tiles):
    width = modes.shape[1] - begin
    return pl.pallas_call(
        functools.partial(last_kernel, offsets, begin, tiles),
        out_shape=jax.ShapeDtypeStruct(modes.shape, modes.dtype),
        in_specs=[IN_VMEM] + [ANYWHERE] * (len(held) + 1),
        out_specs=ANYWHERE,
        scratch_shapes=[
            pltpu.VMEM((weights.shape[1], width), jnp.bfloat16),
            pltpu.VMEM((modes.shape[0], width), jnp.bfloat16),
            pltpu.SemaphoreType.DMA((len(held),)),
            pltpu.SemaphoreType.DMA((tiles,)),
        ],
        input_output_aliases={1 + len(held): 0},
        compiler_params=pltpu.CompilerParams(vmem_limit_bytes=40 * 2**20),
        cost_estimate=FREE,
        name="rebuild_last",
    )(weights, *held, modes)


def swapped(value, axis, bit):
    route = [(i ^ bit, i) for i in range(lax.axis_size(axis))]
    return lax.ppermute(value, axis, route)


def moved(value, by, swap):
    size = lax.axis_size("tm")
    route = [
        (2 * ((i + by) % size) + (core ^ swap), 2 * i + core)
        for i in range(size)
        for core in range(2)
    ]
    return lax.ppermute(value, ("tm", "inner"), route)


def per_device(eof_basis, snapshots, inverse_energy, eigen_vectors):
    tm, outer = lax.axis_size("tm"), lax.axis_size("outer")
    me, core = lax.axis_index("tm"), lax.axis_index("inner")
    fields = snapshots.T

    cells = fields.shape[1]
    begin = cells // 4 * 3

    first, last, offsets = [fields], [fields], [0]
    for k in range(1, tm):
        first.append(moved(fields[:, :begin], k, 0))
        offsets.append(begin)

    kept, given = project(core, fields, eof_basis, 8)
    mine = kept + swapped(given, "inner", 1)
    bit = 1
    while bit < outer:
        near = swapped(mine, "outer", bit)
        if 2 * bit < outer:
            far, both = (swapped(mine, "outer", b) for b in (2 * bit, 3 * bit))
            mine = (mine + near) + (far + both)
        else:
            mine = mine + near
        bit *= 4
    mine, rest = lax.optimization_barrier((mine, fields[:, begin:]))
    last += [moved(rest, k, 0) for k in range(1, tm)]
    coeffs = [mine, moved(mine, 0, 1)]
    for k in range(1, tm):
        coeffs += [moved(mine, k, 0), moved(mine, k, 1)]

    rows = eigen_vectors.shape[1] // tm
    vectors = lax.dynamic_slice_in_dim(eigen_vectors, me * rows, rows, 1)
    place = jnp.stack([me, core])
    operator, modes, weights = rebuild_first(
        place, inverse_energy, vectors.T, jnp.stack(coeffs), first, cells, begin, 3
    )
    return operator, rebuild_last(weights, last, offsets, modes, begin, 2)


def solution(mesh):
    tm, space = mesh.shape["tm"], mesh.shape["space"]
    split = Mesh(mesh.devices.reshape(tm, space // 2, 2), ("tm", "outer", "inner"))
    cells = ("outer", "inner")
    in_specs = (P(cells, None), P(cells, "tm"), P(), P())
    out_specs = (P(), P("tm", cells))
    return jax.shard_map(
        per_device, mesh=split, in_specs=in_specs, out_specs=out_specs, check_vma=False
    )
```

```python
import functools

import jax
import jax.numpy as jnp
from jax import lax
from jax.experimental import pallas as pl
from jax.experimental.pallas import tpu as pltpu
from jax.sharding import Mesh, PartitionSpec as P

ROWS = (((1,), (0,)), ((), ()))
FIRST = (((0,), (0,)), ((), ()))
LAST = (((1,), (1,)), ((), ()))
FREE = pl.CostEstimate(flops=0, bytes_accessed=0, transcendentals=0)
COST_A = pl.CostEstimate(flops=6 * 10**9, bytes_accessed=0, transcendentals=0)
ANYWHERE = pl.BlockSpec(memory_space=pl.ANY)
IN_VMEM = pl.BlockSpec(memory_space=pltpu.VMEM)


def started(copies):
    for copy in copies:
        copy.start()
    return copies


def waited(copies):
    for copy in copies:
        copy.wait()


def in_parts(value):
    high = value.astype(jnp.bfloat16)
    return high, (value - high.astype(jnp.float32)).astype(jnp.bfloat16)


def product(left, right, dims):
    return lax.dot_general(left, right, dims, preferred_element_type=jnp.float32)


def cut_kernel(fields, early, late, sent):
    begin = early.shape[1]
    waited(
        started(
            [
                pltpu.make_async_copy(fields.at[:, pl.ds(0, begin)], early, sent.at[0]),
                pltpu.make_async_copy(fields.at[:, pl.ds(begin, late.shape[1])], late, sent.at[1]),
            ]
        )
    )


def cut(fields, begin):
    hours, cells = fields.shape
    return pl.pallas_call(
        cut_kernel,
        out_shape=(
            jax.ShapeDtypeStruct((hours, begin), fields.dtype),
            jax.ShapeDtypeStruct((hours, cells - begin), fields.dtype),
        ),
        in_specs=[ANYWHERE],
        out_specs=(ANYWHERE, ANYWHERE),
        scratch_shapes=[pltpu.SemaphoreType.DMA((2,))],
        compiler_params=pltpu.CompilerParams(vmem_limit_bytes=53 * 2**20),
        cost_estimate=FREE,
        name="cut",
    )(fields)


def project_kernel(tiles, snapshots, basis, kept, given, fields, patterns, halves, arrived):
    cells = snapshots.shape[1]
    tile = cells // tiles
    copies = []
    for i in range(tiles):
        span = pl.ds(i * tile, tile)
        copies.append(
            (
                pltpu.make_async_copy(snapshots.at[:, span], fields.at[:, span], arrived.at[0, i]),
                pltpu.make_async_copy(basis.at[span], patterns.at[span], arrived.at[1, i]),
            )
        )
    for pair in copies:
        for copy in pair:
            copy.start()
    total = jnp.zeros((fields.shape[0], patterns.shape[1]), jnp.float32)
    for i, pair in enumerate(copies):
        for copy in pair:
            copy.wait()
        span = pl.ds(i * tile, tile)
        total += product(fields[:, span], patterns[span], ROWS)
    half = kept.shape[0]
    core = lax.axis_index("inner")
    halves[0] = total[:half]
    halves[1] = total[half:]
    kept[...] = halves[core]
    given[...] = halves[1 - core]


def project(snapshots, basis, tiles):
    hours = snapshots.shape[0]
    rank = basis.shape[1]
    half = jax.ShapeDtypeStruct((hours // 2, rank), jnp.float32)
    return pl.pallas_call(
        functools.partial(project_kernel, tiles),
        out_shape=(half, half),
        in_specs=[ANYWHERE] * 2,
        out_specs=(pl.BlockSpec(memory_space=pltpu.VMEM),) * 2,
        scratch_shapes=[
            pltpu.VMEM(snapshots.shape, snapshots.dtype),
            pltpu.VMEM(basis.shape, basis.dtype),
            pltpu.VMEM((2, hours // 2, rank), jnp.float32),
            pltpu.SemaphoreType.DMA((2, tiles)),
        ],
        compiler_params=pltpu.CompilerParams(vmem_limit_bytes=53 * 2**20),
        cost_estimate=FREE,
        name="project",
    )(snapshots, basis)


def gathered(held, fields, begin, arrived):
    width = fields.shape[1]
    copies, row = [], 0
    for n, (block, offset) in enumerate(held):
        rows = block.shape[0]
        copies.append(
            pltpu.make_async_copy(
                block.at[:, pl.ds(begin - offset, width)],
                fields.at[pl.ds(row, rows)],
                arrived.at[n],
            )
        )
        row += rows
    return copies


def rebuilt(weights, fields, made, modes, begin, tiles, sent):
    width = fields.shape[1] // tiles
    copies = []
    for i in range(tiles):
        span = pl.ds(i * width, width)
        made[:, span] = product(weights, fields[:, span], ROWS).astype(made.dtype)
        target = modes.at[:, pl.ds(begin + i * width, width)]
        copies += started([pltpu.make_async_copy(made.at[:, span], target, sent.at[i])])
    return copies


def by_hours(known):
    me, core = lax.axis_index("tm"), lax.axis_index("inner")
    count = known.shape[0] // 2
    order = [
        2 * lax.rem(count + block - me, count) + lax.rem(2 + half - core, 2)
        for block in range(count)
        for half in range(2)
    ]
    return jnp.concatenate([known[at] for at in order], axis=0)


def lagged_and_scaled(every, energy):
    hour = lax.broadcasted_iota(jnp.int32, every.shape, 0)
    return jnp.where(hour == 0, 0.0, pltpu.roll(every, 1, 0)) * energy


def first_kernel(offsets, tiles, energy, vectors, coeffs, *refs):
    held, refs = refs[: len(offsets)], refs[len(offsets) :]
    modes, weights, fields, known, turned, scale, scaled, made, arrived, sent = refs
    count, hours = coeffs.shape[0] // 2, 2 * coeffs.shape[1]
    inputs = started(
        [
            pltpu.make_async_copy(source, target, arrived.at[len(held) + n])
            for n, (source, target) in enumerate(
                ((coeffs, known), (vectors, turned), (energy, scale))
            )
        ]
    )
    blocks = started(gathered(list(zip(held, offsets)), fields, 0, arrived))
    waited(inputs)
    scaled[...] = lagged_and_scaled(by_hours(known), scale[...])
    me = lax.axis_index("tm")
    first = [lax.rem(me + k, count) * hours for k in range(count)]
    ordered = jnp.concatenate(
        [scaled[pl.ds(pl.multiple_of(at, hours), hours)] for at in first], axis=0
    )
    high, low = in_parts(ordered)
    weights[...] = (product(turned[...], high, LAST) + product(turned[...], low, LAST)).astype(
        jnp.bfloat16
    )
    waited(blocks)
    waited(rebuilt(weights[...], fields, made, modes, 0, tiles, sent))


def operator_kernel(energy, coeffs, operator, scale, known, arrived):
    waited(
        started(
            [
                pltpu.make_async_copy(coeffs, known, arrived.at[0]),
                pltpu.make_async_copy(energy, scale, arrived.at[1]),
            ]
        )
    )
    every = by_hours(known)
    high, low = in_parts(every)
    s_high, s_low = in_parts(lagged_and_scaled(every, scale[...]))
    operator[...] = (
        product(high, s_high, FIRST) + product(high, s_low, FIRST) + product(low, s_high, FIRST)
    )


def last_kernel(offsets, begin, tiles, weights, *refs):
    held, refs = refs[: len(offsets)], refs[len(offsets) :]
    _, modes, fields, made, arrived, sent = refs
    waited(started(gathered(list(zip(held, offsets)), fields, begin, arrived)))
    waited(rebuilt(weights[...], fields, made, modes, begin, tiles, sent))


def rebuild_first(energy, vectors, coeffs, held, cells, width, tiles):
    blocks, half, rank = coeffs.shape
    hours, modes = blocks * half, vectors.shape[0]
    return pl.pallas_call(
        functools.partial(first_kernel, [0] * len(held), tiles),
        out_shape=(
            jax.ShapeDtypeStruct((modes, cells), jnp.bfloat16),
            jax.ShapeDtypeStruct((modes, hours), jnp.bfloat16),
        ),
        in_specs=[ANYWHERE] * (3 + len(held)),
        out_specs=(ANYWHERE, IN_VMEM),
        scratch_shapes=[
            pltpu.VMEM((hours, width), jnp.bfloat16),
            pltpu.VMEM(coeffs.shape, jnp.float32),
            pltpu.VMEM(vectors.shape, vectors.dtype),
            pltpu.VMEM(energy.shape, energy.dtype),
            pltpu.VMEM((hours, rank), jnp.float32),
            pltpu.VMEM((modes, width), jnp.bfloat16),
            pltpu.SemaphoreType.DMA((len(held) + 3,)),
            pltpu.SemaphoreType.DMA((tiles,)),
        ],
        compiler_params=pltpu.CompilerParams(vmem_limit_bytes=40 * 2**20),
        cost_estimate=COST_A,
        name="rebuild_first",
    )(energy, vectors, coeffs, *held)


def operate(energy, coeffs):
    rank = coeffs.shape[2]
    return pl.pallas_call(
        operator_kernel,
        out_shape=jax.ShapeDtypeStruct((rank, rank), jnp.float32),
        in_specs=[ANYWHERE] * 2,
        out_specs=IN_VMEM,
        scratch_shapes=[
            pltpu.VMEM(energy.shape, energy.dtype),
            pltpu.VMEM(coeffs.shape, coeffs.dtype),
            pltpu.SemaphoreType.DMA((2,)),
        ],
        cost_estimate=FREE,
        name="operate",
    )(energy, coeffs)


def rebuild_last(weights, held, offsets, modes, begin, tiles):
    width = modes.shape[1] - begin
    return pl.pallas_call(
        functools.partial(last_kernel, offsets, begin, tiles),
        out_shape=jax.ShapeDtypeStruct(modes.shape, modes.dtype),
        in_specs=[IN_VMEM] + [ANYWHERE] * (len(held) + 1),
        out_specs=ANYWHERE,
        scratch_shapes=[
            pltpu.VMEM((weights.shape[1], width), jnp.bfloat16),
            pltpu.VMEM((modes.shape[0], width), jnp.bfloat16),
            pltpu.SemaphoreType.DMA((len(held),)),
            pltpu.SemaphoreType.DMA((tiles,)),
        ],
        input_output_aliases={1 + len(held): 0},
        compiler_params=pltpu.CompilerParams(vmem_limit_bytes=40 * 2**20),
        cost_estimate=FREE,
        name="rebuild_last",
    )(weights, *held, modes)


def swapped(value, axis, bit):
    route = [(i ^ bit, i) for i in range(lax.axis_size(axis))]
    return lax.ppermute(value, axis, route)


def moved(value, by, swap):
    size = lax.axis_size("tm")
    route = [
        (2 * ((i + by) % size) + (core ^ swap), 2 * i + core)
        for i in range(size)
        for core in range(2)
    ]
    return lax.ppermute(value, ("tm", "inner"), route)


def per_device(eof_basis, snapshots, inverse_energy, eigen_vectors):
    tm, outer = lax.axis_size("tm"), lax.axis_size("outer")
    me = lax.axis_index("tm")
    fields = snapshots.T

    cells = fields.shape[1]
    begin = cells // 16 * 13

    early, late = cut(fields, begin)
    first, last, offsets = [fields], [late], [begin]
    for k in range(1, tm):
        first.append(moved(early, k, 0))
        offsets.append(begin)

    kept, given = project(fields, eof_basis, 8)
    mine = kept + swapped(given, "inner", 1)
    bit = 1
    while bit < outer:
        near = swapped(mine, "outer", bit)
        if 2 * bit < outer:
            far, both = (swapped(mine, "outer", b) for b in (2 * bit, 3 * bit))
            mine = (mine + near) + (far + both)
        else:
            mine = mine + near
        bit *= 4
    mine, late = lax.optimization_barrier((mine, late))
    last += [moved(late, k, 0) for k in range(1, tm)]
    coeffs = [mine, moved(mine, 0, 1)]
    for k in range(1, tm):
        coeffs += [moved(mine, k, 0), moved(mine, k, 1)]

    rows = eigen_vectors.shape[1] // tm
    vectors = lax.dynamic_slice_in_dim(eigen_vectors, me * rows, rows, 1)
    energy, coeffs = inverse_energy[None, :], jnp.stack(coeffs)
    modes, weights = rebuild_first(energy, vectors.T, coeffs, first, cells, begin, 4)
    weights, coeffs = lax.optimization_barrier((weights, coeffs))
    operator = operate(energy, coeffs)
    return operator, rebuild_last(weights, last, offsets, modes, begin, 2)


def solution(mesh):
    tm, space = mesh.shape["tm"], mesh.shape["space"]
    split = Mesh(mesh.devices.reshape(tm, space // 2, 2), ("tm", "outer", "inner"))
    cells = ("outer", "inner")
    in_specs = (P(cells, None), P(cells, "tm"), P(), P())
    out_specs = (P(), P("tm", cells))
    return jax.shard_map(
        per_device, mesh=split, in_specs=in_specs, out_specs=out_specs, check_vma=False
    )
```

```python
import functools

import jax
import jax.numpy as jnp
from jax import lax
from jax.experimental import pallas as pl
from jax.experimental.pallas import tpu as pltpu
from jax.sharding import Mesh, PartitionSpec as P

ROWS = (((1,), (0,)), ((), ()))
FIRST = (((0,), (0,)), ((), ()))
LAST = (((1,), (1,)), ((), ()))
FREE = pl.CostEstimate(flops=0, bytes_accessed=0, transcendentals=0)
COST_A = pl.CostEstimate(flops=10**9, bytes_accessed=0, transcendentals=0)
ANYWHERE = pl.BlockSpec(memory_space=pl.ANY)
IN_VMEM = pl.BlockSpec(memory_space=pltpu.VMEM)


def started(copies):
    for copy in copies:
        copy.start()
    return copies


def waited(copies):
    for copy in copies:
        copy.wait()


def in_parts(value):
    high = value.astype(jnp.bfloat16)
    return high, (value - high.astype(jnp.float32)).astype(jnp.bfloat16)


def product(left, right, dims):
    return lax.dot_general(left, right, dims, preferred_element_type=jnp.float32)


def cut_kernel(fields, early, late, sent):
    begin = early.shape[1]
    waited(
        started(
            [
                pltpu.make_async_copy(fields.at[:, pl.ds(0, begin)], early, sent.at[0]),
                pltpu.make_async_copy(fields.at[:, pl.ds(begin, late.shape[1])], late, sent.at[1]),
            ]
        )
    )


def cut(fields, begin):
    hours, cells = fields.shape
    return pl.pallas_call(
        cut_kernel,
        out_shape=(
            jax.ShapeDtypeStruct((hours, begin), fields.dtype),
            jax.ShapeDtypeStruct((hours, cells - begin), fields.dtype),
        ),
        in_specs=[ANYWHERE],
        out_specs=(ANYWHERE, ANYWHERE),
        scratch_shapes=[pltpu.SemaphoreType.DMA((2,))],
        compiler_params=pltpu.CompilerParams(vmem_limit_bytes=52 * 2**20),
        cost_estimate=FREE,
        name="cut",
    )(fields)


def project_kernel(tiles, snapshots, basis, kept, given, fields, patterns, halves, arrived):
    cells = snapshots.shape[1]
    tile = cells // tiles
    copies = []
    for i in range(tiles):
        span = pl.ds(i * tile, tile)
        copies.append(
            (
                pltpu.make_async_copy(snapshots.at[:, span], fields.at[:, span], arrived.at[0, i]),
                pltpu.make_async_copy(basis.at[span], patterns.at[span], arrived.at[1, i]),
            )
        )
    for pair in copies:
        for copy in pair:
            copy.start()
    total = jnp.zeros((fields.shape[0], patterns.shape[1]), jnp.float32)
    for i, pair in enumerate(copies):
        for copy in pair:
            copy.wait()
        span = pl.ds(i * tile, tile)
        total += product(fields[:, span], patterns[span], ROWS)
    half = kept.shape[0]
    core = lax.axis_index("inner")
    halves[0] = total[:half]
    halves[1] = total[half:]
    kept[...] = halves[core]
    given[...] = halves[1 - core]


def project(snapshots, basis, tiles):
    hours = snapshots.shape[0]
    rank = basis.shape[1]
    half = jax.ShapeDtypeStruct((hours // 2, rank), jnp.float32)
    return pl.pallas_call(
        functools.partial(project_kernel, tiles),
        out_shape=(half, half),
        in_specs=[ANYWHERE] * 2,
        out_specs=(pl.BlockSpec(memory_space=pltpu.VMEM),) * 2,
        scratch_shapes=[
            pltpu.VMEM(snapshots.shape, snapshots.dtype),
            pltpu.VMEM(basis.shape, basis.dtype),
            pltpu.VMEM((2, hours // 2, rank), jnp.float32),
            pltpu.SemaphoreType.DMA((2, tiles)),
        ],
        compiler_params=pltpu.CompilerParams(vmem_limit_bytes=53 * 2**20),
        cost_estimate=FREE,
        name="project",
    )(snapshots, basis)


def gathered(held, fields, begin, arrived):
    width = fields.shape[1]
    copies, row = [], 0
    for n, (block, offset) in enumerate(held):
        rows = block.shape[0]
        copies.append(
            pltpu.make_async_copy(
                block.at[:, pl.ds(begin - offset, width)],
                fields.at[pl.ds(row, rows)],
                arrived.at[n],
            )
        )
        row += rows
    return copies


def rebuilt(weights, fields, made, modes, begin, tiles, sent, between):
    width = fields.shape[1] // tiles
    copies = []
    for i in range(tiles):
        span = pl.ds(i * width, width)
        if i == tiles - 1:
            copies += between()
        made[:, span] = product(weights, fields[:, span], ROWS).astype(made.dtype)
        target = modes.at[:, pl.ds(begin + i * width, width)]
        copies += started([pltpu.make_async_copy(made.at[:, span], target, sent.at[i])])
    return copies


def by_hours(known):
    me, core = lax.axis_index("tm"), lax.axis_index("inner")
    count = known.shape[0] // 2
    order = [
        2 * lax.rem(count + block - me, count) + lax.rem(2 + half - core, 2)
        for block in range(count)
        for half in range(2)
    ]
    return jnp.concatenate([known[at] for at in order], axis=0)


def lagged_and_scaled(every, energy):
    hour = lax.broadcasted_iota(jnp.int32, every.shape, 0)
    return jnp.where(hour == 0, 0.0, pltpu.roll(every, 1, 0)) * energy


def first_kernel(offsets, tiles, energy, vectors, coeffs, *refs):
    held, refs = refs[: len(offsets)], refs[len(offsets) :]
    operator, modes, weights, fields, known, turned, scale, scaled, made, square, arrived, sent = refs
    count, hours = coeffs.shape[0] // 2, 2 * coeffs.shape[1]
    inputs = started(
        [
            pltpu.make_async_copy(source, target, arrived.at[len(held) + n])
            for n, (source, target) in enumerate(
                ((coeffs, known), (vectors, turned), (energy, scale))
            )
        ]
    )
    blocks = started(gathered(list(zip(held, offsets)), fields, 0, arrived))
    waited(inputs)
    every = by_hours(known)
    scaled[...] = lagged_and_scaled(every, scale[...])
    me = lax.axis_index("tm")
    first = [lax.rem(me + k, count) * hours for k in range(count)]
    ordered = jnp.concatenate(
        [scaled[pl.ds(pl.multiple_of(at, hours), hours)] for at in first], axis=0
    )
    high, low = in_parts(ordered)
    weights[...] = (product(turned[...], high, LAST) + product(turned[...], low, LAST)).astype(
        jnp.bfloat16
    )
    waited(blocks)

    def rest():
        high, low = in_parts(every)
        s_high, s_low = in_parts(scaled[...])
        square[...] = (
            product(high, s_high, FIRST)
            + product(high, s_low, FIRST)
            + product(low, s_high, FIRST)
        )
        return started([pltpu.make_async_copy(square, operator, sent.at[tiles])])

    waited(rebuilt(weights[...], fields, made, modes, 0, tiles, sent, rest))


def last_kernel(offsets, begin, tiles, weights, *refs):
    held, refs = refs[: len(offsets)], refs[len(offsets) :]
    _, modes, fields, made, arrived, sent = refs
    waited(started(gathered(list(zip(held, offsets)), fields, begin, arrived)))
    waited(rebuilt(weights[...], fields, made, modes, begin, tiles, sent, list))


def rebuild_first(energy, vectors, coeffs, held, cells, width, tiles):
    blocks, half, rank = coeffs.shape
    hours, modes = blocks * half, vectors.shape[0]
    return pl.pallas_call(
        functools.partial(first_kernel, [0] * len(held), tiles),
        out_shape=(
            jax.ShapeDtypeStruct((rank, rank), jnp.float32),
            jax.ShapeDtypeStruct((modes, cells), jnp.bfloat16),
            jax.ShapeDtypeStruct((modes, hours), jnp.bfloat16),
        ),
        in_specs=[ANYWHERE] * (3 + len(held)),
        out_specs=(ANYWHERE, ANYWHERE, IN_VMEM),
        scratch_shapes=[
            pltpu.VMEM((hours, width), jnp.bfloat16),
            pltpu.VMEM(coeffs.shape, jnp.float32),
            pltpu.VMEM(vectors.shape, vectors.dtype),
            pltpu.VMEM(energy.shape, energy.dtype),
            pltpu.VMEM((hours, rank), jnp.float32),
            pltpu.VMEM((modes, width), jnp.bfloat16),
            pltpu.VMEM((rank, rank), jnp.float32),
            pltpu.SemaphoreType.DMA((len(held) + 3,)),
            pltpu.SemaphoreType.DMA((tiles + 1,)),
        ],
        compiler_params=pltpu.CompilerParams(vmem_limit_bytes=40 * 2**20),
        cost_estimate=COST_A,
        name="rebuild_first",
    )(energy, vectors, coeffs, *held)


def rebuild_last(weights, held, offsets, modes, begin, tiles):
    width = modes.shape[1] - begin
    return pl.pallas_call(
        functools.partial(last_kernel, offsets, begin, tiles),
        out_shape=jax.ShapeDtypeStruct(modes.shape, modes.dtype),
        in_specs=[IN_VMEM] + [ANYWHERE] * (len(held) + 1),
        out_specs=ANYWHERE,
        scratch_shapes=[
            pltpu.VMEM((weights.shape[1], width), jnp.bfloat16),
            pltpu.VMEM((modes.shape[0], width), jnp.bfloat16),
            pltpu.SemaphoreType.DMA((len(held),)),
            pltpu.SemaphoreType.DMA((tiles,)),
        ],
        input_output_aliases={1 + len(held): 0},
        compiler_params=pltpu.CompilerParams(vmem_limit_bytes=40 * 2**20),
        cost_estimate=FREE,
        name="rebuild_last",
    )(weights, *held, modes)


def swapped(value, axis, bit):
    route = [(i ^ bit, i) for i in range(lax.axis_size(axis))]
    return lax.ppermute(value, axis, route)


def moved(value, by, swap):
    size = lax.axis_size("tm")
    route = [
        (2 * ((i + by) % size) + (core ^ swap), 2 * i + core)
        for i in range(size)
        for core in range(2)
    ]
    return lax.ppermute(value, ("tm", "inner"), route)


def per_device(eof_basis, snapshots, inverse_energy, eigen_vectors):
    tm, outer = lax.axis_size("tm"), lax.axis_size("outer")
    me = lax.axis_index("tm")
    fields = snapshots.T

    cells = fields.shape[1]
    begin = cells // 4 * 3

    early, late = cut(fields, begin)
    first, last, offsets = [fields], [fields], [0]
    for k in range(1, tm):
        first.append(moved(early, k, 0))
        offsets.append(begin)

    kept, given = project(fields, eof_basis, 8)
    mine = kept + swapped(given, "inner", 1)
    bit = 1
    while bit < outer:
        near = swapped(mine, "outer", bit)
        if 2 * bit < outer:
            far, both = (swapped(mine, "outer", b) for b in (2 * bit, 3 * bit))
            mine = (mine + near) + (far + both)
        else:
            mine = mine + near
        bit *= 4
    mine, late = lax.optimization_barrier((mine, late))
    last += [moved(late, k, 0) for k in range(1, tm)]
    coeffs = [mine, moved(mine, 0, 1)]
    for k in range(1, tm):
        theirs = moved(mine, k, 0)
        coeffs += [theirs, moved(theirs, 0, 1)]

    rows = eigen_vectors.shape[1] // tm
    vectors = lax.dynamic_slice_in_dim(eigen_vectors, me * rows, rows, 1)
    energy, coeffs = inverse_energy[None, :], jnp.stack(coeffs)
    operator, modes, weights = rebuild_first(energy, vectors.T, coeffs, first, cells, begin, 3)
    return operator, rebuild_last(weights, last, offsets, modes, begin, 2)


def solution(mesh):
    tm, space = mesh.shape["tm"], mesh.shape["space"]
    split = Mesh(mesh.devices.reshape(tm, space // 2, 2), ("tm", "outer", "inner"))
    cells = ("outer", "inner")
    in_specs = (P(cells, None), P(cells, "tm"), P(), P())
    out_specs = (P(), P("tm", cells))
    return jax.shard_map(
        per_device, mesh=split, in_specs=in_specs, out_specs=out_specs, check_vma=False
    )
```

```python
import functools

import jax
import jax.numpy as jnp
from jax import lax
from jax.experimental import pallas as pl
from jax.experimental.pallas import tpu as pltpu
from jax.sharding import Mesh, PartitionSpec as P

ROWS = (((1,), (0,)), ((), ()))
FIRST = (((0,), (0,)), ((), ()))
LAST = (((1,), (1,)), ((), ()))
STRIP = 256
FREE = pl.CostEstimate(flops=0, bytes_accessed=0, transcendentals=0)
ANYWHERE = pl.BlockSpec(memory_space=pl.ANY)
IN_VMEM = pl.BlockSpec(memory_space=pltpu.VMEM)


def started(copies):
    for copy in copies:
        copy.start()
    return copies


def waited(copies):
    for copy in copies:
        copy.wait()


def in_parts(value):
    high = value.astype(jnp.bfloat16)
    return high, (value - high.astype(jnp.float32)).astype(jnp.bfloat16)


def product(left, right, dims):
    return lax.dot_general(left, right, dims, preferred_element_type=jnp.float32)


def project_kernel(tiles, snapshots, basis, kept, given, fields, patterns, halves, arrived):
    cells = snapshots.shape[1]
    tile = cells // tiles
    copies = []
    for i in range(tiles):
        span = pl.ds(i * tile, tile)
        copies.append(
            (
                pltpu.make_async_copy(snapshots.at[:, span], fields.at[:, span], arrived.at[0, i]),
                pltpu.make_async_copy(basis.at[span], patterns.at[span], arrived.at[1, i]),
            )
        )
    for pair in copies:
        for copy in pair:
            copy.start()
    total = jnp.zeros((fields.shape[0], patterns.shape[1]), jnp.float32)
    for i, pair in enumerate(copies):
        for copy in pair:
            copy.wait()
        span = pl.ds(i * tile, tile)
        total += product(fields[:, span], patterns[span], ROWS)
    half = kept.shape[0]
    core = lax.axis_index("inner")
    halves[0] = total[:half]
    halves[1] = total[half:]
    kept[...] = halves[core]
    given[...] = halves[1 - core]


def project(snapshots, basis, tiles):
    hours = snapshots.shape[0]
    rank = basis.shape[1]
    half = jax.ShapeDtypeStruct((hours // 2, rank), jnp.float32)
    return pl.pallas_call(
        functools.partial(project_kernel, tiles),
        out_shape=(half, half),
        in_specs=[ANYWHERE] * 2,
        out_specs=(pl.BlockSpec(memory_space=pltpu.VMEM),) * 2,
        scratch_shapes=[
            pltpu.VMEM(snapshots.shape, snapshots.dtype),
            pltpu.VMEM(basis.shape, basis.dtype),
            pltpu.VMEM((2, hours // 2, rank), jnp.float32),
            pltpu.SemaphoreType.DMA((2, tiles)),
        ],
        compiler_params=pltpu.CompilerParams(vmem_limit_bytes=53 * 2**20),
        cost_estimate=FREE,
        name="project",
    )(snapshots, basis)


def gathered(held, fields, begin, width, arrived):
    rows = held[0].shape[0]
    span = pl.ds(begin, width)
    return [
        pltpu.make_async_copy(
            block.at[:, span], fields.at[pl.ds(k * rows, rows), span], arrived.at[k]
        )
        for k, block in enumerate(held)
    ]


def by_hours(known):
    me, core = lax.axis_index("tm"), lax.axis_index("inner")
    count = known.shape[0] // 2
    order = [
        2 * lax.rem(count + block - me, count) + lax.rem(2 + half - core, 2)
        for block in range(count)
        for half in range(2)
    ]
    return jnp.concatenate([known[at] for at in order], axis=0)


def lagged_and_scaled(every, energy):
    hour = lax.broadcasted_iota(jnp.int32, every.shape, 0)
    return jnp.where(hour == 0, 0.0, pltpu.roll(every, 1, 0)) * energy


def rebuild_kernel(parts, tiles, energy, vectors, coeffs, *refs):
    count, hours = coeffs.shape[0] // 2, 2 * coeffs.shape[1]
    held, refs = refs[:count], refs[count:]
    operator, modes, fields, known, turned, scale, scaled, made, square, arrived, sent = refs
    cells = modes.shape[1]
    sources = ((coeffs, known), (vectors, turned), (energy, scale))
    inputs = started(
        [
            pltpu.make_async_copy(source, target, arrived.at[parts + n, 0])
            for n, (source, target) in enumerate(sources)
        ]
    )
    width = cells // parts
    blocks = [
        started(gathered(held, fields, i * width, width, arrived.at[i])) for i in range(parts)
    ]
    waited(inputs)
    every = by_hours(known)
    scaled[...] = lagged_and_scaled(every.astype(jnp.float32), scale[...])
    me = lax.axis_index("tm")
    first = [lax.rem(me + k, count) * hours for k in range(count)]
    ordered = jnp.concatenate(
        [scaled[pl.ds(pl.multiple_of(at, hours), hours)] for at in first], axis=0
    )
    high, low = in_parts(ordered)
    weights = (product(turned[...], high, LAST) + product(turned[...], low, LAST)).astype(
        jnp.bfloat16
    )
    width = cells // tiles
    outgoing = []
    for i in range(tiles):
        if i % (tiles // parts) == 0:
            waited(blocks[i // (tiles // parts)])
        if i == tiles - 1:
            high, low = in_parts(scaled[...])
            square[...] = product(every, high, FIRST) + product(every, low, FIRST)
            outgoing += started([pltpu.make_async_copy(square, operator, sent.at[tiles])])
        for at in range(i * width, (i + 1) * width, STRIP):
            span = pl.ds(at, STRIP)
            made[:, span] = product(weights, fields[:, span], ROWS).astype(made.dtype)
        span = pl.ds(i * width, width)
        copy = pltpu.make_async_copy(made.at[:, span], modes.at[:, span], sent.at[i])
        outgoing += started([copy])
    waited(outgoing)


def rebuild(energy, vectors, coeffs, held, parts, tiles):
    blocks, half, rank = coeffs.shape
    hours, modes, cells = blocks * half, vectors.shape[0], held[0].shape[1]
    return pl.pallas_call(
        functools.partial(rebuild_kernel, parts, tiles),
        out_shape=(
            jax.ShapeDtypeStruct((rank, rank), jnp.float32),
            jax.ShapeDtypeStruct((modes, cells), jnp.bfloat16),
        ),
        in_specs=[ANYWHERE] * (3 + len(held)),
        out_specs=(ANYWHERE, ANYWHERE),
        scratch_shapes=[
            pltpu.VMEM((hours, cells), jnp.bfloat16),
            pltpu.VMEM(coeffs.shape, coeffs.dtype),
            pltpu.VMEM(vectors.shape, vectors.dtype),
            pltpu.VMEM(energy.shape, energy.dtype),
            pltpu.VMEM((hours, rank), jnp.float32),
            pltpu.VMEM((modes, cells), jnp.bfloat16),
            pltpu.VMEM((rank, rank), jnp.float32),
            pltpu.SemaphoreType.DMA((parts + 3, len(held))),
            pltpu.SemaphoreType.DMA((tiles + 1,)),
        ],
        compiler_params=pltpu.CompilerParams(vmem_limit_bytes=40 * 2**20),
        cost_estimate=FREE,
        name="rebuild",
    )(energy, vectors, coeffs, *held)


def swapped(value, axis, bit):
    route = [(i ^ bit, i) for i in range(lax.axis_size(axis))]
    return lax.ppermute(value, axis, route)


def moved(value, by, swap):
    size = lax.axis_size("tm")
    route = [
        (2 * ((i + by) % size) + (core ^ swap), 2 * i + core)
        for i in range(size)
        for core in range(2)
    ]
    return lax.ppermute(value, ("tm", "inner"), route)


def per_device(eof_basis, snapshots, inverse_energy, eigen_vectors):
    tm, outer = lax.axis_size("tm"), lax.axis_size("outer")
    me = lax.axis_index("tm")
    fields = snapshots.T

    held = [fields] + [moved(fields, k, 0) for k in range(1, tm)]

    kept, given = project(fields, eof_basis, 8)
    mine = kept + swapped(given, "inner", 1)
    bit = 1
    while bit < outer:
        near = swapped(mine, "outer", bit)
        if 2 * bit < outer:
            far, both = (swapped(mine, "outer", b) for b in (2 * bit, 3 * bit))
            mine = (mine + near) + (far + both)
        else:
            mine = mine + near
        bit *= 4
    mine = mine.astype(jnp.bfloat16)
    coeffs = [mine, moved(mine, 0, 1)]
    for k in range(1, tm):
        coeffs += [moved(mine, k, 0), moved(mine, k, 1)]

    rows = eigen_vectors.shape[1] // tm
    vectors = lax.dynamic_slice_in_dim(eigen_vectors, me * rows, rows, 1)
    energy, coeffs = inverse_energy[None, :], jnp.stack(coeffs)
    return rebuild(energy, vectors.T, coeffs, held, 2, 4)


def solution(mesh):
    tm, space = mesh.shape["tm"], mesh.shape["space"]
    split = Mesh(mesh.devices.reshape(tm, space // 2, 2), ("tm", "outer", "inner"))
    cells = ("outer", "inner")
    in_specs = (P(cells, None), P(cells, "tm"), P(), P())
    out_specs = (P(), P("tm", cells))
    return jax.shard_map(
        per_device, mesh=split, in_specs=in_specs, out_specs=out_specs, check_vma=False
    )
```

```python
import functools

import jax
import jax.numpy as jnp
from jax import lax
from jax.experimental import pallas as pl
from jax.experimental.pallas import tpu as pltpu
from jax.sharding import Mesh, PartitionSpec as P

ROWS = (((1,), (0,)), ((), ()))
FIRST = (((0,), (0,)), ((), ()))
LAST = (((1,), (1,)), ((), ()))
STRIP = 256
FREE = pl.CostEstimate(flops=0, bytes_accessed=0, transcendentals=0)
ANYWHERE = pl.BlockSpec(memory_space=pl.ANY)
IN_VMEM = pl.BlockSpec(memory_space=pltpu.VMEM)


def started(copies):
    for copy in copies:
        copy.start()
    return copies


def waited(copies):
    for copy in copies:
        copy.wait()


def in_parts(value):
    high = value.astype(jnp.bfloat16)
    return high, (value - high.astype(jnp.float32)).astype(jnp.bfloat16)


def product(left, right, dims):
    return lax.dot_general(left, right, dims, preferred_element_type=jnp.float32)


def project_kernel(tiles, snapshots, basis, kept, given, fields, patterns, halves, arrived):
    cells = snapshots.shape[1]
    tile = cells // tiles
    copies = []
    for i in range(tiles):
        span = pl.ds(i * tile, tile)
        copies.append(
            (
                pltpu.make_async_copy(snapshots.at[:, span], fields.at[:, span], arrived.at[0, i]),
                pltpu.make_async_copy(basis.at[span], patterns.at[span], arrived.at[1, i]),
            )
        )
    for pair in copies:
        for copy in pair:
            copy.start()
    total = jnp.zeros((fields.shape[0], patterns.shape[1]), jnp.float32)
    for i, pair in enumerate(copies):
        for copy in pair:
            copy.wait()
        span = pl.ds(i * tile, tile)
        total += product(fields[:, span], patterns[span], ROWS)
    half = kept.shape[0]
    core = lax.axis_index("inner")
    halves[0] = total[:half]
    halves[1] = total[half:]
    kept[...] = halves[core]
    given[...] = halves[1 - core]


def project(snapshots, basis, tiles):
    hours = snapshots.shape[0]
    rank = basis.shape[1]
    half = jax.ShapeDtypeStruct((hours // 2, rank), jnp.float32)
    return pl.pallas_call(
        functools.partial(project_kernel, tiles),
        out_shape=(half, half),
        in_specs=[ANYWHERE] * 2,
        out_specs=(pl.BlockSpec(memory_space=pltpu.VMEM),) * 2,
        scratch_shapes=[
            pltpu.VMEM(snapshots.shape, snapshots.dtype),
            pltpu.VMEM(basis.shape, basis.dtype),
            pltpu.VMEM((2, hours // 2, rank), jnp.float32),
            pltpu.SemaphoreType.DMA((2, tiles)),
        ],
        compiler_params=pltpu.CompilerParams(vmem_limit_bytes=53 * 2**20),
        cost_estimate=FREE,
        name="project",
    )(snapshots, basis)


def gathered(held, fields, begin, width, arrived):
    rows = held[0].shape[0]
    span = pl.ds(begin, width)
    return [
        pltpu.make_async_copy(
            block.at[:, span], fields.at[pl.ds(k * rows, rows), span], arrived.at[k]
        )
        for k, block in enumerate(held)
    ]


def by_hours(known):
    me, core = lax.axis_index("tm"), lax.axis_index("inner")
    count = known.shape[0] // 2
    order = [
        2 * lax.rem(count + block - me, count) + lax.rem(2 + half - core, 2)
        for block in range(count)
        for half in range(2)
    ]
    return jnp.concatenate([known[at] for at in order], axis=0)


def lagged_and_scaled(every, energy):
    hour = lax.broadcasted_iota(jnp.int32, every.shape, 0)
    return jnp.where(hour == 0, 0.0, pltpu.roll(every, 1, 0)) * energy


def rebuild_kernel(parts, tiles, energy, vectors, *refs):
    count = (len(refs) - 11) // 2
    held, coeffs, refs = refs[:count], refs[count : 2 * count], refs[2 * count :]
    operator, modes, fields, known, turned, scale, scaled, made, square, arrived, sent = refs
    hours, cells = held[0].shape
    inputs = started(
        [
            pltpu.make_async_copy(block, known.at[pl.ds(2 * k, 2)], arrived.at[parts, k])
            for k, block in enumerate(coeffs)
        ]
        + [
            pltpu.make_async_copy(energy, scale, arrived.at[parts + 1, 0]),
            pltpu.make_async_copy(vectors, turned, arrived.at[parts + 2, 0]),
        ]
    )
    width = cells // parts
    blocks = [
        started(gathered(held, fields, i * width, width, arrived.at[i])) for i in range(parts)
    ]
    waited(inputs)
    every = by_hours(known)
    scaled[...] = lagged_and_scaled(every.astype(jnp.float32), scale[...])
    me = lax.axis_index("tm")
    first = [lax.rem(me + k, count) * hours for k in range(count)]
    ordered = jnp.concatenate(
        [scaled[pl.ds(pl.multiple_of(at, hours), hours)] for at in first], axis=0
    )
    high, low = in_parts(ordered)
    weights = (product(turned[...], high, LAST) + product(turned[...], low, LAST)).astype(
        jnp.bfloat16
    )
    width = cells // tiles
    outgoing = []
    for i in range(tiles):
        if i % (tiles // parts) == 0:
            waited(blocks[i // (tiles // parts)])
        for at in range(i * width, (i + 1) * width, STRIP):
            span = pl.ds(at, STRIP)
            made[:, span] = product(weights, fields[:, span], ROWS).astype(made.dtype)
        span = pl.ds(i * width, width)
        copy = pltpu.make_async_copy(made.at[:, span], modes.at[:, span], sent.at[i])
        outgoing += started([copy])
    high, low = in_parts(scaled[...])
    square[...] = product(every, high, FIRST) + product(every, low, FIRST)
    outgoing += started([pltpu.make_async_copy(square, operator, sent.at[tiles])])
    waited(outgoing)


def rebuild(energy, vectors, held, coeffs, parts, tiles):
    _, half, rank = coeffs[0].shape
    hours, cells = held[0].shape
    hours, modes = len(held) * hours, vectors.shape[0]
    return pl.pallas_call(
        functools.partial(rebuild_kernel, parts, tiles),
        out_shape=(
            jax.ShapeDtypeStruct((rank, rank), jnp.float32),
            jax.ShapeDtypeStruct((modes, cells), jnp.bfloat16),
        ),
        in_specs=[ANYWHERE] * (2 + 2 * len(held)),
        out_specs=(ANYWHERE, ANYWHERE),
        scratch_shapes=[
            pltpu.VMEM((hours, cells), jnp.bfloat16),
            pltpu.VMEM((2 * len(held), half, rank), coeffs[0].dtype),
            pltpu.VMEM(vectors.shape, vectors.dtype),
            pltpu.VMEM(energy.shape, energy.dtype),
            pltpu.VMEM((hours, rank), jnp.float32),
            pltpu.VMEM((modes, cells), jnp.bfloat16),
            pltpu.VMEM((rank, rank), jnp.float32),
            pltpu.SemaphoreType.DMA((parts + 3, len(held))),
            pltpu.SemaphoreType.DMA((tiles + 1,)),
        ],
        compiler_params=pltpu.CompilerParams(vmem_limit_bytes=40 * 2**20),
        cost_estimate=FREE,
        name="rebuild",
    )(energy, vectors, *held, *coeffs)


def swapped(value, axis, bit):
    route = [(i ^ bit, i) for i in range(lax.axis_size(axis))]
    return lax.ppermute(value, axis, route)


def moved(value, by, swap):
    size = lax.axis_size("tm")
    route = [
        (2 * ((i + by) % size) + (core ^ swap), 2 * i + core)
        for i in range(size)
        for core in range(2)
    ]
    return lax.ppermute(value, ("tm", "inner"), route)


def per_device(eof_basis, snapshots, inverse_energy, eigen_vectors):
    tm, outer = lax.axis_size("tm"), lax.axis_size("outer")
    me = lax.axis_index("tm")
    fields = snapshots.T

    held = [fields] + [moved(fields, k, 0) for k in range(1, tm)]

    kept, given = project(fields, eof_basis, 8)
    mine = kept + swapped(given, "inner", 1)
    bit = 1
    while bit < outer:
        near = swapped(mine, "outer", bit)
        if 2 * bit < outer:
            far, both = (swapped(mine, "outer", b) for b in (2 * bit, 3 * bit))
            mine = (mine + near) + (far + both)
        else:
            mine = mine + near
        bit *= 4
    mine = mine.astype(jnp.bfloat16)
    both = jnp.stack([mine, moved(mine, 0, 1)])
    coeffs = [both] + [moved(both, k, 0) for k in range(1, tm)]

    rows = eigen_vectors.shape[1] // tm
    vectors = lax.dynamic_slice_in_dim(eigen_vectors, me * rows, rows, 1)
    return rebuild(inverse_energy[None, :], vectors.T, held, coeffs, 2, 4)


def solution(mesh):
    tm, space = mesh.shape["tm"], mesh.shape["space"]
    split = Mesh(mesh.devices.reshape(tm, space // 2, 2), ("tm", "outer", "inner"))
    cells = ("outer", "inner")
    in_specs = (P(cells, None), P(cells, "tm"), P(), P())
    out_specs = (P(), P("tm", cells))
    return jax.shard_map(
        per_device, mesh=split, in_specs=in_specs, out_specs=out_specs, check_vma=False
    )
```

```python
import functools

import jax
import jax.numpy as jnp
from jax import lax
from jax.experimental import pallas as pl
from jax.experimental.pallas import tpu as pltpu
from jax.sharding import Mesh, PartitionSpec as P

ROWS = (((1,), (0,)), ((), ()))
FIRST = (((0,), (0,)), ((), ()))
LAST = (((1,), (1,)), ((), ()))
STRIP = 256
FREE = pl.CostEstimate(flops=0, bytes_accessed=0, transcendentals=0)
ANYWHERE = pl.BlockSpec(memory_space=pl.ANY)
IN_VMEM = pl.BlockSpec(memory_space=pltpu.VMEM)


def started(copies):
    for copy in copies:
        copy.start()
    return copies


def waited(copies):
    for copy in copies:
        copy.wait()


def in_parts(value):
    high = value.astype(jnp.bfloat16)
    return high, (value - high.astype(jnp.float32)).astype(jnp.bfloat16)


def product(left, right, dims):
    return lax.dot_general(left, right, dims, preferred_element_type=jnp.float32)


def project_kernel(tiles, snapshots, basis, kept, given, fields, patterns, halves, arrived):
    cells = snapshots.shape[1]
    tile = cells // tiles
    copies = []
    for i in range(tiles):
        span = pl.ds(i * tile, tile)
        copies.append(
            (
                pltpu.make_async_copy(snapshots.at[:, span], fields.at[:, span], arrived.at[0, i]),
                pltpu.make_async_copy(basis.at[span], patterns.at[span], arrived.at[1, i]),
            )
        )
    for pair in copies:
        for copy in pair:
            copy.start()
    total = jnp.zeros((fields.shape[0], patterns.shape[1]), jnp.float32)
    for i, pair in enumerate(copies):
        for copy in pair:
            copy.wait()
        span = pl.ds(i * tile, tile)
        total += product(fields[:, span], patterns[span], ROWS)
    half = kept.shape[0]
    core = lax.axis_index("inner")
    halves[0] = total[:half]
    halves[1] = total[half:]
    kept[...] = halves[core]
    given[...] = halves[1 - core]


def project(snapshots, basis, tiles):
    hours = snapshots.shape[0]
    rank = basis.shape[1]
    half = jax.ShapeDtypeStruct((hours // 2, rank), jnp.float32)
    return pl.pallas_call(
        functools.partial(project_kernel, tiles),
        out_shape=(half, half),
        in_specs=[ANYWHERE] * 2,
        out_specs=(pl.BlockSpec(memory_space=pltpu.VMEM),) * 2,
        scratch_shapes=[
            pltpu.VMEM(snapshots.shape, snapshots.dtype),
            pltpu.VMEM(basis.shape, basis.dtype),
            pltpu.VMEM((2, hours // 2, rank), jnp.float32),
            pltpu.SemaphoreType.DMA((2, tiles)),
        ],
        compiler_params=pltpu.CompilerParams(vmem_limit_bytes=53 * 2**20),
        cost_estimate=FREE,
        name="project",
    )(snapshots, basis)


def by_hours(known):
    me, core = lax.axis_index("tm"), lax.axis_index("inner")
    count = known.shape[0] // 2
    order = [
        2 * lax.rem(count + block - me, count) + lax.rem(2 + half - core, 2)
        for block in range(count)
        for half in range(2)
    ]
    return jnp.concatenate([known[at] for at in order], axis=0)


def lagged_and_scaled(every, energy):
    hour = lax.broadcasted_iota(jnp.int32, every.shape, 0)
    return jnp.where(hour == 0, 0.0, pltpu.roll(every, 1, 0)) * energy


def rebuild_kernel(tiles, energy, vectors, *refs):
    count = (len(refs) - 10) // 2
    held, coeffs, refs = refs[:count], refs[count : 2 * count], refs[2 * count :]
    operator, modes, known, turned, scale, scaled, made, square, arrived, sent = refs
    hours, cells = held[0].shape
    inputs = started(
        [
            pltpu.make_async_copy(block, known.at[pl.ds(2 * k, 2)], arrived.at[0, k])
            for k, block in enumerate(coeffs)
        ]
        + [
            pltpu.make_async_copy(energy, scale, arrived.at[1, 0]),
            pltpu.make_async_copy(vectors, turned, arrived.at[2, 0]),
        ]
    )
    waited(inputs)
    every = by_hours(known)
    scaled[...] = lagged_and_scaled(every.astype(jnp.float32), scale[...])
    me = lax.axis_index("tm")
    first = [lax.rem(me + k, count) * hours for k in range(count)]
    ordered = jnp.concatenate(
        [scaled[pl.ds(pl.multiple_of(at, hours), hours)] for at in first], axis=0
    )
    high, low = in_parts(ordered)
    weights = (product(turned[...], high, LAST) + product(turned[...], low, LAST)).astype(
        jnp.bfloat16
    )
    width = cells // tiles
    outgoing = []
    for i in range(tiles):
        for at in range(i * width, (i + 1) * width, STRIP):
            span = pl.ds(at, STRIP)
            fields = jnp.concatenate([block[:, span] for block in held], axis=0)
            made[:, span] = product(weights, fields, ROWS).astype(made.dtype)
        span = pl.ds(i * width, width)
        copy = pltpu.make_async_copy(made.at[:, span], modes.at[:, span], sent.at[i])
        outgoing += started([copy])
    high, low = in_parts(scaled[...])
    square[...] = product(every, high, FIRST) + product(every, low, FIRST)
    outgoing += started([pltpu.make_async_copy(square, operator, sent.at[tiles])])
    waited(outgoing)


def rebuild(energy, vectors, held, coeffs, tiles):
    _, half, rank = coeffs[0].shape
    hours, cells = held[0].shape
    hours, modes = len(held) * hours, vectors.shape[0]
    return pl.pallas_call(
        functools.partial(rebuild_kernel, tiles),
        out_shape=(
            jax.ShapeDtypeStruct((rank, rank), jnp.float32),
            jax.ShapeDtypeStruct((modes, cells), jnp.bfloat16),
        ),
        in_specs=[ANYWHERE] * 2 + [IN_VMEM] * len(held) + [ANYWHERE] * len(held),
        out_specs=(ANYWHERE, ANYWHERE),
        scratch_shapes=[
            pltpu.VMEM((2 * len(held), half, rank), coeffs[0].dtype),
            pltpu.VMEM(vectors.shape, vectors.dtype),
            pltpu.VMEM(energy.shape, energy.dtype),
            pltpu.VMEM((hours, rank), jnp.float32),
            pltpu.VMEM((modes, cells), jnp.bfloat16),
            pltpu.VMEM((rank, rank), jnp.float32),
            pltpu.SemaphoreType.DMA((3, len(held))),
            pltpu.SemaphoreType.DMA((tiles + 1,)),
        ],
        compiler_params=pltpu.CompilerParams(vmem_limit_bytes=40 * 2**20),
        cost_estimate=FREE,
        name="rebuild",
    )(energy, vectors, *held, *coeffs)


def swapped(value, axis, bit):
    route = [(i ^ bit, i) for i in range(lax.axis_size(axis))]
    return lax.ppermute(value, axis, route)


def moved(value, by, swap):
    size = lax.axis_size("tm")
    route = [
        (2 * ((i + by) % size) + (core ^ swap), 2 * i + core)
        for i in range(size)
        for core in range(2)
    ]
    return lax.ppermute(value, ("tm", "inner"), route)


def per_device(eof_basis, snapshots, inverse_energy, eigen_vectors):
    tm, outer = lax.axis_size("tm"), lax.axis_size("outer")
    me = lax.axis_index("tm")
    fields = snapshots.T

    held = [fields] + [moved(fields, k, 0) for k in range(1, tm)]

    kept, given = project(fields, eof_basis, 8)
    mine = kept + swapped(given, "inner", 1)
    bit = 1
    while bit < outer:
        near = swapped(mine, "outer", bit)
        if 2 * bit < outer:
            far, both = (swapped(mine, "outer", b) for b in (2 * bit, 3 * bit))
            mine = (mine + near) + (far + both)
        else:
            mine = mine + near
        bit *= 4
    mine = mine.astype(jnp.bfloat16)
    both = jnp.stack([mine, moved(mine, 0, 1)])
    coeffs = [both] + [moved(both, k, 0) for k in range(1, tm)]

    rows = eigen_vectors.shape[1] // tm
    vectors = lax.dynamic_slice_in_dim(eigen_vectors, me * rows, rows, 1)
    return rebuild(inverse_energy[None, :], vectors.T, held, coeffs, 4)


def solution(mesh):
    tm, space = mesh.shape["tm"], mesh.shape["space"]
    split = Mesh(mesh.devices.reshape(tm, space // 2, 2), ("tm", "outer", "inner"))
    cells = ("outer", "inner")
    in_specs = (P(cells, None), P(cells, "tm"), P(), P())
    out_specs = (P(), P("tm", cells))
    return jax.shard_map(
        per_device, mesh=split, in_specs=in_specs, out_specs=out_specs, check_vma=False
    )
```

```python
import functools

import jax
import jax.numpy as jnp
from jax import lax
from jax.experimental import pallas as pl
from jax.experimental.pallas import tpu as pltpu
from jax.sharding import Mesh, PartitionSpec as P

ROWS = (((1,), (0,)), ((), ()))
FIRST = (((0,), (0,)), ((), ()))
LAST = (((1,), (1,)), ((), ()))
STRIP = 256
FREE = pl.CostEstimate(flops=0, bytes_accessed=0, transcendentals=0)
ANYWHERE = pl.BlockSpec(memory_space=pl.ANY)
IN_VMEM = pl.BlockSpec(memory_space=pltpu.VMEM)


def started(copies):
    for copy in copies:
        copy.start()
    return copies


def waited(copies):
    for copy in copies:
        copy.wait()


def in_parts(value):
    high = value.astype(jnp.bfloat16)
    return high, (value - high.astype(jnp.float32)).astype(jnp.bfloat16)


def product(left, right, dims):
    return lax.dot_general(left, right, dims, preferred_element_type=jnp.float32)


def project_kernel(tiles, snapshots, basis, kept, given, fields, patterns, halves, arrived):
    cells = snapshots.shape[1]
    tile = cells // tiles
    copies = []
    for i in range(tiles):
        span = pl.ds(i * tile, tile)
        copies.append(
            (
                pltpu.make_async_copy(snapshots.at[:, span], fields.at[:, span], arrived.at[0, i]),
                pltpu.make_async_copy(basis.at[span], patterns.at[span], arrived.at[1, i]),
            )
        )
    for pair in copies:
        for copy in pair:
            copy.start()
    total = jnp.zeros((fields.shape[0], patterns.shape[1]), jnp.float32)
    for i, pair in enumerate(copies):
        for copy in pair:
            copy.wait()
        span = pl.ds(i * tile, tile)
        total += product(fields[:, span], patterns[span], ROWS)
    half = kept.shape[0]
    core = lax.axis_index("inner")
    halves[0] = total[:half]
    halves[1] = total[half:]
    kept[...] = halves[core]
    given[...] = halves[1 - core]


def project(snapshots, basis, tiles):
    hours = snapshots.shape[0]
    rank = basis.shape[1]
    half = jax.ShapeDtypeStruct((hours // 2, rank), jnp.float32)
    return pl.pallas_call(
        functools.partial(project_kernel, tiles),
        out_shape=(half, half),
        in_specs=[ANYWHERE] * 2,
        out_specs=(pl.BlockSpec(memory_space=pltpu.VMEM),) * 2,
        scratch_shapes=[
            pltpu.VMEM(snapshots.shape, snapshots.dtype),
            pltpu.VMEM(basis.shape, basis.dtype),
            pltpu.VMEM((2, hours // 2, rank), jnp.float32),
            pltpu.SemaphoreType.DMA((2, tiles)),
        ],
        compiler_params=pltpu.CompilerParams(vmem_limit_bytes=53 * 2**20),
        cost_estimate=FREE,
        name="project",
    )(snapshots, basis)


def lagged_and_scaled(every, energy):
    hour = lax.broadcasted_iota(jnp.int32, every.shape, 0)
    return jnp.where(hour == 0, 0.0, pltpu.roll(every, 1, 0)) * energy


def rebuild_kernel(tiles, energy, vectors, *refs):
    count = (len(refs) - 7) // 2
    held, coeffs, refs = refs[:count], refs[count : 2 * count], refs[2 * count :]
    operator, modes, known, scaled, made, square, sent = refs
    hours, cells = held[0].shape
    half = hours // 2
    me, core = lax.axis_index("tm"), lax.axis_index("inner")
    first = [lax.rem(me + k, count) * hours for k in range(count)]
    for k, block in enumerate(coeffs):
        for n in range(2):
            at = pl.multiple_of(first[k] + lax.rem(core + n, 2) * half, half)
            known[pl.ds(at, half)] = block[n].astype(jnp.float32)
    every = known[...].astype(jnp.bfloat16)
    scaled[...] = lagged_and_scaled(known[...], energy[...])
    ordered = jnp.concatenate(
        [scaled[pl.ds(pl.multiple_of(at, hours), hours)] for at in first], axis=0
    )
    high, low = in_parts(ordered)
    weights = (product(vectors[...], high, LAST) + product(vectors[...], low, LAST)).astype(
        jnp.bfloat16
    )
    width = cells // tiles
    outgoing = []
    for i in range(tiles):
        for at in range(i * width, (i + 1) * width, STRIP):
            span = pl.ds(at, STRIP)
            fields = jnp.concatenate([block[:, span] for block in held], axis=0)
            made[:, span] = product(weights, fields, ROWS).astype(made.dtype)
        span = pl.ds(i * width, width)
        copy = pltpu.make_async_copy(made.at[:, span], modes.at[:, span], sent.at[i])
        outgoing += started([copy])
    high, low = in_parts(scaled[...])
    square[...] = product(every, high, FIRST) + product(every, low, FIRST)
    outgoing += started([pltpu.make_async_copy(square, operator, sent.at[tiles])])
    waited(outgoing)


def rebuild(energy, vectors, held, coeffs, tiles):
    rank = coeffs[0].shape[2]
    hours, cells = held[0].shape
    hours, modes = len(held) * hours, vectors.shape[0]
    return pl.pallas_call(
        functools.partial(rebuild_kernel, tiles),
        out_shape=(
            jax.ShapeDtypeStruct((rank, rank), jnp.float32),
            jax.ShapeDtypeStruct((modes, cells), jnp.bfloat16),
        ),
        in_specs=[IN_VMEM] * (2 + 2 * len(held)),
        out_specs=(ANYWHERE, ANYWHERE),
        scratch_shapes=[
            pltpu.VMEM((hours, rank), jnp.float32),
            pltpu.VMEM((hours, rank), jnp.float32),
            pltpu.VMEM((modes, cells), jnp.bfloat16),
            pltpu.VMEM((rank, rank), jnp.float32),
            pltpu.SemaphoreType.DMA((tiles + 1,)),
        ],
        compiler_params=pltpu.CompilerParams(vmem_limit_bytes=40 * 2**20),
        cost_estimate=FREE,
        name="rebuild",
    )(energy, vectors, *held, *coeffs)


def swapped(value, axis, bit):
    route = [(i ^ bit, i) for i in range(lax.axis_size(axis))]
    return lax.ppermute(value, axis, route)


def moved(value, by, swap):
    size = lax.axis_size("tm")
    route = [
        (2 * ((i + by) % size) + (core ^ swap), 2 * i + core)
        for i in range(size)
        for core in range(2)
    ]
    return lax.ppermute(value, ("tm", "inner"), route)


def per_device(eof_basis, snapshots, inverse_energy, eigen_vectors):
    tm, outer = lax.axis_size("tm"), lax.axis_size("outer")
    me = lax.axis_index("tm")
    fields = snapshots.T

    held = [fields] + [moved(fields, k, 0) for k in range(1, tm)]

    kept, given = project(fields, eof_basis, 8)
    mine = kept + swapped(given, "inner", 1)
    bit = 1
    while bit < outer:
        near = swapped(mine, "outer", bit)
        if 2 * bit < outer:
            far, both = (swapped(mine, "outer", b) for b in (2 * bit, 3 * bit))
            mine = (mine + near) + (far + both)
        else:
            mine = mine + near
        bit *= 4
    mine = mine.astype(jnp.bfloat16)
    both = jnp.stack([mine, moved(mine, 0, 1)])
    coeffs = [both] + [moved(both, k, 0) for k in range(1, tm)]

    rows = eigen_vectors.shape[1] // tm
    vectors = lax.dynamic_slice_in_dim(eigen_vectors, me * rows, rows, 1)
    return rebuild(inverse_energy[None, :], vectors.T, held, coeffs, 4)


def solution(mesh):
    tm, space = mesh.shape["tm"], mesh.shape["space"]
    split = Mesh(mesh.devices.reshape(tm, space // 2, 2), ("tm", "outer", "inner"))
    cells = ("outer", "inner")
    in_specs = (P(cells, None), P(cells, "tm"), P(), P())
    out_specs = (P(), P("tm", cells))
    return jax.shard_map(
        per_device, mesh=split, in_specs=in_specs, out_specs=out_specs, check_vma=False
    )
```

```python
import functools

import jax
import jax.numpy as jnp
from jax import lax
from jax.experimental import pallas as pl
from jax.experimental.pallas import tpu as pltpu
from jax.sharding import Mesh, PartitionSpec as P

ROWS = (((1,), (0,)), ((), ()))
FIRST = (((0,), (0,)), ((), ()))
LAST = (((1,), (1,)), ((), ()))
STRIP = 256
FREE = pl.CostEstimate(flops=0, bytes_accessed=0, transcendentals=0)
LONG = pl.CostEstimate(flops=3 * 10**9, bytes_accessed=0, transcendentals=0)
ANYWHERE = pl.BlockSpec(memory_space=pl.ANY)
IN_VMEM = pl.BlockSpec(memory_space=pltpu.VMEM)


def started(copies):
    for copy in copies:
        copy.start()
    return copies


def waited(copies):
    for copy in copies:
        copy.wait()


def in_parts(value):
    high = value.astype(jnp.bfloat16)
    return high, (value - high.astype(jnp.float32)).astype(jnp.bfloat16)


def product(left, right, dims):
    return lax.dot_general(left, right, dims, preferred_element_type=jnp.float32)


def cut_kernel(rows, parts, fields, early, sent):
    width = early.shape[1] // parts
    waited(
        started(
            [
                pltpu.make_async_copy(
                    fields.at[pl.ds(at, rows), pl.ds(i * width, width)],
                    early.at[pl.ds(at, rows), pl.ds(i * width, width)],
                    sent.at[at // rows, i],
                )
                for at in range(0, fields.shape[0], rows)
                for i in range(parts)
            ]
        )
    )


def cut(fields, width, rows, parts):
    hours = fields.shape[0]
    return pl.pallas_call(
        functools.partial(cut_kernel, rows, parts),
        out_shape=jax.ShapeDtypeStruct((hours, width), fields.dtype),
        in_specs=[ANYWHERE],
        out_specs=ANYWHERE,
        scratch_shapes=[pltpu.SemaphoreType.DMA((hours // rows, parts))],
        compiler_params=pltpu.CompilerParams(vmem_limit_bytes=52 * 2**20),
        cost_estimate=FREE,
        name="cut",
    )(fields)


def project_kernel(tiles, snapshots, basis, kept, given, fields, patterns, halves, arrived):
    cells = snapshots.shape[1]
    tile = cells // tiles
    copies = []
    for i in range(tiles):
        span = pl.ds(i * tile, tile)
        copies.append(
            (
                pltpu.make_async_copy(snapshots.at[:, span], fields.at[:, span], arrived.at[0, i]),
                pltpu.make_async_copy(basis.at[span], patterns.at[span], arrived.at[1, i]),
            )
        )
    for pair in copies:
        for copy in pair:
            copy.start()
    total = jnp.zeros((fields.shape[0], patterns.shape[1]), jnp.float32)
    for i, pair in enumerate(copies):
        for copy in pair:
            copy.wait()
        span = pl.ds(i * tile, tile)
        total += product(fields[:, span], patterns[span], ROWS)
    half = kept.shape[0]
    core = lax.axis_index("inner")
    halves[0] = total[:half]
    halves[1] = total[half:]
    kept[...] = halves[core]
    given[...] = halves[1 - core]


def project(snapshots, basis, tiles):
    hours = snapshots.shape[0]
    rank = basis.shape[1]
    half = jax.ShapeDtypeStruct((hours // 2, rank), jnp.float32)
    return pl.pallas_call(
        functools.partial(project_kernel, tiles),
        out_shape=(half, half),
        in_specs=[ANYWHERE] * 2,
        out_specs=(pl.BlockSpec(memory_space=pltpu.VMEM),) * 2,
        scratch_shapes=[
            pltpu.VMEM(snapshots.shape, snapshots.dtype),
            pltpu.VMEM(basis.shape, basis.dtype),
            pltpu.VMEM((2, hours // 2, rank), jnp.float32),
            pltpu.SemaphoreType.DMA((2, tiles)),
        ],
        compiler_params=pltpu.CompilerParams(vmem_limit_bytes=53 * 2**20),
        cost_estimate=FREE,
        name="project",
    )(snapshots, basis)


def lagged_and_scaled(every, energy):
    hour = lax.broadcasted_iota(jnp.int32, every.shape, 0)
    return jnp.where(hour == 0, 0.0, pltpu.roll(every, 1, 0)) * energy


def columns(held, begin, width):
    return jnp.concatenate([b[:, pl.ds(begin - at, width)] for b, at in held], axis=0)


def rebuilt(weights, held, made, modes, begin, tiles, sent):
    width = made.shape[1] // tiles
    outgoing = []
    for i in range(tiles):
        for at in range(i * width, (i + 1) * width, STRIP):
            fields = columns(held, begin + at, STRIP)
            made[:, pl.ds(at, STRIP)] = product(weights, fields, ROWS).astype(made.dtype)
        target = modes.at[:, pl.ds(begin + i * width, width)]
        copy = pltpu.make_async_copy(made.at[:, pl.ds(i * width, width)], target, sent.at[i])
        outgoing += started([copy])
    return outgoing


def first_kernel(tiles, energy, vectors, *refs):
    count = (len(refs) - 8) // 2
    held, coeffs, refs = refs[:count], refs[count : 2 * count], refs[2 * count :]
    operator, modes, weights, known, scaled, made, square, sent = refs
    hours = held[0].shape[0]
    half = hours // 2
    me, core = lax.axis_index("tm"), lax.axis_index("inner")
    first = [lax.rem(me + k, count) * hours for k in range(count)]
    for k, block in enumerate(coeffs):
        for n in range(2):
            at = pl.multiple_of(first[k] + lax.rem(core + n, 2) * half, half)
            known[pl.ds(at, half)] = block[n].astype(jnp.float32)
    every = known[...].astype(jnp.bfloat16)
    scaled[...] = lagged_and_scaled(known[...], energy[...])
    ordered = jnp.concatenate(
        [scaled[pl.ds(pl.multiple_of(at, hours), hours)] for at in first], axis=0
    )
    high, low = in_parts(ordered)
    value = (product(vectors[...], high, LAST) + product(vectors[...], low, LAST)).astype(
        jnp.bfloat16
    )
    weights[...] = value
    outgoing = rebuilt(value, [(b, 0) for b in held], made, modes, 0, tiles, sent)
    high, low = in_parts(scaled[...])
    square[...] = product(every, high, FIRST) + product(every, low, FIRST)
    outgoing += started([pltpu.make_async_copy(square, operator, sent.at[tiles])])
    waited(outgoing)


def last_kernel(begin, tiles, weights, *refs):
    held, (_, modes, made, sent) = refs[:-4], refs[-4:]
    blocks = [(held[0], 0)] + [(b, begin) for b in held[1:]]
    waited(rebuilt(weights[...], blocks, made, modes, begin, tiles, sent))


def rebuild_first(energy, vectors, held, coeffs, width, tiles):
    rank = coeffs[0].shape[2]
    hours, cells = held[0].shape
    hours, modes = len(held) * hours, vectors.shape[0]
    return pl.pallas_call(
        functools.partial(first_kernel, tiles),
        out_shape=(
            jax.ShapeDtypeStruct((rank, rank), jnp.float32),
            jax.ShapeDtypeStruct((modes, cells), jnp.bfloat16),
            jax.ShapeDtypeStruct((modes, hours), jnp.bfloat16),
        ),
        in_specs=[IN_VMEM] * (2 + 2 * len(held)),
        out_specs=(ANYWHERE, ANYWHERE, IN_VMEM),
        scratch_shapes=[
            pltpu.VMEM((hours, rank), jnp.float32),
            pltpu.VMEM((hours, rank), jnp.float32),
            pltpu.VMEM((modes, width), jnp.bfloat16),
            pltpu.VMEM((rank, rank), jnp.float32),
            pltpu.SemaphoreType.DMA((tiles + 1,)),
        ],
        compiler_params=pltpu.CompilerParams(vmem_limit_bytes=40 * 2**20),
        cost_estimate=LONG,
        name="rebuild_first",
    )(energy, vectors, *held, *coeffs)


def rebuild_last(weights, held, modes, begin, tiles):
    return pl.pallas_call(
        functools.partial(last_kernel, begin, tiles),
        out_shape=jax.ShapeDtypeStruct(modes.shape, modes.dtype),
        in_specs=[IN_VMEM] * (1 + len(held)) + [ANYWHERE],
        out_specs=ANYWHERE,
        scratch_shapes=[
            pltpu.VMEM((modes.shape[0], modes.shape[1] - begin), modes.dtype),
            pltpu.SemaphoreType.DMA((tiles,)),
        ],
        input_output_aliases={1 + len(held): 0},
        compiler_params=pltpu.CompilerParams(vmem_limit_bytes=40 * 2**20),
        cost_estimate=FREE,
        name="rebuild_last",
    )(weights, *held, modes)


def swapped(value, axis, bit):
    route = [(i ^ bit, i) for i in range(lax.axis_size(axis))]
    return lax.ppermute(value, axis, route)


def moved(value, by, swap):
    size = lax.axis_size("tm")
    route = [
        (2 * ((i + by) % size) + (core ^ swap), 2 * i + core)
        for i in range(size)
        for core in range(2)
    ]
    return lax.ppermute(value, ("tm", "inner"), route)


def per_device(eof_basis, snapshots, inverse_energy, eigen_vectors):
    tm, outer = lax.axis_size("tm"), lax.axis_size("outer")
    me = lax.axis_index("tm")
    fields = snapshots.T

    begin = fields.shape[1] // 8 * 7

    early, late = cut(fields, begin, 16, 2), fields[:, begin:]
    first = [fields] + [moved(early, k, 0) for k in range(1, tm)]

    kept, given = project(fields, eof_basis, 8)
    mine = kept + swapped(given, "inner", 1)
    bit = 1
    while bit < outer:
        near = swapped(mine, "outer", bit)
        if 2 * bit < outer:
            far, both = (swapped(mine, "outer", b) for b in (2 * bit, 3 * bit))
            mine = (mine + near) + (far + both)
        else:
            mine = mine + near
        bit *= 4
    mine = mine.astype(jnp.bfloat16)
    both = jnp.stack([mine, moved(mine, 0, 1)])
    both, late = lax.optimization_barrier((both, late))
    last = [fields] + [moved(late, k, 0) for k in range(1, tm)]
    coeffs = [both] + [moved(both, k, 0) for k in range(1, tm)]

    rows = eigen_vectors.shape[1] // tm
    vectors = lax.dynamic_slice_in_dim(eigen_vectors, me * rows, rows, 1)
    operator, modes, weights = rebuild_first(
        inverse_energy[None, :], vectors.T, first, coeffs, begin, 4
    )
    return operator, rebuild_last(weights, last, modes, begin, 2)


def solution(mesh):
    tm, space = mesh.shape["tm"], mesh.shape["space"]
    split = Mesh(mesh.devices.reshape(tm, space // 2, 2), ("tm", "outer", "inner"))
    cells = ("outer", "inner")
    in_specs = (P(cells, None), P(cells, "tm"), P(), P())
    out_specs = (P(), P("tm", cells))
    return jax.shard_map(
        per_device, mesh=split, in_specs=in_specs, out_specs=out_specs, check_vma=False
    )
```

```python
import functools

import jax
import jax.numpy as jnp
from jax import lax
from jax.experimental import pallas as pl
from jax.experimental.pallas import tpu as pltpu
from jax.sharding import Mesh, PartitionSpec as P

ROWS = (((1,), (0,)), ((), ()))
FIRST = (((0,), (0,)), ((), ()))
LAST = (((1,), (1,)), ((), ()))
STRIP = 256
FREE = pl.CostEstimate(flops=0, bytes_accessed=0, transcendentals=0)
LONG = pl.CostEstimate(flops=3 * 10**9, bytes_accessed=0, transcendentals=0)
ANYWHERE = pl.BlockSpec(memory_space=pl.ANY)
IN_VMEM = pl.BlockSpec(memory_space=pltpu.VMEM)


def started(copies):
    for copy in copies:
        copy.start()
    return copies


def waited(copies):
    for copy in copies:
        copy.wait()


def in_parts(value):
    high = value.astype(jnp.bfloat16)
    return high, (value - high.astype(jnp.float32)).astype(jnp.bfloat16)


def product(left, right, dims):
    return lax.dot_general(left, right, dims, preferred_element_type=jnp.float32)


def cut_kernel(rows, begin, fields, early, late, sent):
    half = begin // 2
    copies = []
    for n, at in enumerate(range(0, fields.shape[0], rows)):
        here = pl.ds(at, rows)
        for i in range(2):
            span = pl.ds(i * half, half)
            copies.append(
                pltpu.make_async_copy(fields.at[here, span], early.at[here, span], sent.at[n, i])
            )
    span = pl.ds(begin, late.shape[1])
    copies.append(pltpu.make_async_copy(fields.at[:, span], late, sent.at[0, 2]))
    waited(started(copies))


def cut(fields, begin, rows):
    hours, cells = fields.shape
    return pl.pallas_call(
        functools.partial(cut_kernel, rows, begin),
        out_shape=(
            jax.ShapeDtypeStruct((hours, begin), fields.dtype),
            jax.ShapeDtypeStruct((hours, cells - begin), fields.dtype),
        ),
        in_specs=[ANYWHERE],
        out_specs=(ANYWHERE, ANYWHERE),
        scratch_shapes=[pltpu.SemaphoreType.DMA((hours // rows, 3))],
        compiler_params=pltpu.CompilerParams(vmem_limit_bytes=52 * 2**20),
        cost_estimate=FREE,
        name="cut",
    )(fields)


def project_kernel(tiles, early, late, basis, kept, given, patterns, halves, arrived):
    cells = basis.shape[0]
    tile, begin = cells // tiles, early.shape[1]
    spans = [pl.ds(i * tile, tile) for i in range(tiles)]
    copies = started(
        [
            pltpu.make_async_copy(basis.at[span], patterns.at[span], arrived.at[i])
            for i, span in enumerate(spans)
        ]
    )
    total = jnp.zeros((early.shape[0], patterns.shape[1]), jnp.float32)
    for i, span in enumerate(spans):
        copies[i].wait()
        at = i * tile
        fields = early[:, span] if at < begin else late[:, pl.ds(at - begin, tile)]
        total += product(fields, patterns[span], ROWS)
    half = kept.shape[0]
    core = lax.axis_index("inner")
    halves[0] = total[:half]
    halves[1] = total[half:]
    kept[...] = halves[core]
    given[...] = halves[1 - core]


def project(early, late, basis, tiles):
    hours, rank = early.shape[0], basis.shape[1]
    half = jax.ShapeDtypeStruct((hours // 2, rank), jnp.float32)
    return pl.pallas_call(
        functools.partial(project_kernel, tiles),
        out_shape=(half, half),
        in_specs=[IN_VMEM, IN_VMEM, ANYWHERE],
        out_specs=(IN_VMEM, IN_VMEM),
        scratch_shapes=[
            pltpu.VMEM(basis.shape, basis.dtype),
            pltpu.VMEM((2, hours // 2, rank), jnp.float32),
            pltpu.SemaphoreType.DMA((tiles,)),
        ],
        compiler_params=pltpu.CompilerParams(vmem_limit_bytes=52 * 2**20),
        cost_estimate=FREE,
        name="project",
    )(early, late, basis)


def lagged_and_scaled(every, energy):
    hour = lax.broadcasted_iota(jnp.int32, every.shape, 0)
    return jnp.where(hour == 0, 0.0, pltpu.roll(every, 1, 0)) * energy


def columns(held, begin, width):
    return jnp.concatenate([b[:, pl.ds(begin - at, width)] for b, at in held], axis=0)


def rebuilt(weights, held, made, modes, begin, tiles, sent):
    width = made.shape[1] // tiles
    outgoing = []
    for i in range(tiles):
        for at in range(i * width, (i + 1) * width, STRIP):
            fields = columns(held, begin + at, STRIP)
            made[:, pl.ds(at, STRIP)] = product(weights, fields, ROWS).astype(made.dtype)
        target = modes.at[:, pl.ds(begin + i * width, width)]
        copy = pltpu.make_async_copy(made.at[:, pl.ds(i * width, width)], target, sent.at[i])
        outgoing += started([copy])
    return outgoing


def first_kernel(tiles, energy, vectors, *refs):
    count = (len(refs) - 8) // 2
    held, coeffs, refs = refs[:count], refs[count : 2 * count], refs[2 * count :]
    operator, modes, weights, known, scaled, made, square, sent = refs
    hours = held[0].shape[0]
    half = hours // 2
    me, core = lax.axis_index("tm"), lax.axis_index("inner")
    first = [lax.rem(me + k, count) * hours for k in range(count)]
    for k, block in enumerate(coeffs):
        for n in range(2):
            at = pl.multiple_of(first[k] + lax.rem(core + n, 2) * half, half)
            known[pl.ds(at, half)] = block[n].astype(jnp.float32)
    every = known[...].astype(jnp.bfloat16)
    scaled[...] = lagged_and_scaled(known[...], energy[...])
    ordered = jnp.concatenate(
        [scaled[pl.ds(pl.multiple_of(at, hours), hours)] for at in first], axis=0
    )
    high, low = in_parts(ordered)
    value = (product(vectors[...], high, LAST) + product(vectors[...], low, LAST)).astype(
        jnp.bfloat16
    )
    weights[...] = value
    outgoing = rebuilt(value, [(b, 0) for b in held], made, modes, 0, tiles, sent)
    high, low = in_parts(scaled[...])
    square[...] = product(every, high, FIRST) + product(every, low, FIRST)
    outgoing += started([pltpu.make_async_copy(square, operator, sent.at[tiles])])
    waited(outgoing)


def last_kernel(begin, tiles, weights, *refs):
    held, (_, modes, made, sent) = refs[:-4], refs[-4:]
    blocks = [(b, begin) for b in held]
    waited(rebuilt(weights[...], blocks, made, modes, begin, tiles, sent))


def rebuild_first(energy, vectors, held, coeffs, cells, tiles):
    rank = coeffs[0].shape[2]
    hours, modes = len(held) * held[0].shape[0], vectors.shape[0]
    return pl.pallas_call(
        functools.partial(first_kernel, tiles),
        out_shape=(
            jax.ShapeDtypeStruct((rank, rank), jnp.float32),
            jax.ShapeDtypeStruct((modes, cells), jnp.bfloat16),
            jax.ShapeDtypeStruct((modes, hours), jnp.bfloat16),
        ),
        in_specs=[IN_VMEM] * (2 + 2 * len(held)),
        out_specs=(ANYWHERE, ANYWHERE, IN_VMEM),
        scratch_shapes=[
            pltpu.VMEM((hours, rank), jnp.float32),
            pltpu.VMEM((hours, rank), jnp.float32),
            pltpu.VMEM((modes, held[0].shape[1]), jnp.bfloat16),
            pltpu.VMEM((rank, rank), jnp.float32),
            pltpu.SemaphoreType.DMA((tiles + 1,)),
        ],
        compiler_params=pltpu.CompilerParams(vmem_limit_bytes=40 * 2**20),
        cost_estimate=LONG,
        name="rebuild_first",
    )(energy, vectors, *held, *coeffs)


def rebuild_last(weights, held, modes, begin, tiles):
    return pl.pallas_call(
        functools.partial(last_kernel, begin, tiles),
        out_shape=jax.ShapeDtypeStruct(modes.shape, modes.dtype),
        in_specs=[IN_VMEM] * (1 + len(held)) + [ANYWHERE],
        out_specs=ANYWHERE,
        scratch_shapes=[
            pltpu.VMEM((modes.shape[0], modes.shape[1] - begin), modes.dtype),
            pltpu.SemaphoreType.DMA((tiles,)),
        ],
        input_output_aliases={1 + len(held): 0},
        compiler_params=pltpu.CompilerParams(vmem_limit_bytes=40 * 2**20),
        cost_estimate=FREE,
        name="rebuild_last",
    )(weights, *held, modes)


def swapped(value, axis, bit):
    route = [(i ^ bit, i) for i in range(lax.axis_size(axis))]
    return lax.ppermute(value, axis, route)


def moved(value, by, swap):
    size = lax.axis_size("tm")
    route = [
        (2 * ((i + by) % size) + (core ^ swap), 2 * i + core)
        for i in range(size)
        for core in range(2)
    ]
    return lax.ppermute(value, ("tm", "inner"), route)


def per_device(eof_basis, snapshots, inverse_energy, eigen_vectors):
    tm, outer = lax.axis_size("tm"), lax.axis_size("outer")
    me = lax.axis_index("tm")
    fields = snapshots.T

    cells = fields.shape[1]
    begin = cells // 8 * 7

    early, late = cut(fields, begin, 16)
    first = [early] + [moved(early, k, 0) for k in range(1, tm)]

    kept, given = project(early, late, eof_basis, 8)
    mine = kept + swapped(given, "inner", 1)
    bit = 1
    while bit < outer:
        near = swapped(mine, "outer", bit)
        if 2 * bit < outer:
            far, both = (swapped(mine, "outer", b) for b in (2 * bit, 3 * bit))
            mine = (mine + near) + (far + both)
        else:
            mine = mine + near
        bit *= 4
    mine = mine.astype(jnp.bfloat16)
    both = jnp.stack([mine, moved(mine, 0, 1)])
    both, behind = lax.optimization_barrier((both, late))
    last = [late] + [moved(behind, k, 0) for k in range(1, tm)]
    coeffs = [both] + [moved(both, k, 0) for k in range(1, tm)]

    rows = eigen_vectors.shape[1] // tm
    vectors = lax.dynamic_slice_in_dim(eigen_vectors, me * rows, rows, 1)
    operator, modes, weights = rebuild_first(
        inverse_energy[None, :], vectors.T, first, coeffs, cells, 4
    )
    return operator, rebuild_last(weights, last, modes, begin, 2)


def solution(mesh):
    tm, space = mesh.shape["tm"], mesh.shape["space"]
    split = Mesh(mesh.devices.reshape(tm, space // 2, 2), ("tm", "outer", "inner"))
    cells = ("outer", "inner")
    in_specs = (P(cells, None), P(cells, "tm"), P(), P())
    out_specs = (P(), P("tm", cells))
    return jax.shard_map(
        per_device, mesh=split, in_specs=in_specs, out_specs=out_specs, check_vma=False
    )
```

```python
import functools

import jax
import jax.numpy as jnp
from jax import lax
from jax.experimental import pallas as pl
from jax.experimental.pallas import tpu as pltpu
from jax.sharding import Mesh, PartitionSpec as P

ROWS = (((1,), (0,)), ((), ()))
FIRST = (((0,), (0,)), ((), ()))
LAST = (((1,), (1,)), ((), ()))
STRIP = 256
FREE = pl.CostEstimate(flops=0, bytes_accessed=0, transcendentals=0)
LONG = pl.CostEstimate(flops=3 * 10**9, bytes_accessed=0, transcendentals=0)
ANYWHERE = pl.BlockSpec(memory_space=pl.ANY)
IN_VMEM = pl.BlockSpec(memory_space=pltpu.VMEM)


def started(copies):
    for copy in copies:
        copy.start()
    return copies


def waited(copies):
    for copy in copies:
        copy.wait()


def in_parts(value):
    high = value.astype(jnp.bfloat16)
    return high, (value - high.astype(jnp.float32)).astype(jnp.bfloat16)


def product(left, right, dims):
    return lax.dot_general(left, right, dims, preferred_element_type=jnp.float32)


def cut_kernel(begin, fields, early, late, sent):
    spans = pl.ds(0, begin), pl.ds(begin, late.shape[1])
    waited(
        started(
            [
                pltpu.make_async_copy(fields.at[:, span], piece, sent.at[i])
                for i, (span, piece) in enumerate(zip(spans, (early, late)))
            ]
        )
    )


def cut(fields, begin):
    hours, cells = fields.shape
    return pl.pallas_call(
        functools.partial(cut_kernel, begin),
        out_shape=(
            jax.ShapeDtypeStruct((hours, begin), fields.dtype),
            jax.ShapeDtypeStruct((hours, cells - begin), fields.dtype),
        ),
        in_specs=[ANYWHERE],
        out_specs=(ANYWHERE, ANYWHERE),
        scratch_shapes=[pltpu.SemaphoreType.DMA((2,))],
        compiler_params=pltpu.CompilerParams(vmem_limit_bytes=52 * 2**20),
        cost_estimate=FREE,
        name="cut",
    )(fields)


def project_kernel(tiles, early, late, basis, kept, given, patterns, halves, arrived):
    cells = basis.shape[0]
    tile, begin = cells // tiles, early.shape[1]
    spans = [pl.ds(i * tile, tile) for i in range(tiles)]
    copies = started(
        [
            pltpu.make_async_copy(basis.at[span], patterns.at[span], arrived.at[i])
            for i, span in enumerate(spans)
        ]
    )
    total = jnp.zeros((early.shape[0], patterns.shape[1]), jnp.float32)
    for i, span in enumerate(spans):
        copies[i].wait()
        at = i * tile
        fields = early[:, span] if at < begin else late[:, pl.ds(at - begin, tile)]
        total += product(fields, patterns[span], ROWS)
    half = kept.shape[0]
    core = lax.axis_index("inner")
    halves[0] = total[:half]
    halves[1] = total[half:]
    kept[...] = halves[core]
    given[...] = halves[1 - core]


def project(early, late, basis, tiles):
    hours, rank = early.shape[0], basis.shape[1]
    half = jax.ShapeDtypeStruct((hours // 2, rank), jnp.float32)
    return pl.pallas_call(
        functools.partial(project_kernel, tiles),
        out_shape=(half, half),
        in_specs=[IN_VMEM, IN_VMEM, ANYWHERE],
        out_specs=(IN_VMEM, IN_VMEM),
        scratch_shapes=[
            pltpu.VMEM(basis.shape, basis.dtype),
            pltpu.VMEM((2, hours // 2, rank), jnp.float32),
            pltpu.SemaphoreType.DMA((tiles,)),
        ],
        compiler_params=pltpu.CompilerParams(vmem_limit_bytes=52 * 2**20),
        cost_estimate=FREE,
        name="project",
    )(early, late, basis)


def lagged_and_scaled(every, energy):
    hour = lax.broadcasted_iota(jnp.int32, every.shape, 0)
    return jnp.where(hour == 0, 0.0, pltpu.roll(every, 1, 0)) * energy


def columns(held, begin, width):
    return jnp.concatenate([b[:, pl.ds(begin - at, width)] for b, at in held], axis=0)


def rebuilt(weights, held, made, modes, begin, tiles, sent, between=list):
    width = made.shape[1] // tiles
    outgoing = []
    for i in range(tiles):
        if i == tiles - 1:
            outgoing += between()
        for at in range(i * width, (i + 1) * width, STRIP):
            fields = columns(held, begin + at, STRIP)
            made[:, pl.ds(at, STRIP)] = product(weights, fields, ROWS).astype(made.dtype)
        target = modes.at[:, pl.ds(begin + i * width, width)]
        copy = pltpu.make_async_copy(made.at[:, pl.ds(i * width, width)], target, sent.at[i])
        outgoing += started([copy])
    return outgoing


def first_kernel(tiles, energy, vectors, *refs):
    count = (len(refs) - 8) // 2
    held, coeffs, refs = refs[:count], refs[count : 2 * count], refs[2 * count :]
    operator, modes, weights, known, scaled, made, square, sent = refs
    hours = held[0].shape[0]
    half = hours // 2
    me, core = lax.axis_index("tm"), lax.axis_index("inner")
    first = [lax.rem(me + k, count) * hours for k in range(count)]
    for k, block in enumerate(coeffs):
        for n in range(2):
            at = pl.multiple_of(first[k] + lax.rem(core + n, 2) * half, half)
            known[pl.ds(at, half)] = block[n].astype(jnp.float32)
    every = known[...].astype(jnp.bfloat16)
    scaled[...] = lagged_and_scaled(known[...], energy[...])
    ordered = jnp.concatenate(
        [scaled[pl.ds(pl.multiple_of(at, hours), hours)] for at in first], axis=0
    )
    high, low = in_parts(ordered)
    value = (product(vectors[...], high, LAST) + product(vectors[...], low, LAST)).astype(
        jnp.bfloat16
    )
    weights[...] = value

    def operate():
        high, low = in_parts(scaled[...])
        square[...] = product(every, high, FIRST) + product(every, low, FIRST)
        return started([pltpu.make_async_copy(square, operator, sent.at[tiles])])

    waited(rebuilt(value, [(b, 0) for b in held], made, modes, 0, tiles, sent, operate))


def last_kernel(begin, tiles, weights, *refs):
    held, (_, modes, made, sent) = refs[:-4], refs[-4:]
    blocks = [(b, begin) for b in held]
    waited(rebuilt(weights[...], blocks, made, modes, begin, tiles, sent))


def rebuild_first(energy, vectors, held, coeffs, cells, tiles):
    rank = coeffs[0].shape[2]
    hours, modes = len(held) * held[0].shape[0], vectors.shape[0]
    return pl.pallas_call(
        functools.partial(first_kernel, tiles),
        out_shape=(
            jax.ShapeDtypeStruct((rank, rank), jnp.float32),
            jax.ShapeDtypeStruct((modes, cells), jnp.bfloat16),
            jax.ShapeDtypeStruct((modes, hours), jnp.bfloat16),
        ),
        in_specs=[IN_VMEM] * (2 + 2 * len(held)),
        out_specs=(ANYWHERE, ANYWHERE, IN_VMEM),
        scratch_shapes=[
            pltpu.VMEM((hours, rank), jnp.float32),
            pltpu.VMEM((hours, rank), jnp.float32),
            pltpu.VMEM((modes, held[0].shape[1]), jnp.bfloat16),
            pltpu.VMEM((rank, rank), jnp.float32),
            pltpu.SemaphoreType.DMA((tiles + 1,)),
        ],
        compiler_params=pltpu.CompilerParams(vmem_limit_bytes=40 * 2**20),
        cost_estimate=LONG,
        name="rebuild_first",
    )(energy, vectors, *held, *coeffs)


def rebuild_last(weights, held, modes, begin, tiles):
    return pl.pallas_call(
        functools.partial(last_kernel, begin, tiles),
        out_shape=jax.ShapeDtypeStruct(modes.shape, modes.dtype),
        in_specs=[IN_VMEM] * (1 + len(held)) + [ANYWHERE],
        out_specs=ANYWHERE,
        scratch_shapes=[
            pltpu.VMEM((modes.shape[0], modes.shape[1] - begin), modes.dtype),
            pltpu.SemaphoreType.DMA((tiles,)),
        ],
        input_output_aliases={1 + len(held): 0},
        compiler_params=pltpu.CompilerParams(vmem_limit_bytes=40 * 2**20),
        cost_estimate=FREE,
        name="rebuild_last",
    )(weights, *held, modes)


def swapped(value, axis, bit):
    route = [(i ^ bit, i) for i in range(lax.axis_size(axis))]
    return lax.ppermute(value, axis, route)


def moved(value, by, swap):
    size = lax.axis_size("tm")
    route = [
        (2 * ((i + by) % size) + (core ^ swap), 2 * i + core)
        for i in range(size)
        for core in range(2)
    ]
    return lax.ppermute(value, ("tm", "inner"), route)


def per_device(eof_basis, snapshots, inverse_energy, eigen_vectors):
    tm, outer = lax.axis_size("tm"), lax.axis_size("outer")
    me = lax.axis_index("tm")
    fields = snapshots.T

    cells = fields.shape[1]
    begin = cells // 8 * 7

    early, late = cut(fields, begin)
    first = [early] + [moved(early, k, 0) for k in range(1, tm)]

    kept, given = project(early, late, eof_basis, 8)
    mine = kept + swapped(given, "inner", 1)
    bit = 1
    while bit < outer:
        near = swapped(mine, "outer", bit)
        if 2 * bit < outer:
            far, both = (swapped(mine, "outer", b) for b in (2 * bit, 3 * bit))
            mine = (mine + near) + (far + both)
        else:
            mine = mine + near
        bit *= 4
    mine = mine.astype(jnp.bfloat16)
    both = jnp.stack([mine, moved(mine, 0, 1)])
    both, behind = lax.optimization_barrier((both, late))
    last = [late] + [moved(behind, k, 0) for k in range(1, tm)]
    coeffs = [both] + [moved(both, k, 0) for k in range(1, tm)]

    rows = eigen_vectors.shape[1] // tm
    vectors = lax.dynamic_slice_in_dim(eigen_vectors, me * rows, rows, 1)
    operator, modes, weights = rebuild_first(
        inverse_energy[None, :], vectors.T, first, coeffs, cells, 4
    )
    return operator, rebuild_last(weights, last, modes, begin, 2)


def solution(mesh):
    tm, space = mesh.shape["tm"], mesh.shape["space"]
    split = Mesh(mesh.devices.reshape(tm, space // 2, 2), ("tm", "outer", "inner"))
    cells = ("outer", "inner")
    in_specs = (P(cells, None), P(cells, "tm"), P(), P())
    out_specs = (P(), P("tm", cells))
    return jax.shard_map(
        per_device, mesh=split, in_specs=in_specs, out_specs=out_specs, check_vma=False
    )
```

```python
import functools

import jax
import jax.numpy as jnp
from jax import lax
from jax.experimental import pallas as pl
from jax.experimental.pallas import tpu as pltpu
from jax.sharding import Mesh, PartitionSpec as P

ROWS = (((1,), (0,)), ((), ()))
FIRST = (((0,), (0,)), ((), ()))
LAST = (((1,), (1,)), ((), ()))
STRIP = 256
FREE = pl.CostEstimate(flops=0, bytes_accessed=0, transcendentals=0)
LONG = pl.CostEstimate(flops=3 * 10**9, bytes_accessed=0, transcendentals=0)
ANYWHERE = pl.BlockSpec(memory_space=pl.ANY)
IN_VMEM = pl.BlockSpec(memory_space=pltpu.VMEM)


def started(copies):
    for copy in copies:
        copy.start()
    return copies


def waited(copies):
    for copy in copies:
        copy.wait()


def in_parts(value):
    high = value.astype(jnp.bfloat16)
    return high, (value - high.astype(jnp.float32)).astype(jnp.bfloat16)


def product(left, right, dims):
    return lax.dot_general(left, right, dims, preferred_element_type=jnp.float32)


def cut_kernel(begin, fields, early, late, sent):
    spans = pl.ds(0, begin), pl.ds(begin, late.shape[1])
    waited(
        started(
            [
                pltpu.make_async_copy(fields.at[:, span], piece, sent.at[i])
                for i, (span, piece) in enumerate(zip(spans, (early, late)))
            ]
        )
    )


def cut(fields, begin):
    hours, cells = fields.shape
    return pl.pallas_call(
        functools.partial(cut_kernel, begin),
        out_shape=(
            jax.ShapeDtypeStruct((hours, begin), fields.dtype),
            jax.ShapeDtypeStruct((hours, cells - begin), fields.dtype),
        ),
        in_specs=[ANYWHERE],
        out_specs=(ANYWHERE, ANYWHERE),
        scratch_shapes=[pltpu.SemaphoreType.DMA((2,))],
        compiler_params=pltpu.CompilerParams(vmem_limit_bytes=52 * 2**20),
        cost_estimate=FREE,
        name="cut",
    )(fields)


def project_kernel(tiles, early, late, basis, kept, given, patterns, halves, arrived):
    cells = basis.shape[0]
    tile, begin = cells // tiles, early.shape[1]
    spans = [pl.ds(i * tile, tile) for i in range(tiles)]
    copies = started(
        [
            pltpu.make_async_copy(basis.at[span], patterns.at[span], arrived.at[i])
            for i, span in enumerate(spans)
        ]
    )
    total = jnp.zeros((early.shape[0], patterns.shape[1]), jnp.float32)
    for i, span in enumerate(spans):
        copies[i].wait()
        at = i * tile
        fields = early[:, span] if at < begin else late[:, pl.ds(at - begin, tile)]
        total += product(fields, patterns[span], ROWS)
    half = kept.shape[0]
    core = lax.axis_index("inner")
    halves[0] = total[:half]
    halves[1] = total[half:]
    kept[...] = halves[core]
    given[...] = halves[1 - core]


def project(early, late, basis, tiles):
    hours, rank = early.shape[0], basis.shape[1]
    half = jax.ShapeDtypeStruct((hours // 2, rank), jnp.float32)
    return pl.pallas_call(
        functools.partial(project_kernel, tiles),
        out_shape=(half, half),
        in_specs=[IN_VMEM, IN_VMEM, ANYWHERE],
        out_specs=(IN_VMEM, IN_VMEM),
        scratch_shapes=[
            pltpu.VMEM(basis.shape, basis.dtype),
            pltpu.VMEM((2, hours // 2, rank), jnp.float32),
            pltpu.SemaphoreType.DMA((tiles,)),
        ],
        compiler_params=pltpu.CompilerParams(vmem_limit_bytes=52 * 2**20),
        cost_estimate=FREE,
        name="project",
    )(early, late, basis)


def lagged_and_scaled(every, energy):
    hour = lax.broadcasted_iota(jnp.int32, every.shape, 0)
    return jnp.where(hour == 0, 0.0, pltpu.roll(every, 1, 0)) * energy


def columns(held, begin, width):
    return jnp.concatenate([b[:, pl.ds(begin - at, width)] for b, at in held], axis=0)


def rebuilt(weights, held, made, modes, begin, tiles, sent, between=list):
    strips = made.shape[1] // STRIP
    edges = [strips * i // tiles * STRIP for i in range(tiles + 1)]
    outgoing = []
    for i in range(tiles):
        if i == tiles - 1:
            outgoing += between()
        for at in range(edges[i], edges[i + 1], STRIP):
            fields = columns(held, begin + at, STRIP)
            made[:, pl.ds(at, STRIP)] = product(weights, fields, ROWS).astype(made.dtype)
        width = edges[i + 1] - edges[i]
        source, target = made.at[:, pl.ds(edges[i], width)], pl.ds(begin + edges[i], width)
        outgoing += started([pltpu.make_async_copy(source, modes.at[:, target], sent.at[i])])
    return outgoing


def first_kernel(tiles, energy, vectors, *refs):
    count = (len(refs) - 8) // 2
    held, coeffs, refs = refs[:count], refs[count : 2 * count], refs[2 * count :]
    operator, modes, weights, known, scaled, made, square, sent = refs
    hours = held[0].shape[0]
    half = hours // 2
    me, core = lax.axis_index("tm"), lax.axis_index("inner")
    first = [lax.rem(me + k, count) * hours for k in range(count)]
    for k, block in enumerate(coeffs):
        for n in range(2):
            at = pl.multiple_of(first[k] + lax.rem(core + n, 2) * half, half)
            known[pl.ds(at, half)] = block[n].astype(jnp.float32)
    every = known[...].astype(jnp.bfloat16)
    scaled[...] = lagged_and_scaled(known[...], energy[...])
    ordered = jnp.concatenate(
        [scaled[pl.ds(pl.multiple_of(at, hours), hours)] for at in first], axis=0
    )
    high, low = in_parts(ordered)
    value = (product(vectors[...], high, LAST) + product(vectors[...], low, LAST)).astype(
        jnp.bfloat16
    )
    weights[...] = value

    def operate():
        high, low = in_parts(scaled[...])
        square[...] = product(every, high, FIRST) + product(every, low, FIRST)
        return started([pltpu.make_async_copy(square, operator, sent.at[tiles])])

    waited(rebuilt(value, [(b, 0) for b in held], made, modes, 0, tiles, sent, operate))


def last_kernel(begin, tiles, weights, *refs):
    held, (_, modes, made, sent) = refs[:-4], refs[-4:]
    blocks = [(b, begin) for b in held]
    waited(rebuilt(weights[...], blocks, made, modes, begin, tiles, sent))


def rebuild_first(energy, vectors, held, coeffs, cells, tiles):
    rank = coeffs[0].shape[2]
    hours, modes = len(held) * held[0].shape[0], vectors.shape[0]
    return pl.pallas_call(
        functools.partial(first_kernel, tiles),
        out_shape=(
            jax.ShapeDtypeStruct((rank, rank), jnp.float32),
            jax.ShapeDtypeStruct((modes, cells), jnp.bfloat16),
            jax.ShapeDtypeStruct((modes, hours), jnp.bfloat16),
        ),
        in_specs=[IN_VMEM] * (2 + 2 * len(held)),
        out_specs=(ANYWHERE, ANYWHERE, IN_VMEM),
        scratch_shapes=[
            pltpu.VMEM((hours, rank), jnp.float32),
            pltpu.VMEM((hours, rank), jnp.float32),
            pltpu.VMEM((modes, held[0].shape[1]), jnp.bfloat16),
            pltpu.VMEM((rank, rank), jnp.float32),
            pltpu.SemaphoreType.DMA((tiles + 1,)),
        ],
        compiler_params=pltpu.CompilerParams(vmem_limit_bytes=40 * 2**20),
        cost_estimate=LONG,
        name="rebuild_first",
    )(energy, vectors, *held, *coeffs)


def rebuild_last(weights, held, modes, begin, tiles):
    return pl.pallas_call(
        functools.partial(last_kernel, begin, tiles),
        out_shape=jax.ShapeDtypeStruct(modes.shape, modes.dtype),
        in_specs=[IN_VMEM] * (1 + len(held)) + [ANYWHERE],
        out_specs=ANYWHERE,
        scratch_shapes=[
            pltpu.VMEM((modes.shape[0], modes.shape[1] - begin), modes.dtype),
            pltpu.SemaphoreType.DMA((tiles,)),
        ],
        input_output_aliases={1 + len(held): 0},
        compiler_params=pltpu.CompilerParams(vmem_limit_bytes=40 * 2**20),
        cost_estimate=FREE,
        name="rebuild_last",
    )(weights, *held, modes)


def swapped(value, axis, bit):
    route = [(i ^ bit, i) for i in range(lax.axis_size(axis))]
    return lax.ppermute(value, axis, route)


def moved(value, by, swap):
    size = lax.axis_size("tm")
    route = [
        (2 * ((i + by) % size) + (core ^ swap), 2 * i + core)
        for i in range(size)
        for core in range(2)
    ]
    return lax.ppermute(value, ("tm", "inner"), route)


def per_device(eof_basis, snapshots, inverse_energy, eigen_vectors):
    tm, outer = lax.axis_size("tm"), lax.axis_size("outer")
    me = lax.axis_index("tm")
    fields = snapshots.T

    cells = fields.shape[1]
    begin = cells // 16 * 13

    early, late = cut(fields, begin)
    first = [early] + [moved(early, k, 0) for k in range(1, tm)]

    kept, given = project(early, late, eof_basis, 16)
    mine = kept + swapped(given, "inner", 1)
    bit = 1
    while bit < outer:
        near = swapped(mine, "outer", bit)
        if 2 * bit < outer:
            far, both = (swapped(mine, "outer", b) for b in (2 * bit, 3 * bit))
            mine = (mine + near) + (far + both)
        else:
            mine = mine + near
        bit *= 4
    mine = mine.astype(jnp.bfloat16)
    both = jnp.stack([mine, moved(mine, 0, 1)])
    both, behind = lax.optimization_barrier((both, late))
    last = [late] + [moved(behind, k, 0) for k in range(1, tm)]
    coeffs = [both] + [moved(both, k, 0) for k in range(1, tm)]

    rows = eigen_vectors.shape[1] // tm
    vectors = lax.dynamic_slice_in_dim(eigen_vectors, me * rows, rows, 1)
    operator, modes, weights = rebuild_first(
        inverse_energy[None, :], vectors.T, first, coeffs, cells, 4
    )
    return operator, rebuild_last(weights, last, modes, begin, 2)


def solution(mesh):
    tm, space = mesh.shape["tm"], mesh.shape["space"]
    split = Mesh(mesh.devices.reshape(tm, space // 2, 2), ("tm", "outer", "inner"))
    cells = ("outer", "inner")
    in_specs = (P(cells, None), P(cells, "tm"), P(), P())
    out_specs = (P(), P("tm", cells))
    return jax.shard_map(
        per_device, mesh=split, in_specs=in_specs, out_specs=out_specs, check_vma=False
    )
```

```python
import functools

import jax
import jax.numpy as jnp
from jax import lax
from jax.experimental import pallas as pl
from jax.experimental.pallas import tpu as pltpu
from jax.sharding import Mesh, PartitionSpec as P

ROWS = (((1,), (0,)), ((), ()))
FIRST = (((0,), (0,)), ((), ()))
LAST = (((1,), (1,)), ((), ()))
STRIP = 256
FREE = pl.CostEstimate(flops=0, bytes_accessed=0, transcendentals=0)
LONG = pl.CostEstimate(flops=2 * 10**9, bytes_accessed=0, transcendentals=0)
ANYWHERE = pl.BlockSpec(memory_space=pl.ANY)
IN_VMEM = pl.BlockSpec(memory_space=pltpu.VMEM)


def started(copies):
    for copy in copies:
        copy.start()
    return copies


def waited(copies):
    for copy in copies:
        copy.wait()


def in_parts(value):
    high = value.astype(jnp.bfloat16)
    return high, (value - high.astype(jnp.float32)).astype(jnp.bfloat16)


def product(left, right, dims):
    return lax.dot_general(left, right, dims, preferred_element_type=jnp.float32)


def cut_kernel(begin, fields, early, late, sent):
    spans = pl.ds(0, begin), pl.ds(begin, late.shape[1])
    waited(
        started(
            [
                pltpu.make_async_copy(fields.at[:, span], piece, sent.at[i])
                for i, (span, piece) in enumerate(zip(spans, (early, late)))
            ]
        )
    )


def cut(fields, begin):
    hours, cells = fields.shape
    return pl.pallas_call(
        functools.partial(cut_kernel, begin),
        out_shape=(
            jax.ShapeDtypeStruct((hours, begin), fields.dtype),
            jax.ShapeDtypeStruct((hours, cells - begin), fields.dtype),
        ),
        in_specs=[ANYWHERE],
        out_specs=(ANYWHERE, ANYWHERE),
        scratch_shapes=[pltpu.SemaphoreType.DMA((2,))],
        compiler_params=pltpu.CompilerParams(vmem_limit_bytes=52 * 2**20),
        cost_estimate=FREE,
        name="cut",
    )(fields)


def project_kernel(tiles, early, late, basis, kept, given, patterns, halves, arrived):
    cells = basis.shape[0]
    tile, begin = cells // tiles, early.shape[1]
    spans = [pl.ds(i * tile, tile) for i in range(tiles)]
    copies = started(
        [
            pltpu.make_async_copy(basis.at[span], patterns.at[span], arrived.at[i])
            for i, span in enumerate(spans)
        ]
    )
    total = jnp.zeros((early.shape[0], patterns.shape[1]), jnp.float32)
    for i, span in enumerate(spans):
        copies[i].wait()
        at = i * tile
        fields = early[:, span] if at < begin else late[:, pl.ds(at - begin, tile)]
        total += product(fields, patterns[span], ROWS)
    half = kept.shape[0]
    core = lax.axis_index("inner")
    halves[0] = total[:half]
    halves[1] = total[half:]
    kept[...] = halves[core]
    given[...] = halves[1 - core]


def project(early, late, basis, tiles):
    hours, rank = early.shape[0], basis.shape[1]
    half = jax.ShapeDtypeStruct((hours // 2, rank), jnp.float32)
    return pl.pallas_call(
        functools.partial(project_kernel, tiles),
        out_shape=(half, half),
        in_specs=[IN_VMEM, IN_VMEM, ANYWHERE],
        out_specs=(IN_VMEM, IN_VMEM),
        scratch_shapes=[
            pltpu.VMEM(basis.shape, basis.dtype),
            pltpu.VMEM((2, hours // 2, rank), jnp.float32),
            pltpu.SemaphoreType.DMA((tiles,)),
        ],
        compiler_params=pltpu.CompilerParams(vmem_limit_bytes=52 * 2**20),
        cost_estimate=FREE,
        name="project",
    )(early, late, basis)


def lagged_and_scaled(every, energy):
    hour = lax.broadcasted_iota(jnp.int32, every.shape, 0)
    return jnp.where(hour == 0, 0.0, pltpu.roll(every, 1, 0)) * energy


def columns(held, begin, width):
    return jnp.concatenate([b[:, pl.ds(begin - at, width)] for b, at in held], axis=0)


def rebuilt(weights, held, made, modes, begin, tiles, sent, between=list):
    strips = made.shape[1] // STRIP
    edges = [strips * i // tiles * STRIP for i in range(tiles + 1)]
    outgoing = []
    for i in range(tiles):
        if i == tiles - 1:
            outgoing += between()
        for at in range(edges[i], edges[i + 1], STRIP):
            fields = columns(held, begin + at, STRIP)
            made[:, pl.ds(at, STRIP)] = product(weights, fields, ROWS).astype(made.dtype)
        width = edges[i + 1] - edges[i]
        source, target = made.at[:, pl.ds(edges[i], width)], pl.ds(begin + edges[i], width)
        outgoing += started([pltpu.make_async_copy(source, modes.at[:, target], sent.at[i])])
    return outgoing


def first_kernel(tiles, energy, vectors, *refs):
    count = (len(refs) - 8) // 3
    held, coeffs, refs = refs[:count], refs[count : 3 * count], refs[3 * count :]
    operator, modes, weights, known, scaled, made, square, sent = refs
    hours = held[0].shape[0]
    half = hours // 2
    me, core = lax.axis_index("tm"), lax.axis_index("inner")
    first = [lax.rem(me + k, count) * hours for k in range(count)]
    for n, block in enumerate(coeffs):
        at = pl.multiple_of(first[n // 2] + lax.rem(core + n % 2, 2) * half, half)
        known[pl.ds(at, half)] = block[...].astype(jnp.float32)
    every = known[...].astype(jnp.bfloat16)
    scaled[...] = lagged_and_scaled(known[...], energy[...])
    ordered = jnp.concatenate(
        [scaled[pl.ds(pl.multiple_of(at, hours), hours)] for at in first], axis=0
    )
    high, low = in_parts(ordered)
    value = (product(vectors[...], high, LAST) + product(vectors[...], low, LAST)).astype(
        jnp.bfloat16
    )
    weights[...] = value

    def operate():
        high, low = in_parts(scaled[...])
        square[...] = product(every, high, FIRST) + product(every, low, FIRST)
        return started([pltpu.make_async_copy(square, operator, sent.at[tiles])])

    waited(rebuilt(value, [(b, 0) for b in held], made, modes, 0, tiles, sent, operate))


def last_kernel(begin, tiles, weights, *refs):
    held, (_, modes, made, sent) = refs[:-4], refs[-4:]
    blocks = [(b, begin) for b in held]
    waited(rebuilt(weights[...], blocks, made, modes, begin, tiles, sent))


def rebuild_first(energy, vectors, held, coeffs, cells, tiles):
    rank = coeffs[0].shape[1]
    hours, modes = len(held) * held[0].shape[0], vectors.shape[0]
    return pl.pallas_call(
        functools.partial(first_kernel, tiles),
        out_shape=(
            jax.ShapeDtypeStruct((rank, rank), jnp.float32),
            jax.ShapeDtypeStruct((modes, cells), jnp.bfloat16),
            jax.ShapeDtypeStruct((modes, hours), jnp.bfloat16),
        ),
        in_specs=[IN_VMEM] * (2 + 3 * len(held)),
        out_specs=(ANYWHERE, ANYWHERE, IN_VMEM),
        scratch_shapes=[
            pltpu.VMEM((hours, rank), jnp.float32),
            pltpu.VMEM((hours, rank), jnp.float32),
            pltpu.VMEM((modes, held[0].shape[1]), jnp.bfloat16),
            pltpu.VMEM((rank, rank), jnp.float32),
            pltpu.SemaphoreType.DMA((tiles + 1,)),
        ],
        compiler_params=pltpu.CompilerParams(vmem_limit_bytes=40 * 2**20),
        cost_estimate=LONG,
        name="rebuild_first",
    )(energy, vectors, *held, *coeffs)


def rebuild_last(weights, held, modes, begin, tiles):
    return pl.pallas_call(
        functools.partial(last_kernel, begin, tiles),
        out_shape=jax.ShapeDtypeStruct(modes.shape, modes.dtype),
        in_specs=[IN_VMEM] * (1 + len(held)) + [ANYWHERE],
        out_specs=ANYWHERE,
        scratch_shapes=[
            pltpu.VMEM((modes.shape[0], modes.shape[1] - begin), modes.dtype),
            pltpu.SemaphoreType.DMA((tiles,)),
        ],
        input_output_aliases={1 + len(held): 0},
        compiler_params=pltpu.CompilerParams(vmem_limit_bytes=40 * 2**20),
        cost_estimate=FREE,
        name="rebuild_last",
    )(weights, *held, modes)


def swapped(value, axis, bit):
    route = [(i ^ bit, i) for i in range(lax.axis_size(axis))]
    return lax.ppermute(value, axis, route)


def moved(value, by, swap):
    size = lax.axis_size("tm")
    route = [
        (2 * ((i + by) % size) + (core ^ swap), 2 * i + core)
        for i in range(size)
        for core in range(2)
    ]
    return lax.ppermute(value, ("tm", "inner"), route)


def per_device(eof_basis, snapshots, inverse_energy, eigen_vectors):
    tm, outer = lax.axis_size("tm"), lax.axis_size("outer")
    me = lax.axis_index("tm")
    fields = snapshots.T

    cells = fields.shape[1]
    begin = cells // 16 * 13

    early, late = cut(fields, begin)
    first = [early] + [moved(early, k, 0) for k in range(1, tm)]

    kept, given = project(early, late, eof_basis, 16)
    mine = kept + swapped(given, "inner", 1)
    bit = 1
    while bit < outer:
        near = swapped(mine, "outer", bit)
        if 2 * bit < outer:
            far, both = (swapped(mine, "outer", b) for b in (2 * bit, 3 * bit))
            mine = (mine + near) + (far + both)
        else:
            mine = mine + near
        bit *= 4
    mine = mine.astype(jnp.bfloat16)
    mine, behind = lax.optimization_barrier((mine, late))
    coeffs = []
    for k in range(tm):
        theirs = moved(mine, k, 0) if k else mine
        coeffs += [theirs, moved(theirs, 0, 1)]
    last = [late] + [moved(behind, k, 0) for k in range(1, tm)]

    rows = eigen_vectors.shape[1] // tm
    vectors = lax.dynamic_slice_in_dim(eigen_vectors, me * rows, rows, 1)
    operator, modes, weights = rebuild_first(
        inverse_energy[None, :], vectors.T, first, coeffs, cells, 4
    )
    return operator, rebuild_last(weights, last, modes, begin, 2)


def solution(mesh):
    tm, space = mesh.shape["tm"], mesh.shape["space"]
    split = Mesh(mesh.devices.reshape(tm, space // 2, 2), ("tm", "outer", "inner"))
    cells = ("outer", "inner")
    in_specs = (P(cells, None), P(cells, "tm"), P(), P())
    out_specs = (P(), P("tm", cells))
    return jax.shard_map(
        per_device, mesh=split, in_specs=in_specs, out_specs=out_specs, check_vma=False
    )
```

```python
import functools

import jax
import jax.numpy as jnp
from jax import lax
from jax.experimental import pallas as pl
from jax.experimental.pallas import tpu as pltpu
from jax.sharding import Mesh, PartitionSpec as P

ROWS = (((1,), (0,)), ((), ()))
FIRST = (((0,), (0,)), ((), ()))
LAST = (((1,), (1,)), ((), ()))
STRIP = 256
FREE = pl.CostEstimate(flops=0, bytes_accessed=0, transcendentals=0)
LONG = pl.CostEstimate(flops=2 * 10**9, bytes_accessed=0, transcendentals=0)
ANYWHERE = pl.BlockSpec(memory_space=pl.ANY)
IN_VMEM = pl.BlockSpec(memory_space=pltpu.VMEM)


def started(copies):
    for copy in copies:
        copy.start()
    return copies


def waited(copies):
    for copy in copies:
        copy.wait()


def in_parts(value):
    high = value.astype(jnp.bfloat16)
    return high, (value - high.astype(jnp.float32)).astype(jnp.bfloat16)


def product(left, right, dims):
    return lax.dot_general(left, right, dims, preferred_element_type=jnp.float32)


def cut_kernel(begin, fields, early, late, sent):
    half = begin // 2
    copies = [
        pltpu.make_async_copy(
            fields.at[:, pl.ds(at, half)], early.at[:, pl.ds(at, half)], sent.at[at // half]
        )
        for at in (0, half)
    ]
    rest = fields.at[:, pl.ds(begin, late.shape[1])]
    waited(started(copies + [pltpu.make_async_copy(rest, late, sent.at[2])]))


def cut(fields, begin):
    hours, cells = fields.shape
    return pl.pallas_call(
        functools.partial(cut_kernel, begin),
        out_shape=(
            jax.ShapeDtypeStruct((hours, begin), fields.dtype),
            jax.ShapeDtypeStruct((hours, cells - begin), fields.dtype),
        ),
        in_specs=[ANYWHERE],
        out_specs=(ANYWHERE, ANYWHERE),
        scratch_shapes=[pltpu.SemaphoreType.DMA((3,))],
        compiler_params=pltpu.CompilerParams(vmem_limit_bytes=52 * 2**20),
        cost_estimate=FREE,
        name="cut",
    )(fields)


def project_kernel(tiles, early, late, basis, kept, given, patterns, halves, arrived):
    cells = basis.shape[0]
    tile, begin = cells // tiles, early.shape[1]
    spans = [pl.ds(i * tile, tile) for i in range(tiles)]
    copies = started(
        [
            pltpu.make_async_copy(basis.at[span], patterns.at[span], arrived.at[i])
            for i, span in enumerate(spans)
        ]
    )
    total = jnp.zeros((early.shape[0], patterns.shape[1]), jnp.float32)
    for i, span in enumerate(spans):
        copies[i].wait()
        at = i * tile
        fields = early[:, span] if at < begin else late[:, pl.ds(at - begin, tile)]
        total += product(fields, patterns[span], ROWS)
    half = kept.shape[0]
    core = lax.axis_index("inner")
    halves[0] = total[:half]
    halves[1] = total[half:]
    kept[...] = halves[core]
    given[...] = halves[1 - core]


def project(early, late, basis, tiles):
    hours, rank = early.shape[0], basis.shape[1]
    half = jax.ShapeDtypeStruct((hours // 2, rank), jnp.float32)
    return pl.pallas_call(
        functools.partial(project_kernel, tiles),
        out_shape=(half, half),
        in_specs=[IN_VMEM, IN_VMEM, ANYWHERE],
        out_specs=(IN_VMEM, IN_VMEM),
        scratch_shapes=[
            pltpu.VMEM(basis.shape, basis.dtype),
            pltpu.VMEM((2, hours // 2, rank), jnp.float32),
            pltpu.SemaphoreType.DMA((tiles,)),
        ],
        compiler_params=pltpu.CompilerParams(vmem_limit_bytes=52 * 2**20),
        cost_estimate=FREE,
        name="project",
    )(early, late, basis)


def lagged_and_scaled(every, energy):
    hour = lax.broadcasted_iota(jnp.int32, every.shape, 0)
    return jnp.where(hour == 0, 0.0, pltpu.roll(every, 1, 0)) * energy


def columns(held, begin, width):
    return jnp.concatenate([b[:, pl.ds(begin - at, width)] for b, at in held], axis=0)


def rebuilt(weights, held, made, modes, begin, tiles, sent, between=list):
    strips = made.shape[1] // STRIP
    edges = [strips * i // tiles * STRIP for i in range(tiles + 1)]
    outgoing = []
    for i in range(tiles):
        if i == tiles - 1:
            outgoing += between()
        for at in range(edges[i], edges[i + 1], STRIP):
            fields = columns(held, begin + at, STRIP)
            made[:, pl.ds(at, STRIP)] = product(weights, fields, ROWS).astype(made.dtype)
        width = edges[i + 1] - edges[i]
        source, target = made.at[:, pl.ds(edges[i], width)], pl.ds(begin + edges[i], width)
        outgoing += started([pltpu.make_async_copy(source, modes.at[:, target], sent.at[i])])
    return outgoing


def first_kernel(tiles, energy, vectors, *refs):
    count = (len(refs) - 8) // 3
    held, coeffs, refs = refs[:count], refs[count : 3 * count], refs[3 * count :]
    operator, modes, weights, known, scaled, made, square, sent = refs
    hours = held[0].shape[0]
    half = hours // 2
    me, core = lax.axis_index("tm"), lax.axis_index("inner")
    first = [lax.rem(me + k, count) * hours for k in range(count)]
    for n, block in enumerate(coeffs):
        at = pl.multiple_of(first[n // 2] + lax.rem(core + n % 2, 2) * half, half)
        known[pl.ds(at, half)] = block[...].astype(jnp.float32)
    every = known[...].astype(jnp.bfloat16)
    scaled[...] = lagged_and_scaled(known[...], energy[...])
    ordered = jnp.concatenate(
        [scaled[pl.ds(pl.multiple_of(at, hours), hours)] for at in first], axis=0
    )
    high, low = in_parts(ordered)
    value = (product(vectors[...], high, LAST) + product(vectors[...], low, LAST)).astype(
        jnp.bfloat16
    )
    weights[...] = value

    def operate():
        high, low = in_parts(scaled[...])
        square[...] = product(every, high, FIRST) + product(every, low, FIRST)
        return started([pltpu.make_async_copy(square, operator, sent.at[tiles])])

    waited(rebuilt(value, [(b, 0) for b in held], made, modes, 0, tiles, sent, operate))


def last_kernel(begin, tiles, weights, *refs):
    held, (_, modes, made, sent) = refs[:-4], refs[-4:]
    blocks = [(b, begin) for b in held]
    waited(rebuilt(weights[...], blocks, made, modes, begin, tiles, sent))


def rebuild_first(energy, vectors, held, coeffs, cells, tiles):
    rank = coeffs[0].shape[1]
    hours, modes = len(held) * held[0].shape[0], vectors.shape[0]
    return pl.pallas_call(
        functools.partial(first_kernel, tiles),
        out_shape=(
            jax.ShapeDtypeStruct((rank, rank), jnp.float32),
            jax.ShapeDtypeStruct((modes, cells), jnp.bfloat16),
            jax.ShapeDtypeStruct((modes, hours), jnp.bfloat16),
        ),
        in_specs=[IN_VMEM] * (2 + 3 * len(held)),
        out_specs=(ANYWHERE, ANYWHERE, IN_VMEM),
        scratch_shapes=[
            pltpu.VMEM((hours, rank), jnp.float32),
            pltpu.VMEM((hours, rank), jnp.float32),
            pltpu.VMEM((modes, held[0].shape[1]), jnp.bfloat16),
            pltpu.VMEM((rank, rank), jnp.float32),
            pltpu.SemaphoreType.DMA((tiles + 1,)),
        ],
        compiler_params=pltpu.CompilerParams(vmem_limit_bytes=40 * 2**20),
        cost_estimate=LONG,
        name="rebuild_first",
    )(energy, vectors, *held, *coeffs)


def rebuild_last(weights, held, modes, begin, tiles):
    return pl.pallas_call(
        functools.partial(last_kernel, begin, tiles),
        out_shape=jax.ShapeDtypeStruct(modes.shape, modes.dtype),
        in_specs=[IN_VMEM] * (1 + len(held)) + [ANYWHERE],
        out_specs=ANYWHERE,
        scratch_shapes=[
            pltpu.VMEM((modes.shape[0], modes.shape[1] - begin), modes.dtype),
            pltpu.SemaphoreType.DMA((tiles,)),
        ],
        input_output_aliases={1 + len(held): 0},
        compiler_params=pltpu.CompilerParams(vmem_limit_bytes=40 * 2**20),
        cost_estimate=FREE,
        name="rebuild_last",
    )(weights, *held, modes)


def swapped(value, axis, bit):
    route = [(i ^ bit, i) for i in range(lax.axis_size(axis))]
    return lax.ppermute(value, axis, route)


def moved(value, by, swap):
    size = lax.axis_size("tm")
    route = [
        (2 * ((i + by) % size) + (core ^ swap), 2 * i + core)
        for i in range(size)
        for core in range(2)
    ]
    return lax.ppermute(value, ("tm", "inner"), route)


def per_device(eof_basis, snapshots, inverse_energy, eigen_vectors):
    tm, outer = lax.axis_size("tm"), lax.axis_size("outer")
    me = lax.axis_index("tm")
    fields = snapshots.T

    cells = fields.shape[1]
    begin = cells // 16 * 13

    early, late = cut(fields, begin)
    first = [early] + [moved(early, k, 0) for k in range(1, tm)]

    kept, given = project(early, late, eof_basis, 16)
    mine = kept + swapped(given, "inner", 1)
    bit = 1
    while bit < outer:
        near = swapped(mine, "outer", bit)
        if 2 * bit < outer:
            far, both = (swapped(mine, "outer", b) for b in (2 * bit, 3 * bit))
            mine = (mine + near) + (far + both)
        else:
            mine = mine + near
        bit *= 4
    mine = mine.astype(jnp.bfloat16)
    mine, behind = lax.optimization_barrier((mine, late))
    coeffs = []
    for k in range(tm):
        theirs = moved(mine, k, 0) if k else mine
        coeffs += [theirs, moved(theirs, 0, 1)]
    last = [late] + [moved(behind, k, 0) for k in range(1, tm)]

    rows = eigen_vectors.shape[1] // tm
    vectors = lax.dynamic_slice_in_dim(eigen_vectors, me * rows, rows, 1)
    operator, modes, weights = rebuild_first(
        inverse_energy[None, :], vectors.T, first, coeffs, cells, 6
    )
    return operator, rebuild_last(weights, last, modes, begin, 3)


def solution(mesh):
    tm, space = mesh.shape["tm"], mesh.shape["space"]
    split = Mesh(mesh.devices.reshape(tm, space // 2, 2), ("tm", "outer", "inner"))
    cells = ("outer", "inner")
    in_specs = (P(cells, None), P(cells, "tm"), P(), P())
    out_specs = (P(), P("tm", cells))
    return jax.shard_map(
        per_device, mesh=split, in_specs=in_specs, out_specs=out_specs, check_vma=False
    )
```

```python
import functools

import jax
import jax.numpy as jnp
from jax import lax
from jax.experimental import pallas as pl
from jax.experimental.pallas import tpu as pltpu
from jax.sharding import Mesh, PartitionSpec as P

ROWS = (((1,), (0,)), ((), ()))
FIRST = (((0,), (0,)), ((), ()))
LAST = (((1,), (1,)), ((), ()))
STRIP = 256
FREE = pl.CostEstimate(flops=0, bytes_accessed=0, transcendentals=0)
LONG = pl.CostEstimate(flops=2 * 10**9, bytes_accessed=0, transcendentals=0)
ANYWHERE = pl.BlockSpec(memory_space=pl.ANY)
IN_VMEM = pl.BlockSpec(memory_space=pltpu.VMEM)


def started(copies):
    for copy in copies:
        copy.start()
    return copies


def waited(copies):
    for copy in copies:
        copy.wait()


def in_parts(value):
    high = value.astype(jnp.bfloat16)
    return high, (value - high.astype(jnp.float32)).astype(jnp.bfloat16)


def product(left, right, dims):
    return lax.dot_general(left, right, dims, preferred_element_type=jnp.float32)


def cut_kernel(fields, early, sent):
    half = early.shape[1] // 2
    spans = [pl.ds(at, half) for at in (0, half)]
    waited(
        started(
            [
                pltpu.make_async_copy(fields.at[:, span], early.at[:, span], sent.at[i])
                for i, span in enumerate(spans)
            ]
        )
    )


def cut(fields, width):
    return pl.pallas_call(
        cut_kernel,
        out_shape=jax.ShapeDtypeStruct((fields.shape[0], width), fields.dtype),
        in_specs=[ANYWHERE],
        out_specs=ANYWHERE,
        scratch_shapes=[pltpu.SemaphoreType.DMA((2,))],
        compiler_params=pltpu.CompilerParams(vmem_limit_bytes=53 * 2**20),
        cost_estimate=FREE,
        name="cut",
    )(fields)


def project_kernel(
    tiles, early, fields, basis, kept, given, late, patterns, halves, arrived, landed
):
    cells = basis.shape[0]
    tile, begin = cells // tiles, early.shape[1]
    spans = [pl.ds(i * tile, tile) for i in range(tiles)]
    rest = fields.at[:, pl.ds(begin, late.shape[1])]
    rest = pltpu.make_async_copy(rest, late, landed.at[0])
    copies = started(
        [
            pltpu.make_async_copy(basis.at[span], patterns.at[span], arrived.at[i])
            for i, span in enumerate(spans)
        ]
    )
    rest.start()
    total = jnp.zeros((early.shape[0], patterns.shape[1]), jnp.float32)
    for i, span in enumerate(spans):
        at = i * tile
        if at == begin:
            rest.wait()
        copies[i].wait()
        held = early[:, span] if at < begin else late[:, pl.ds(at - begin, tile)]
        total += product(held, patterns[span], ROWS)
    half = kept.shape[0]
    core = lax.axis_index("inner")
    halves[0] = total[:half]
    halves[1] = total[half:]
    kept[...] = halves[core]
    given[...] = halves[1 - core]


def project(early, fields, basis, tiles):
    (hours, cells), rank = fields.shape, basis.shape[1]
    half = jax.ShapeDtypeStruct((hours // 2, rank), jnp.float32)
    return pl.pallas_call(
        functools.partial(project_kernel, tiles),
        out_shape=(
            half,
            half,
            jax.ShapeDtypeStruct((hours, cells - early.shape[1]), fields.dtype),
        ),
        in_specs=[IN_VMEM, ANYWHERE, ANYWHERE],
        out_specs=(IN_VMEM,) * 3,
        scratch_shapes=[
            pltpu.VMEM(basis.shape, basis.dtype),
            pltpu.VMEM((2, hours // 2, rank), jnp.float32),
            pltpu.SemaphoreType.DMA((tiles,)),
            pltpu.SemaphoreType.DMA((1,)),
        ],
        compiler_params=pltpu.CompilerParams(vmem_limit_bytes=52 * 2**20),
        cost_estimate=FREE,
        name="project",
    )(early, fields, basis)


def lagged_and_scaled(every, energy):
    hour = lax.broadcasted_iota(jnp.int32, every.shape, 0)
    return jnp.where(hour == 0, 0.0, pltpu.roll(every, 1, 0)) * energy


def columns(held, begin, width):
    return jnp.concatenate([b[:, pl.ds(begin - at, width)] for b, at in held], axis=0)


def rebuilt(weights, held, made, modes, begin, tiles, sent, between=list):
    strips = made.shape[1] // STRIP
    edges = [strips * i // tiles * STRIP for i in range(tiles + 1)]
    outgoing = []
    for i in range(tiles):
        if i == tiles - 1:
            outgoing += between()
        for at in range(edges[i], edges[i + 1], STRIP):
            fields = columns(held, begin + at, STRIP)
            made[:, pl.ds(at, STRIP)] = product(weights, fields, ROWS).astype(made.dtype)
        width = edges[i + 1] - edges[i]
        source, target = made.at[:, pl.ds(edges[i], width)], pl.ds(begin + edges[i], width)
        outgoing += started([pltpu.make_async_copy(source, modes.at[:, target], sent.at[i])])
    return outgoing


def first_kernel(tiles, energy, vectors, *refs):
    count = (len(refs) - 8) // 3
    held, coeffs, refs = refs[:count], refs[count : 3 * count], refs[3 * count :]
    operator, modes, weights, known, scaled, made, square, sent = refs
    hours = held[0].shape[0]
    half = hours // 2
    me, core = lax.axis_index("tm"), lax.axis_index("inner")
    first = [lax.rem(me + k, count) * hours for k in range(count)]
    for n, block in enumerate(coeffs):
        at = pl.multiple_of(first[n // 2] + lax.rem(core + n % 2, 2) * half, half)
        known[pl.ds(at, half)] = block[...].astype(jnp.float32)
    every = known[...].astype(jnp.bfloat16)
    scaled[...] = lagged_and_scaled(known[...], energy[...])
    ordered = jnp.concatenate(
        [scaled[pl.ds(pl.multiple_of(at, hours), hours)] for at in first], axis=0
    )
    high, low = in_parts(ordered)
    value = (product(vectors[...], high, LAST) + product(vectors[...], low, LAST)).astype(
        jnp.bfloat16
    )
    weights[...] = value

    def operate():
        high, low = in_parts(scaled[...])
        square[...] = product(every, high, FIRST) + product(every, low, FIRST)
        return started([pltpu.make_async_copy(square, operator, sent.at[tiles])])

    waited(rebuilt(value, [(b, 0) for b in held], made, modes, 0, tiles, sent, operate))


def last_kernel(begin, tiles, weights, *refs):
    held, (_, modes, made, sent) = refs[:-4], refs[-4:]
    blocks = [(b, begin) for b in held]
    waited(rebuilt(weights[...], blocks, made, modes, begin, tiles, sent))


def rebuild_first(energy, vectors, held, coeffs, cells, tiles):
    rank = coeffs[0].shape[1]
    hours, modes = len(held) * held[0].shape[0], vectors.shape[0]
    return pl.pallas_call(
        functools.partial(first_kernel, tiles),
        out_shape=(
            jax.ShapeDtypeStruct((rank, rank), jnp.float32),
            jax.ShapeDtypeStruct((modes, cells), jnp.bfloat16),
            jax.ShapeDtypeStruct((modes, hours), jnp.bfloat16),
        ),
        in_specs=[IN_VMEM] * (2 + 3 * len(held)),
        out_specs=(ANYWHERE, ANYWHERE, IN_VMEM),
        scratch_shapes=[
            pltpu.VMEM((hours, rank), jnp.float32),
            pltpu.VMEM((hours, rank), jnp.float32),
            pltpu.VMEM((modes, held[0].shape[1]), jnp.bfloat16),
            pltpu.VMEM((rank, rank), jnp.float32),
            pltpu.SemaphoreType.DMA((tiles + 1,)),
        ],
        compiler_params=pltpu.CompilerParams(vmem_limit_bytes=40 * 2**20),
        cost_estimate=LONG,
        name="rebuild_first",
    )(energy, vectors, *held, *coeffs)


def rebuild_last(weights, held, modes, begin, tiles):
    return pl.pallas_call(
        functools.partial(last_kernel, begin, tiles),
        out_shape=jax.ShapeDtypeStruct(modes.shape, modes.dtype),
        in_specs=[IN_VMEM] * (1 + len(held)) + [ANYWHERE],
        out_specs=ANYWHERE,
        scratch_shapes=[
            pltpu.VMEM((modes.shape[0], modes.shape[1] - begin), modes.dtype),
            pltpu.SemaphoreType.DMA((tiles,)),
        ],
        input_output_aliases={1 + len(held): 0},
        compiler_params=pltpu.CompilerParams(vmem_limit_bytes=40 * 2**20),
        cost_estimate=FREE,
        name="rebuild_last",
    )(weights, *held, modes)


def swapped(value, axis, bit):
    route = [(i ^ bit, i) for i in range(lax.axis_size(axis))]
    return lax.ppermute(value, axis, route)


def moved(value, by, swap):
    size = lax.axis_size("tm")
    route = [
        (2 * ((i + by) % size) + (core ^ swap), 2 * i + core)
        for i in range(size)
        for core in range(2)
    ]
    return lax.ppermute(value, ("tm", "inner"), route)


def per_device(eof_basis, snapshots, inverse_energy, eigen_vectors):
    tm, outer = lax.axis_size("tm"), lax.axis_size("outer")
    me = lax.axis_index("tm")
    fields = snapshots.T

    cells = fields.shape[1]
    begin = cells // 16 * 13

    early = cut(fields, begin)
    first = [early] + [moved(early, k, 0) for k in range(1, tm)]

    kept, given, late = project(early, fields, eof_basis, 16)
    mine = kept + swapped(given, "inner", 1)
    bit = 1
    while bit < outer:
        near = swapped(mine, "outer", bit)
        if 2 * bit < outer:
            far, both = (swapped(mine, "outer", b) for b in (2 * bit, 3 * bit))
            mine = (mine + near) + (far + both)
        else:
            mine = mine + near
        bit *= 4
    mine = mine.astype(jnp.bfloat16)
    mine, behind = lax.optimization_barrier((mine, late))
    coeffs = []
    for k in range(tm):
        theirs = moved(mine, k, 0) if k else mine
        coeffs += [theirs, moved(theirs, 0, 1)]
    last = [late] + [moved(behind, k, 0) for k in range(1, tm)]

    rows = eigen_vectors.shape[1] // tm
    vectors = lax.dynamic_slice_in_dim(eigen_vectors, me * rows, rows, 1)
    operator, modes, weights = rebuild_first(
        inverse_energy[None, :], vectors.T, first, coeffs, cells, 9
    )
    return operator, rebuild_last(weights, last, modes, begin, 6)


def solution(mesh):
    tm, space = mesh.shape["tm"], mesh.shape["space"]
    split = Mesh(mesh.devices.reshape(tm, space // 2, 2), ("tm", "outer", "inner"))
    cells = ("outer", "inner")
    in_specs = (P(cells, None), P(cells, "tm"), P(), P())
    out_specs = (P(), P("tm", cells))
    return jax.shard_map(
        per_device, mesh=split, in_specs=in_specs, out_specs=out_specs, check_vma=False
    )
```

```python
import functools

import jax
import jax.numpy as jnp
from jax import lax
from jax.experimental import pallas as pl
from jax.experimental.pallas import tpu as pltpu
from jax.sharding import Mesh, PartitionSpec as P

ROWS = (((1,), (0,)), ((), ()))
FIRST = (((0,), (0,)), ((), ()))
LAST = (((1,), (1,)), ((), ()))
STRIP = 512
FREE = pl.CostEstimate(flops=0, bytes_accessed=0, transcendentals=0)
LONG = pl.CostEstimate(flops=2 * 10**9, bytes_accessed=0, transcendentals=0)
ANYWHERE = pl.BlockSpec(memory_space=pl.ANY)
IN_VMEM = pl.BlockSpec(memory_space=pltpu.VMEM)


def started(copies):
    for copy in copies:
        copy.start()
    return copies


def waited(copies):
    for copy in copies:
        copy.wait()


def in_parts(value):
    high = value.astype(jnp.bfloat16)
    return high, (value - high.astype(jnp.float32)).astype(jnp.bfloat16)


def product(left, right, dims):
    return lax.dot_general(left, right, dims, preferred_element_type=jnp.float32)


def cut_kernel(fields, early, sent):
    half = early.shape[1] // 2
    spans = [pl.ds(at, half) for at in (0, half)]
    waited(
        started(
            [
                pltpu.make_async_copy(fields.at[:, span], early.at[:, span], sent.at[i])
                for i, span in enumerate(spans)
            ]
        )
    )


def cut(fields, width):
    return pl.pallas_call(
        cut_kernel,
        out_shape=jax.ShapeDtypeStruct((fields.shape[0], width), fields.dtype),
        in_specs=[ANYWHERE],
        out_specs=ANYWHERE,
        scratch_shapes=[pltpu.SemaphoreType.DMA((2,))],
        compiler_params=pltpu.CompilerParams(vmem_limit_bytes=53 * 2**20),
        cost_estimate=FREE,
        name="cut",
    )(fields)


def project_kernel(
    tiles, early, fields, basis, kept, given, late, patterns, halves, arrived, landed
):
    cells = basis.shape[0]
    tile, begin = cells // tiles, early.shape[1]
    spans = [pl.ds(i * tile, tile) for i in range(tiles)]
    rest = fields.at[:, pl.ds(begin, late.shape[1])]
    rest = pltpu.make_async_copy(rest, late, landed.at[0])
    copies = started(
        [
            pltpu.make_async_copy(basis.at[span], patterns.at[span], arrived.at[i])
            for i, span in enumerate(spans)
        ]
    )
    rest.start()
    total = jnp.zeros((early.shape[0], patterns.shape[1]), jnp.float32)
    for i, span in enumerate(spans):
        at = i * tile
        if at == begin:
            rest.wait()
        copies[i].wait()
        held = early[:, span] if at < begin else late[:, pl.ds(at - begin, tile)]
        total += product(held, patterns[span], ROWS)
    half = kept.shape[0]
    core = lax.axis_index("inner")
    halves[0] = total[:half]
    halves[1] = total[half:]
    kept[...] = halves[core]
    given[...] = halves[1 - core]


def project(early, fields, basis, tiles):
    (hours, cells), rank = fields.shape, basis.shape[1]
    half = jax.ShapeDtypeStruct((hours // 2, rank), jnp.float32)
    return pl.pallas_call(
        functools.partial(project_kernel, tiles),
        out_shape=(
            half,
            half,
            jax.ShapeDtypeStruct((hours, cells - early.shape[1]), fields.dtype),
        ),
        in_specs=[IN_VMEM, ANYWHERE, ANYWHERE],
        out_specs=(IN_VMEM,) * 3,
        scratch_shapes=[
            pltpu.VMEM(basis.shape, basis.dtype),
            pltpu.VMEM((2, hours // 2, rank), jnp.float32),
            pltpu.SemaphoreType.DMA((tiles,)),
            pltpu.SemaphoreType.DMA((1,)),
        ],
        compiler_params=pltpu.CompilerParams(vmem_limit_bytes=52 * 2**20),
        cost_estimate=FREE,
        name="project",
    )(early, fields, basis)


def lagged_and_scaled(every, energy):
    hour = lax.broadcasted_iota(jnp.int32, every.shape, 0)
    return jnp.where(hour == 0, 0.0, pltpu.roll(every, 1, 0)) * energy


def columns(held, begin, width):
    return jnp.concatenate([b[:, pl.ds(begin - at, width)] for b, at in held], axis=0)


def rebuilt(weights, held, made, modes, begin, tiles, sent, between=list):
    strips = made.shape[1] // STRIP
    edges = [strips * i // tiles * STRIP for i in range(tiles + 1)]
    outgoing = []
    for i in range(tiles):
        if i == tiles - 1:
            outgoing += between()
        for at in range(edges[i], edges[i + 1], STRIP):
            fields = columns(held, begin + at, STRIP)
            made[:, pl.ds(at, STRIP)] = product(weights, fields, ROWS).astype(made.dtype)
        width = edges[i + 1] - edges[i]
        source, target = made.at[:, pl.ds(edges[i], width)], pl.ds(begin + edges[i], width)
        outgoing += started([pltpu.make_async_copy(source, modes.at[:, target], sent.at[i])])
    return outgoing


def first_kernel(tiles, energy, vectors, *refs):
    count = (len(refs) - 8) // 3
    held, coeffs, refs = refs[:count], refs[count : 3 * count], refs[3 * count :]
    operator, modes, weights, known, scaled, made, square, sent = refs
    hours = held[0].shape[0]
    half = hours // 2
    me, core = lax.axis_index("tm"), lax.axis_index("inner")
    first = [lax.rem(me + k, count) * hours for k in range(count)]
    for n, block in enumerate(coeffs):
        at = pl.multiple_of(first[n // 2] + lax.rem(core + n % 2, 2) * half, half)
        known[pl.ds(at, half)] = block[...].astype(jnp.float32)
    every = known[...].astype(jnp.bfloat16)
    scaled[...] = lagged_and_scaled(known[...], energy[...])
    ordered = jnp.concatenate(
        [scaled[pl.ds(pl.multiple_of(at, hours), hours)] for at in first], axis=0
    )
    high, low = in_parts(ordered)
    value = (product(vectors[...], high, LAST) + product(vectors[...], low, LAST)).astype(
        jnp.bfloat16
    )
    weights[...] = value

    def operate():
        high, low = in_parts(scaled[...])
        square[...] = product(every, high, FIRST) + product(every, low, FIRST)
        return started([pltpu.make_async_copy(square, operator, sent.at[tiles])])

    waited(rebuilt(value, [(b, 0) for b in held], made, modes, 0, tiles, sent, operate))


def last_kernel(begin, tiles, weights, *refs):
    held, (_, modes, made, sent) = refs[:-4], refs[-4:]
    blocks = [(b, begin) for b in held]
    waited(rebuilt(weights[...], blocks, made, modes, begin, tiles, sent))


def rebuild_first(energy, vectors, held, coeffs, cells, tiles):
    rank = coeffs[0].shape[1]
    hours, modes = len(held) * held[0].shape[0], vectors.shape[0]
    return pl.pallas_call(
        functools.partial(first_kernel, tiles),
        out_shape=(
            jax.ShapeDtypeStruct((rank, rank), jnp.float32),
            jax.ShapeDtypeStruct((modes, cells), jnp.bfloat16),
            jax.ShapeDtypeStruct((modes, hours), jnp.bfloat16),
        ),
        in_specs=[IN_VMEM] * (2 + 3 * len(held)),
        out_specs=(ANYWHERE, ANYWHERE, IN_VMEM),
        scratch_shapes=[
            pltpu.VMEM((hours, rank), jnp.float32),
            pltpu.VMEM((hours, rank), jnp.float32),
            pltpu.VMEM((modes, held[0].shape[1]), jnp.bfloat16),
            pltpu.VMEM((rank, rank), jnp.float32),
            pltpu.SemaphoreType.DMA((tiles + 1,)),
        ],
        compiler_params=pltpu.CompilerParams(vmem_limit_bytes=40 * 2**20),
        cost_estimate=LONG,
        name="rebuild_first",
    )(energy, vectors, *held, *coeffs)


def rebuild_last(weights, held, modes, begin, tiles):
    return pl.pallas_call(
        functools.partial(last_kernel, begin, tiles),
        out_shape=jax.ShapeDtypeStruct(modes.shape, modes.dtype),
        in_specs=[IN_VMEM] * (1 + len(held)) + [ANYWHERE],
        out_specs=ANYWHERE,
        scratch_shapes=[
            pltpu.VMEM((modes.shape[0], modes.shape[1] - begin), modes.dtype),
            pltpu.SemaphoreType.DMA((tiles,)),
        ],
        input_output_aliases={1 + len(held): 0},
        compiler_params=pltpu.CompilerParams(vmem_limit_bytes=40 * 2**20),
        cost_estimate=FREE,
        name="rebuild_last",
    )(weights, *held, modes)


def swapped(value, axis, bit):
    route = [(i ^ bit, i) for i in range(lax.axis_size(axis))]
    return lax.ppermute(value, axis, route)


def moved(value, by, swap):
    size = lax.axis_size("tm")
    route = [
        (2 * ((i + by) % size) + (core ^ swap), 2 * i + core)
        for i in range(size)
        for core in range(2)
    ]
    return lax.ppermute(value, ("tm", "inner"), route)


def per_device(eof_basis, snapshots, inverse_energy, eigen_vectors):
    tm, outer = lax.axis_size("tm"), lax.axis_size("outer")
    me = lax.axis_index("tm")
    fields = snapshots.T

    cells = fields.shape[1]
    begin = cells // 16 * 13

    early = cut(fields, begin)
    first = [early] + [moved(early, k, 0) for k in range(1, tm)]

    kept, given, late = project(early, fields, eof_basis, 16)
    mine = kept + swapped(given, "inner", 1)
    bit = 1
    while bit < outer:
        near = swapped(mine, "outer", bit)
        if 2 * bit < outer:
            far, both = (swapped(mine, "outer", b) for b in (2 * bit, 3 * bit))
            mine = (mine + near) + (far + both)
        else:
            mine = mine + near
        bit *= 4
    mine = mine.astype(jnp.bfloat16)
    mine, behind = lax.optimization_barrier((mine, late))
    coeffs = []
    for k in range(tm):
        theirs = moved(mine, k, 0) if k else mine
        coeffs += [theirs, moved(theirs, 0, 1)]
    last = [late] + [moved(behind, k, 0) for k in range(1, tm)]

    rows = eigen_vectors.shape[1] // tm
    vectors = lax.dynamic_slice_in_dim(eigen_vectors, me * rows, rows, 1)
    operator, modes, weights = rebuild_first(
        inverse_energy[None, :], vectors.T, first, coeffs, cells, 6
    )
    return operator, rebuild_last(weights, last, modes, begin, 3)


def solution(mesh):
    tm, space = mesh.shape["tm"], mesh.shape["space"]
    split = Mesh(mesh.devices.reshape(tm, space // 2, 2), ("tm", "outer", "inner"))
    cells = ("outer", "inner")
    in_specs = (P(cells, None), P(cells, "tm"), P(), P())
    out_specs = (P(), P("tm", cells))
    return jax.shard_map(
        per_device, mesh=split, in_specs=in_specs, out_specs=out_specs, check_vma=False
    )
```

```python
import functools

import jax
import jax.numpy as jnp
from jax import lax
from jax.experimental import pallas as pl
from jax.experimental.pallas import tpu as pltpu
from jax.sharding import Mesh, PartitionSpec as P

ROWS = (((1,), (0,)), ((), ()))
FIRST = (((0,), (0,)), ((), ()))
LAST = (((1,), (1,)), ((), ()))
STRIP = 512
FREE = pl.CostEstimate(flops=0, bytes_accessed=0, transcendentals=0)
LONG = pl.CostEstimate(flops=2 * 10**9, bytes_accessed=0, transcendentals=0)
ANYWHERE = pl.BlockSpec(memory_space=pl.ANY)
IN_VMEM = pl.BlockSpec(memory_space=pltpu.VMEM)


def started(copies):
    for copy in copies:
        copy.start()
    return copies


def waited(copies):
    for copy in copies:
        copy.wait()


def in_parts(value):
    high = value.astype(jnp.bfloat16)
    return high, (value - high.astype(jnp.float32)).astype(jnp.bfloat16)


def product(left, right, dims):
    return lax.dot_general(left, right, dims, preferred_element_type=jnp.float32)


def cut_kernel(fields, early, sent):
    half = early.shape[1] // 2
    spans = [pl.ds(at, half) for at in (0, half)]
    waited(
        started(
            [
                pltpu.make_async_copy(fields.at[:, span], early.at[:, span], sent.at[i])
                for i, span in enumerate(spans)
            ]
        )
    )


def cut(fields, width):
    return pl.pallas_call(
        cut_kernel,
        out_shape=jax.ShapeDtypeStruct((fields.shape[0], width), fields.dtype),
        in_specs=[ANYWHERE],
        out_specs=ANYWHERE,
        scratch_shapes=[pltpu.SemaphoreType.DMA((2,))],
        compiler_params=pltpu.CompilerParams(vmem_limit_bytes=53 * 2**20),
        cost_estimate=FREE,
        name="cut",
    )(fields)


def project_kernel(
    tiles, early, fields, basis, kept, given, late, patterns, halves, arrived, landed
):
    cells = basis.shape[0]
    tile, begin = cells // tiles, early.shape[1]
    spans = [pl.ds(i * tile, tile) for i in range(tiles)]
    rest = fields.at[:, pl.ds(begin, late.shape[1])]
    rest = pltpu.make_async_copy(rest, late, landed.at[0])
    copies = started(
        [
            pltpu.make_async_copy(basis.at[span], patterns.at[span], arrived.at[i])
            for i, span in enumerate(spans)
        ]
    )
    rest.start()
    total = jnp.zeros((early.shape[0], patterns.shape[1]), jnp.float32)
    for i, span in enumerate(spans):
        at = i * tile
        if at == begin:
            rest.wait()
        copies[i].wait()
        held = early[:, span] if at < begin else late[:, pl.ds(at - begin, tile)]
        total += product(held, patterns[span], ROWS)
    half = kept.shape[0]
    core = lax.axis_index("inner")
    halves[0] = total[:half]
    halves[1] = total[half:]
    kept[...] = halves[core]
    given[...] = halves[1 - core]


def project(early, fields, basis, tiles):
    (hours, cells), rank = fields.shape, basis.shape[1]
    half = jax.ShapeDtypeStruct((hours // 2, rank), jnp.float32)
    return pl.pallas_call(
        functools.partial(project_kernel, tiles),
        out_shape=(
            half,
            half,
            jax.ShapeDtypeStruct((hours, cells - early.shape[1]), fields.dtype),
        ),
        in_specs=[IN_VMEM, ANYWHERE, ANYWHERE],
        out_specs=(IN_VMEM,) * 3,
        scratch_shapes=[
            pltpu.VMEM(basis.shape, basis.dtype),
            pltpu.VMEM((2, hours // 2, rank), jnp.float32),
            pltpu.SemaphoreType.DMA((tiles,)),
            pltpu.SemaphoreType.DMA((1,)),
        ],
        compiler_params=pltpu.CompilerParams(vmem_limit_bytes=52 * 2**20),
        cost_estimate=FREE,
        name="project",
    )(early, fields, basis)


def lagged_and_scaled(every, energy):
    hour = lax.broadcasted_iota(jnp.int32, every.shape, 0)
    return jnp.where(hour == 0, 0.0, pltpu.roll(every, 1, 0)) * energy


def columns(held, begin, width):
    return jnp.concatenate([b[:, pl.ds(begin - at, width)] for b, at in held], axis=0)


def rebuilt(weights, held, made, modes, begin, tiles, sent, between=list):
    strips = made.shape[1] // STRIP
    edges = [strips * i // tiles * STRIP for i in range(tiles + 1)]
    outgoing = []
    for i in range(tiles):
        if i == tiles - 1:
            outgoing += between()
        for at in range(edges[i], edges[i + 1], STRIP):
            fields = columns(held, begin + at, STRIP)
            made[:, pl.ds(at, STRIP)] = product(weights, fields, ROWS).astype(made.dtype)
        width = edges[i + 1] - edges[i]
        source, target = made.at[:, pl.ds(edges[i], width)], pl.ds(begin + edges[i], width)
        outgoing += started([pltpu.make_async_copy(source, modes.at[:, target], sent.at[i])])
    return outgoing


def first_kernel(tiles, energy, vectors, *refs):
    count = (len(refs) - 8) // 3
    held, coeffs, refs = refs[:count], refs[count : 3 * count], refs[3 * count :]
    operator, modes, weights, known, scaled, made, square, sent = refs
    hours = held[0].shape[0]
    half = hours // 2
    me, core = lax.axis_index("tm"), lax.axis_index("inner")
    first = [lax.rem(me + k, count) * hours for k in range(count)]
    for n, block in enumerate(coeffs):
        at = pl.multiple_of(first[n // 2] + lax.rem(core + n % 2, 2) * half, half)
        known[pl.ds(at, half)] = block[...].astype(jnp.float32)
    every = known[...].astype(jnp.bfloat16)
    scaled[...] = lagged_and_scaled(known[...], energy[...])
    ordered = jnp.concatenate(
        [scaled[pl.ds(pl.multiple_of(at, hours), hours)] for at in first], axis=0
    )
    high, low = in_parts(ordered)
    value = (product(vectors[...], high, LAST) + product(vectors[...], low, LAST)).astype(
        jnp.bfloat16
    )
    weights[...] = value

    def operate():
        lagged = lagged_and_scaled(known[...], 1.0).astype(jnp.bfloat16)
        square[...] = product(every, lagged, FIRST) * energy[...]
        return started([pltpu.make_async_copy(square, operator, sent.at[tiles])])

    waited(rebuilt(value, [(b, 0) for b in held], made, modes, 0, tiles, sent, operate))


def last_kernel(begin, tiles, weights, *refs):
    held, (_, modes, made, sent) = refs[:-4], refs[-4:]
    blocks = [(b, begin) for b in held]
    waited(rebuilt(weights[...], blocks, made, modes, begin, tiles, sent))


def rebuild_first(energy, vectors, held, coeffs, cells, tiles):
    rank = coeffs[0].shape[1]
    hours, modes = len(held) * held[0].shape[0], vectors.shape[0]
    return pl.pallas_call(
        functools.partial(first_kernel, tiles),
        out_shape=(
            jax.ShapeDtypeStruct((rank, rank), jnp.float32),
            jax.ShapeDtypeStruct((modes, cells), jnp.bfloat16),
            jax.ShapeDtypeStruct((modes, hours), jnp.bfloat16),
        ),
        in_specs=[IN_VMEM] * (2 + 3 * len(held)),
        out_specs=(ANYWHERE, ANYWHERE, IN_VMEM),
        scratch_shapes=[
            pltpu.VMEM((hours, rank), jnp.float32),
            pltpu.VMEM((hours, rank), jnp.float32),
            pltpu.VMEM((modes, held[0].shape[1]), jnp.bfloat16),
            pltpu.VMEM((rank, rank), jnp.float32),
            pltpu.SemaphoreType.DMA((tiles + 1,)),
        ],
        compiler_params=pltpu.CompilerParams(vmem_limit_bytes=40 * 2**20),
        cost_estimate=LONG,
        name="rebuild_first",
    )(energy, vectors, *held, *coeffs)


def rebuild_last(weights, held, modes, begin, tiles):
    return pl.pallas_call(
        functools.partial(last_kernel, begin, tiles),
        out_shape=jax.ShapeDtypeStruct(modes.shape, modes.dtype),
        in_specs=[IN_VMEM] * (1 + len(held)) + [ANYWHERE],
        out_specs=ANYWHERE,
        scratch_shapes=[
            pltpu.VMEM((modes.shape[0], modes.shape[1] - begin), modes.dtype),
            pltpu.SemaphoreType.DMA((tiles,)),
        ],
        input_output_aliases={1 + len(held): 0},
        compiler_params=pltpu.CompilerParams(vmem_limit_bytes=40 * 2**20),
        cost_estimate=FREE,
        name="rebuild_last",
    )(weights, *held, modes)


def swapped(value, axis, bit):
    route = [(i ^ bit, i) for i in range(lax.axis_size(axis))]
    return lax.ppermute(value, axis, route)


def moved(value, by, swap):
    size = lax.axis_size("tm")
    route = [
        (2 * ((i + by) % size) + (core ^ swap), 2 * i + core)
        for i in range(size)
        for core in range(2)
    ]
    return lax.ppermute(value, ("tm", "inner"), route)


def per_device(eof_basis, snapshots, inverse_energy, eigen_vectors):
    tm, outer = lax.axis_size("tm"), lax.axis_size("outer")
    me = lax.axis_index("tm")
    fields = snapshots.T

    cells = fields.shape[1]
    begin = cells // 16 * 13

    early = cut(fields, begin)
    first = [early] + [moved(early, k, 0) for k in range(1, tm)]

    kept, given, late = project(early, fields, eof_basis, 16)
    mine = kept + swapped(given, "inner", 1)
    bit = 1
    while bit < outer:
        near = swapped(mine, "outer", bit)
        if 2 * bit < outer:
            far, both = (swapped(mine, "outer", b) for b in (2 * bit, 3 * bit))
            mine = (mine + near) + (far + both)
        else:
            mine = mine + near
        bit *= 4
    mine = mine.astype(jnp.bfloat16)
    mine, behind = lax.optimization_barrier((mine, late))
    coeffs = []
    for k in range(tm):
        theirs = moved(mine, k, 0) if k else mine
        coeffs += [theirs, moved(theirs, 0, 1)]
    last = [late] + [moved(behind, k, 0) for k in range(1, tm)]

    rows = eigen_vectors.shape[1] // tm
    vectors = lax.dynamic_slice_in_dim(eigen_vectors, me * rows, rows, 1)
    operator, modes, weights = rebuild_first(
        inverse_energy[None, :], vectors.T, first, coeffs, cells, 6
    )
    return operator, rebuild_last(weights, last, modes, begin, 3)


def solution(mesh):
    tm, space = mesh.shape["tm"], mesh.shape["space"]
    split = Mesh(mesh.devices.reshape(tm, space // 2, 2), ("tm", "outer", "inner"))
    cells = ("outer", "inner")
    in_specs = (P(cells, None), P(cells, "tm"), P(), P())
    out_specs = (P(), P("tm", cells))
    return jax.shard_map(
        per_device, mesh=split, in_specs=in_specs, out_specs=out_specs, check_vma=False
    )
```

```python
import functools

import jax
import jax.numpy as jnp
from jax import lax
from jax.experimental import pallas as pl
from jax.experimental.pallas import tpu as pltpu
from jax.sharding import Mesh, PartitionSpec as P

ROWS = (((1,), (0,)), ((), ()))
FIRST = (((0,), (0,)), ((), ()))
LAST = (((1,), (1,)), ((), ()))
STRIP = 512
FREE = pl.CostEstimate(flops=0, bytes_accessed=0, transcendentals=0)
LONG = pl.CostEstimate(flops=2 * 10**9, bytes_accessed=0, transcendentals=0)
ANYWHERE = pl.BlockSpec(memory_space=pl.ANY)
IN_VMEM = pl.BlockSpec(memory_space=pltpu.VMEM)


def started(copies):
    for copy in copies:
        copy.start()
    return copies


def waited(copies):
    for copy in copies:
        copy.wait()


def in_parts(value):
    high = value.astype(jnp.bfloat16)
    return high, (value - high.astype(jnp.float32)).astype(jnp.bfloat16)


def product(left, right, dims):
    return lax.dot_general(left, right, dims, preferred_element_type=jnp.float32)


def cut_kernel(fields, early, sent):
    half = early.shape[1] // 2
    spans = [pl.ds(at, half) for at in (0, half)]
    waited(
        started(
            [
                pltpu.make_async_copy(fields.at[:, span], early.at[:, span], sent.at[i])
                for i, span in enumerate(spans)
            ]
        )
    )


def cut(fields, width):
    return pl.pallas_call(
        cut_kernel,
        out_shape=jax.ShapeDtypeStruct((fields.shape[0], width), fields.dtype),
        in_specs=[ANYWHERE],
        out_specs=ANYWHERE,
        scratch_shapes=[pltpu.SemaphoreType.DMA((2,))],
        compiler_params=pltpu.CompilerParams(vmem_limit_bytes=53 * 2**20),
        cost_estimate=FREE,
        name="cut",
    )(fields)


def project_kernel(
    tiles, early, fields, basis, kept, given, late, patterns, halves, arrived, landed
):
    cells = basis.shape[0]
    tile, begin = cells // tiles, early.shape[1]
    spans = [pl.ds(i * tile, tile) for i in range(tiles)]
    rest = fields.at[:, pl.ds(begin, late.shape[1])]
    rest = pltpu.make_async_copy(rest, late, landed.at[0])
    copies = started(
        [
            pltpu.make_async_copy(basis.at[span], patterns.at[span], arrived.at[i])
            for i, span in enumerate(spans)
        ]
    )
    rest.start()
    total = jnp.zeros((early.shape[0], patterns.shape[1]), jnp.float32)
    for i, span in enumerate(spans):
        at = i * tile
        if at == begin:
            rest.wait()
        copies[i].wait()
        held = early[:, span] if at < begin else late[:, pl.ds(at - begin, tile)]
        total += product(held, patterns[span], ROWS)
    half = kept.shape[0]
    core = lax.axis_index("inner")
    halves[0] = total[:half]
    halves[1] = total[half:]
    kept[...] = halves[core]
    given[...] = halves[1 - core]


def project(early, fields, basis, tiles):
    (hours, cells), rank = fields.shape, basis.shape[1]
    half = jax.ShapeDtypeStruct((hours // 2, rank), jnp.float32)
    return pl.pallas_call(
        functools.partial(project_kernel, tiles),
        out_shape=(
            half,
            half,
            jax.ShapeDtypeStruct((hours, cells - early.shape[1]), fields.dtype),
        ),
        in_specs=[IN_VMEM, ANYWHERE, ANYWHERE],
        out_specs=(IN_VMEM,) * 3,
        scratch_shapes=[
            pltpu.VMEM(basis.shape, basis.dtype),
            pltpu.VMEM((2, hours // 2, rank), jnp.float32),
            pltpu.SemaphoreType.DMA((tiles,)),
            pltpu.SemaphoreType.DMA((1,)),
        ],
        compiler_params=pltpu.CompilerParams(vmem_limit_bytes=52 * 2**20),
        cost_estimate=FREE,
        name="project",
    )(early, fields, basis)


def lagged_and_scaled(every, energy):
    hour = lax.broadcasted_iota(jnp.int32, every.shape, 0)
    return jnp.where(hour == 0, 0.0, pltpu.roll(every, 1, 0)) * energy


def columns(held, begin, width):
    return jnp.concatenate([b[:, pl.ds(begin - at, width)] for b, at in held], axis=0)


def rebuilt(weights, held, made, modes, begin, tiles, sent, between=list):
    strips = made.shape[1] // STRIP
    edges = [strips * i // tiles * STRIP for i in range(tiles + 1)]
    outgoing = []
    for i in range(tiles):
        if i == tiles - 1:
            outgoing += between()
        for at in range(edges[i], edges[i + 1], STRIP):
            fields = columns(held, begin + at, STRIP)
            made[:, pl.ds(at, STRIP)] = product(weights, fields, ROWS).astype(made.dtype)
        width = edges[i + 1] - edges[i]
        source, target = made.at[:, pl.ds(edges[i], width)], pl.ds(begin + edges[i], width)
        outgoing += started([pltpu.make_async_copy(source, modes.at[:, target], sent.at[i])])
    return outgoing


def first_kernel(tiles, energy, vectors, *refs):
    count = (len(refs) - 8) // 3
    held, coeffs, refs = refs[:count], refs[count : 3 * count], refs[3 * count :]
    operator, modes, weights, known, scaled, made, square, sent = refs
    hours = held[0].shape[0]
    half = hours // 2
    me, core = lax.axis_index("tm"), lax.axis_index("inner")
    first = [lax.rem(me + k, count) * hours for k in range(count)]
    for n, block in enumerate(coeffs):
        at = pl.multiple_of(first[n // 2] + lax.rem(core + n % 2, 2) * half, half)
        known[pl.ds(at, half)] = block[...].astype(jnp.float32)
    every = known[...].astype(jnp.bfloat16)
    scaled[...] = lagged_and_scaled(known[...], energy[...])
    ordered = jnp.concatenate(
        [scaled[pl.ds(pl.multiple_of(at, hours), hours)] for at in first], axis=0
    )
    high, low = in_parts(ordered)
    value = (product(vectors[...], high, LAST) + product(vectors[...], low, LAST)).astype(
        jnp.bfloat16
    )
    weights[...] = value

    def operate():
        lagged = lagged_and_scaled(known[...], 1.0).astype(jnp.bfloat16)
        square[...] = product(every, lagged, FIRST) * energy[...]
        return started([pltpu.make_async_copy(square, operator, sent.at[tiles])])

    waited(rebuilt(value, [(b, 0) for b in held], made, modes, 0, tiles, sent, operate))


def last_kernel(begin, tiles, weights, *refs):
    held, (_, modes, made, sent) = refs[:-4], refs[-4:]
    blocks = [(b, begin) for b in held]
    waited(rebuilt(weights[...], blocks, made, modes, begin, tiles, sent))


def rebuild_first(energy, vectors, held, coeffs, cells, tiles):
    rank = coeffs[0].shape[1]
    hours, modes = len(held) * held[0].shape[0], vectors.shape[0]
    return pl.pallas_call(
        functools.partial(first_kernel, tiles),
        out_shape=(
            jax.ShapeDtypeStruct((rank, rank), jnp.float32),
            jax.ShapeDtypeStruct((modes, cells), jnp.bfloat16),
            jax.ShapeDtypeStruct((modes, hours), jnp.bfloat16),
        ),
        in_specs=[IN_VMEM] * (2 + 3 * len(held)),
        out_specs=(ANYWHERE, ANYWHERE, IN_VMEM),
        scratch_shapes=[
            pltpu.VMEM((hours, rank), jnp.float32),
            pltpu.VMEM((hours, rank), jnp.float32),
            pltpu.VMEM((modes, held[0].shape[1]), jnp.bfloat16),
            pltpu.VMEM((rank, rank), jnp.float32),
            pltpu.SemaphoreType.DMA((tiles + 1,)),
        ],
        compiler_params=pltpu.CompilerParams(vmem_limit_bytes=40 * 2**20),
        cost_estimate=LONG,
        name="rebuild_first",
    )(energy, vectors, *held, *coeffs)


def rebuild_last(weights, held, modes, begin, tiles):
    return pl.pallas_call(
        functools.partial(last_kernel, begin, tiles),
        out_shape=jax.ShapeDtypeStruct(modes.shape, modes.dtype),
        in_specs=[IN_VMEM] * (1 + len(held)) + [ANYWHERE],
        out_specs=ANYWHERE,
        scratch_shapes=[
            pltpu.VMEM((modes.shape[0], modes.shape[1] - begin), modes.dtype),
            pltpu.SemaphoreType.DMA((tiles,)),
        ],
        input_output_aliases={1 + len(held): 0},
        compiler_params=pltpu.CompilerParams(vmem_limit_bytes=40 * 2**20),
        cost_estimate=FREE,
        name="rebuild_last",
    )(weights, *held, modes)


def swapped(value, axis, bit):
    route = [(i ^ bit, i) for i in range(lax.axis_size(axis))]
    return lax.ppermute(value, axis, route)


def moved(value, by, swap):
    size = lax.axis_size("tm")
    route = [
        (2 * ((i + by) % size) + (core ^ swap), 2 * i + core)
        for i in range(size)
        for core in range(2)
    ]
    return lax.ppermute(value, ("tm", "inner"), route)


def per_device(eof_basis, snapshots, inverse_energy, eigen_vectors):
    tm, outer = lax.axis_size("tm"), lax.axis_size("outer")
    me = lax.axis_index("tm")
    fields = snapshots.T

    cells = fields.shape[1]
    begin = cells // 16 * 13

    early = cut(fields, begin)
    first = [early] + [moved(early, k, 0) for k in range(1, tm)]

    kept, given, late = project(early, fields, eof_basis, 16)
    mine = kept + swapped(given, "inner", 1)
    bit = 1
    while bit < outer:
        near = swapped(mine, "outer", bit)
        if 2 * bit < outer:
            far, both = (swapped(mine, "outer", b) for b in (2 * bit, 3 * bit))
            mine = (mine + near) + (far + both)
        else:
            mine = mine + near
        bit *= 4
    mine = mine.astype(jnp.bfloat16)
    mine, behind = lax.optimization_barrier((mine, late))
    coeffs = []
    for k in range(tm):
        theirs = moved(mine, k, 0) if k else mine
        coeffs += [theirs, moved(theirs, 0, 1)]
    last = [late] + [moved(behind, k, 0) for k in range(1, tm)]

    rows = eigen_vectors.shape[1] // tm
    vectors = lax.dynamic_slice_in_dim(eigen_vectors, me * rows, rows, 1)
    operator, modes, weights = rebuild_first(
        inverse_energy[None, :], vectors.T, first, coeffs, cells, 13
    )
    return operator, rebuild_last(weights, last, modes, begin, 3)


def solution(mesh):
    tm, space = mesh.shape["tm"], mesh.shape["space"]
    split = Mesh(mesh.devices.reshape(tm, space // 2, 2), ("tm", "outer", "inner"))
    cells = ("outer", "inner")
    in_specs = (P(cells, None), P(cells, "tm"), P(), P())
    out_specs = (P(), P("tm", cells))
    return jax.shard_map(
        per_device, mesh=split, in_specs=in_specs, out_specs=out_specs, check_vma=False
    )
```
